32 devices in a mesh: xs: 16 (over z, y, core), ys: 2 (over x).
Axes of the slice: x: 2, y: 2, z: 4, core: 2. Of those that a mesh axis runs over, the one named last changes fastest.
Arguments:
- fields: float32 [6, 16, 512, 256], P(None, None, 'xs', 'ys'), may hold values from -6 to 6
- permittivity: float32 [16, 512, 256], P(None, 'xs', 'ys'), may hold values from 1 to 12
- adj_values: float32 [128, 128], P(('xs', 'ys')), may hold values from -6 to 6
- adj_owner: int32 [128, 1], P(('xs', 'ys')), may hold values from 0 to 1; in each aligned block of 4 rows (0 to 3, 4 to 7, ...) at most 4 rows name the same one
- adj_row: int32 [128], P(('xs', 'ys')), may hold values from 0 to 31
- angle_wave: int32 [128], replicated, may hold values from 0 to 4999
Outputs:
- new_fields: float32 [6, 16, 512, 256], P(None, None, 'xs', 'ys')
- far_field: float32 [128, 2, 4, 256], P('xs', None, None, 'ys')
The draws below stay inside these ranges and needn't reach their ends.
Inputs may be any that keep to these rules, and one draw needn't show every extreme that they name: `adj_owner`: among the 4 rows of one device no ys index is named more than 4 times.
All inputs are finite; a program needn't handle non-finite values.
Results may differ from the reference program's by a relative error of at most 0.000071.
Values sent between devices are 32-bit elements; how exact they have to be, the bound alone decides.
No kernel may reach another device: no remote copies, remote signals or barrier semaphores. Data moves between devices by JAX's collectives and lax.ppermute only.
A program may use at most 64 MiB of HBM per device.

```python
import math
import jax
import jax.numpy as jnp
import numpy as np
from jax import lax

CX = 32
CY = 128
NZ = 16
STEPS = 3
CAP = 4
GRID_X = 5000
X0 = 2000
ZS = 8
ADJ_DEV = 4
NX = 512
NY = 256
KA = 128
BLOCKS = 128
N_YS = 2


def place_ends(array, rng, smallest, top_value):
    extent = array.shape
    index_at = [jax.random.randint(jax.random.fold_in(rng, axis), (), 0, extent[axis]) for axis in range(len(extent))]
    array = array.at[tuple(index_at)].set(smallest)
    longest = extent.index(max(extent))
    index_at[longest] = (index_at[longest] + 1) % extent[longest]
    return array.at[tuple(index_at)].set(top_value)


def level_of(own_key, dims, cuts, smallest, largest):
    loudness = 1.0
    for dim, shards_of in cuts:
        heights = jax.random.uniform(jax.random.fold_in(jax.random.fold_in(own_key, 6), dim), (shards_of,), jnp.float32, smallest / len(cuts), largest / len(cuts))
        loudness = loudness * jnp.repeat(jnp.exp(heights), dims[dim] // shards_of).reshape((-1,) + (1,) * (len(dims) - 1 - dim))
    return loudness


def deal_out(stream_key, own, number, rows, count, top, most, slope):
    ranking = jax.random.permutation(stream_key, count)
    heavy_load, ordinary = load_shares(count, rows * top, most, slope, True), load_shares(count, rows * top, most, slope, False)
    places = jnp.arange(count)

    def named(tallies, rotation):
        used = int((tallies > 0).sum())
        fixed = max(1, used // 4)
        moved = fixed + (places - fixed + rotation * (used - fixed)) % max(1, count - fixed)
        return jnp.zeros((count,), jnp.int32).at[ranking[jnp.where(places < fixed, places, moved)]].set(jnp.asarray(tallies, jnp.int32))

    tallies = jnp.where(number % 4 == 0, named(heavy_load, number // 4), named(ordinary, number - number // 4 - 1))
    mixed = jax.random.permutation(jax.random.fold_in(own, 3), count)
    giver, receiver = mixed[0:count // 2 * 2:2], mixed[1:count // 2 * 2:2]
    room = jnp.minimum(tallies[giver] - 1, most - tallies[receiver]) // 2
    room = jnp.where((giver == ranking[0]) | (receiver == ranking[0]) | (tallies[receiver] == 0), 0, jnp.maximum(room, 0))
    moved = jax.random.randint(jax.random.fold_in(own, 4), (count // 2,), 0, 1 << 20) % (room + 1)
    tallies = tallies.at[giver].add(-moved).at[receiver].add(moved)
    labels = jnp.searchsorted(jnp.cumsum(tallies), jnp.arange(rows * top), side="right").astype(jnp.int32)
    listing = labels.reshape(top, rows).T
    listing = listing[jax.random.permutation(jax.random.fold_in(own, 1), rows)]
    rotation = jax.random.randint(jax.random.fold_in(own, 2), (rows, 1), 0, top)
    return jnp.take_along_axis(listing, (jnp.arange(top)[None, :] + rotation) % top, axis=1)


def load_shares(amount, total, bound, slope, full):
    loads = [(1 << 20) // math.isqrt(grade ** slope) + 1 for grade in range(1, amount + 1)]
    largest = bound if full else min(bound, max(-(-total // amount), total * loads[0] // sum(loads)))
    least = 1 if total - largest >= amount - 1 else 0
    given, rest = [largest] + [least] * (amount - 1), total - largest - least * (amount - 1)
    while rest > 0:
        free = [i for i in range(1, amount) if given[i] < largest] or [i for i in range(1, amount) if given[i] < bound]
        mass, remaining = sum([loads[i] for i in free]), rest
        for i in free:
            extra = min(bound - given[i], max(1, remaining * loads[i] // mass), rest)
            given[i] = given[i] + extra
            rest = rest - extra
    return np.array(given)


def bell_draw(key, shape, deviation, bound, cuts=(), kind=jnp.bfloat16):
    loudness = level_of(key, shape, cuts, -0.22, 0.18) if cuts else 1.0
    drawn = jax.random.normal(key, shape, jnp.float32) * deviation * loudness
    return jnp.minimum(jnp.maximum(drawn, -bound), bound).astype(kind)


def setup_inputs(seed: int = 0) -> dict:
    splits = jax.random.split(jax.random.key(seed), 7)
    fields = bell_draw(splits[0], (6, NZ, NX, NY), 1.0, 6.0, ((2, 16), (3, 2)), jnp.float32)
    permittivity = jnp.clip(jnp.exp(math.log(12.0) - 2.4849066 * jax.random.uniform(splits[1], (NZ, NX, NY), jnp.float32) ** level_of(splits[1], (NZ, NX, NY), ((1, 16), (2, 2)), -0.2, 0.2)), 1.0, 12.0)
    adj_values = bell_draw(splits[2], (BLOCKS, CY), 1.0, 6.0, ((0, 32),), jnp.float32)
    adj_owner_keys = jax.random.split(jax.random.fold_in(splits[3], 1), BLOCKS // ADJ_DEV)
    adj_owner_turns = jax.random.permutation(jax.random.fold_in(splits[3], 3), BLOCKS // ADJ_DEV)
    adj_owner = jax.vmap(lambda own, number: deal_out(jax.random.fold_in(splits[3], 2), own, number, ADJ_DEV, N_YS, 1, CAP, 2))(adj_owner_keys, adj_owner_turns).reshape((BLOCKS, 1))
    adj_row = place_ends(jax.random.randint(splits[4], (BLOCKS,), 0, CX), jax.random.fold_in(splits[4], 1), 0, CX - 1).astype(jnp.int32)
    angle_wave = place_ends(jax.random.randint(splits[5], (KA,), 0, GRID_X), jax.random.fold_in(splits[5], 1), 0, GRID_X - 1).astype(jnp.int32)
    return {"fields": fields, "permittivity": permittivity, "adj_values": adj_values, "adj_owner": adj_owner, "adj_row": adj_row, "angle_wave": angle_wave}


time_step = 0.5

def along_next(inner, edge, axis):
    return jnp.concatenate([lax.slice_in_dim(inner, 1, inner.shape[axis], axis=axis), edge], axis)

def along_prev(inner, edge, axis):
    return jnp.concatenate([edge, lax.slice_in_dim(inner, 0, inner.shape[axis] - 1, axis=axis)], axis)

def advance(fields, coeffs, source, next_x, next_y, prev_x, prev_y):
    elec = [fields[0], fields[1], fields[2]]
    magn = [fields[3], fields[4], fields[5]]
    zero_layer = jnp.zeros((1,) + elec[0].shape[1:], jnp.float32)
    edge_x = next_x(jnp.stack([elec[1][:, 0, :], elec[2][:, 0, :]]))
    edge_y = next_y(jnp.stack([elec[0][:, :, 0], elec[2][:, :, 0]]))
    ey_xnext = along_next(elec[1], edge_x[0][:, None, :], 1)
    ez_xnext = along_next(elec[2], edge_x[1][:, None, :], 1)
    ex_ynext = along_next(elec[0], edge_y[0][:, :, None], 2)
    ez_ynext = along_next(elec[2], edge_y[1][:, :, None], 2)
    ex_znext = along_next(elec[0], zero_layer, 0)
    ey_znext = along_next(elec[1], zero_layer, 0)
    hx_new = magn[0] - time_step * (ez_ynext - elec[2] - (ey_znext - elec[1]))
    hy_new = magn[1] - time_step * (ex_znext - elec[0] - (ez_xnext - elec[2]))
    hz_new = magn[2] - time_step * (ey_xnext - elec[1] - (ex_ynext - elec[0]))
    back_x = prev_x(jnp.stack([hy_new[:, -1, :], hz_new[:, -1, :]]))
    back_y = prev_y(jnp.stack([hx_new[:, :, -1], hz_new[:, :, -1]]))
    hy_xprev = along_prev(hy_new, back_x[0][:, None, :], 1)
    hz_xprev = along_prev(hz_new, back_x[1][:, None, :], 1)
    hx_yprev = along_prev(hx_new, back_y[0][:, :, None], 2)
    hz_yprev = along_prev(hz_new, back_y[1][:, :, None], 2)
    hx_zprev = along_prev(hx_new, zero_layer, 0)
    hy_zprev = along_prev(hy_new, zero_layer, 0)
    ex_new = elec[0] + coeffs * (hz_new - hz_yprev - (hy_new - hy_zprev))
    ey_new = elec[1] + coeffs * (hx_new - hx_zprev - (hz_new - hz_xprev))
    ez_new = elec[2] + coeffs * (hy_new - hy_xprev - (hx_new - hx_yprev) - source)
    return jnp.stack([ex_new, ey_new, ez_new, hx_new, hy_new, hz_new])

def spectrum(tile, angles, first_x):
    positions = X0 + first_x + jnp.arange(tile.shape[1], dtype=jnp.int32)
    phase = angles[:, None] * positions[None, :] % GRID_X
    angle = phase.astype(jnp.float32) * (2.0 * math.pi / GRID_X)
    cosine = jnp.cos(angle)
    sine = -jnp.sin(angle)
    real_part = jnp.einsum('ax,cxy->acy', cosine, tile, precision=lax.Precision.HIGHEST)
    imag_part = jnp.einsum('ax,cxy->acy', sine, tile, precision=lax.Precision.HIGHEST)
    return jnp.stack([real_part, imag_part], axis=1)

def zero_rim(plane):
    return jnp.zeros_like(plane)

def reference(fields, permittivity, adj_values, adj_owner, adj_row, angle_wave):
    width_x = fields.shape[2]
    width_y = fields.shape[3]
    device = jnp.arange(adj_values.shape[0], dtype=jnp.int32) // ADJ_DEV
    row_x = device // N_YS * CX + adj_row
    columns = adj_owner[:, 0][:, None] * CY + jnp.arange(CY, dtype=jnp.int32)[None, :]
    rows_full = jnp.broadcast_to(row_x[:, None], columns.shape)
    current = jnp.zeros((width_x, width_y), jnp.float32).at[rows_full, columns].add(adj_values)
    coeffs = time_step / permittivity
    layer_mask = (jnp.arange(NZ, dtype=jnp.int32) == ZS).astype(jnp.float32)[:, None, None]
    source = layer_mask * current[None]
    for iteration in range(STEPS):
        fields = advance(fields, coeffs, source, zero_rim, zero_rim, zero_rim, zero_rim)
    tile = jnp.stack([-fields[4][ZS], fields[3][ZS], fields[1][ZS], -fields[0][ZS]])
    far_field = spectrum(tile, angle_wave, 0) / math.sqrt(width_x)
    return (fields, far_field)
```

```python
import functools
import math

import jax
import jax.numpy as jnp
from jax import lax
from jax.experimental import pallas as pl
from jax.experimental.pallas import tpu as pltpu
from jax.sharding import PartitionSpec as P

STEPS = 3
CAP = 4
GRID_X = 5000
X0 = 2000
ZS = 8

time_step = 0.5

TILE = 8
REACH = 4
SLOT = 8
PARTS = 7
PAIRS = (PARTS + 1) // 2

VMEM = pl.BlockSpec(memory_space=pltpu.VMEM)
SMEM = pl.BlockSpec(memory_space=pltpu.SMEM)
PARAMS = pltpu.CompilerParams(vmem_limit_bytes=24 * 1024 * 1024)


def lanes_of(shape):
    return lax.broadcasted_iota(jnp.int32, shape, len(shape) - 1)


def rows_of(shape):
    return lax.broadcasted_iota(jnp.int32, shape, len(shape) - 2)


def swaps(size):
    found = []
    for first in (0, 1):
        pairs = [(i, i + 1) for i in range(first, size - 1, 2)]
        if pairs:
            found.append(pairs + [(j, i) for i, j in pairs])
    return found


def halo_tile(even, odd, px, c, z, layers):
    at = pl.ds((c * (layers // 2) + z // 2) * TILE, TILE)
    from_even, from_odd = even[at, :], odd[at, :]
    same = px == z % 2
    from_even = jnp.where(same, from_even, pltpu.roll(from_even, REACH, 0))
    from_odd = jnp.where(same, pltpu.roll(from_odd, REACH, 0), from_odd)
    odd_half = (rows_of(from_even.shape) >= REACH) == (px == 0)
    return jnp.where(odd_half, from_odd, from_even)


def pack_x(f_lo, f_hi, p_lo, p_hi, *rest, n_adj):
    if n_adj:
        values, rows, owners, to_even, to_odd, blocks = rest
    else:
        to_even, to_odd = rest
    px = lax.axis_index("xs") % 2
    layers = f_lo.shape[1]
    for c in range(PARTS):
        for pair in range(layers // 2):
            if c < 6:
                lo = [f_lo[c, 2 * pair + k] for k in (0, 1)]
                hi = [f_hi[c, 2 * pair + k] for k in (0, 1)]
            else:
                lo = [time_step / p_lo[2 * pair + k] for k in (0, 1)]
                hi = [time_step / p_hi[2 * pair + k] for k in (0, 1)]
            upper = rows_of(lo[0].shape) >= REACH
            first = jnp.where(upper, pltpu.roll(lo[1], REACH, 0), lo[0])
            last = jnp.where(upper, hi[1], pltpu.roll(hi[0], REACH, 0))
            at = pl.ds((c * (layers // 2) + pair) * TILE, TILE)
            to_even[at, :] = jnp.where(px == 0, last, first)
            to_odd[at, :] = jnp.where(px == 0, first, last)
    if n_adj:
        blocks[...] = jnp.zeros(blocks.shape, jnp.float32)
        blocks[0:n_adj, :] = values[...]
        for b in range(n_adj):
            one = (1, blocks.shape[1])
            blocks[n_adj + b : n_adj + b + 1, :] = jnp.full(one, rows[b], jnp.int32).astype(
                jnp.float32
            )
            blocks[2 * n_adj + b : 2 * n_adj + b + 1, :] = jnp.full(
                one, owners[b, 0], jnp.int32
            ).astype(jnp.float32)
        end = PARTS * (layers // 2) * TILE
        to_even[end:, :] = blocks[...]
        to_odd[end:, :] = blocks[...]


def pack_y(fields, permittivity, even, *rest, n_rows, swap):
    if n_rows:
        blocks, to_y, to_diag = rest
    else:
        to_y, to_diag = rest
    px = lax.axis_index("xs") % 2
    to_next = lax.axis_index("ys") % 2 == swap
    layers, cells_x = fields.shape[1], fields.shape[2]
    tiles = cells_x // TILE
    ring = cells_x + TILE
    offset = jnp.where(to_next, 3, 0)
    width = fields.shape[3]
    quad = ((lanes_of((TILE, width)) + offset) % width) // 4
    half = layers // 2 * TILE
    for q in range(PAIRS):
        for r in range(tiles + 1):
            total = jnp.zeros((TILE, width), jnp.float32)
            for b in range(2):
                c = 2 * q + b
                if c >= PARTS:
                    continue
                for z in range(layers):
                    if r < tiles:
                        rows = slice(r * TILE, (r + 1) * TILE)
                        if c < 6:
                            block = fields[c, z, rows, :]
                        else:
                            block = time_step / permittivity[z, rows, :]
                    else:
                        at = pl.ds(c * half + z // 2 * TILE, TILE)
                        block = even[at, :]
                        block = jnp.where(px == z % 2, block, pltpu.roll(block, REACH, 0))
                    shift = SLOT * z + 4 * b
                    if shift:
                        block = pltpu.roll(block, shift, 1)
                    total = jnp.where(quad == 2 * z + b, block, total)
            to_y[q * ring + r * TILE : q * ring + (r + 1) * TILE, :] = pltpu.roll(total, offset, 1)
    upper = rows_of((TILE, width)) >= REACH
    for k in range(PAIRS // 2):
        starts = [(2 * k + j) * ring for j in (0, 1)]
        lo = [to_y[s : s + TILE, :] for s in starts]
        hi = [to_y[s + cells_x - TILE : s + cells_x, :] for s in starts]
        first = jnp.where(upper, pltpu.roll(lo[1], REACH, 0), lo[0])
        last = jnp.where(upper, hi[1], pltpu.roll(hi[0], REACH, 0))
        to_diag[k * TILE : (k + 1) * TILE, :] = jnp.where(px == 0, first, last)
    if n_rows:
        end = PAIRS * ring
        to_y[end : end + n_rows, :] = blocks[...]
        to_y[end + n_rows : end + 2 * n_rows, :] = even[PARTS * half :, :]
        to_diag[PAIRS // 2 * TILE :, :] = blocks[...]


def gather_sources(sets, px, me, source, n_adj):
    ring, width = source.shape[1:]
    row_at = rows_of((ring, width)).astype(jnp.float32)
    mine = jnp.zeros((ring, width), jnp.float32)
    other = jnp.zeros((ring, width), jnp.float32)
    own_index = jnp.where(me == 0, 0.0, 1.0)
    cells_x = ring - TILE
    for ref, start, is_next in sets:
        for b in range(n_adj):
            value = ref[start + b : start + b + 1, :]
            row = ref[start + n_adj + b : start + n_adj + b + 1, :]
            owner = ref[start + 2 * n_adj + b : start + 2 * n_adj + b + 1, :]
            if is_next is not None:
                after = jnp.where(row < REACH, row + cells_x, -1.0)
                before = jnp.where(row >= cells_x - REACH, row + TILE, -1.0)
                row = jnp.where(is_next, after, before)
            is_mine = owner == own_index
            mine = mine + jnp.where(row_at == jnp.where(is_mine, row, -1.0), value, 0.0)
            other = other + jnp.where(row_at == jnp.where(is_mine, -1.0, row), value, 0.0)
    lane = lanes_of((ring, width))
    slot = (lane >= SLOT * ZS) & (lane < SLOT * (ZS + 1))
    place = lane - SLOT * ZS
    shift = SLOT * ZS + 3
    before = jnp.where(me == 0, 0.0, pltpu.roll(other, shift, 1))
    source[0] = mine
    source[1] = jnp.where(slot, jnp.where(place < 3, before, pltpu.roll(mine, shift, 1)), 0.0)
    shift = SLOT * ZS + 5
    after = jnp.where(me == 0, pltpu.roll(other, shift, 1), 0.0)
    source[2] = jnp.where(slot, jnp.where(place < 5, pltpu.roll(mine, shift, 1), after), 0.0)


def evolve(*refs, n_adj, n_rows, n_swaps):
    fields, permittivity, even, odd = refs[:4]
    y_halos = [refs[4 + 2 * k : 6 + 2 * k] for k in range(n_swaps)]
    rest = refs[4 + 2 * n_swaps :]
    if n_adj:
        blocks, rest = rest[0], rest[1:]
    else:
        given, rest = rest[0], rest[1:]
    out, tile, grid, coeffs, strip, strip_coeffs, source, edge_e, edge_h = rest
    px = lax.axis_index("xs") % 2
    me = lax.axis_index("ys")
    layers, cells_x, width = fields.shape[1:]
    tiles = cells_x // TILE
    ring = cells_x + TILE
    full = (ring, width)
    lane, row = lanes_of(full), rows_of(full)

    for z in range(layers):
        for c in range(6):
            grid[c, z, 0:cells_x, :] = fields[c, z]
            grid[c, z, cells_x:ring, :] = halo_tile(even, odd, px, c, z, layers)
        coeffs[z, 0:cells_x, :] = time_step / permittivity[z]
        coeffs[z, cells_x:ring, :] = halo_tile(even, odd, px, 6, z, layers)

    if n_adj:
        end = PARTS * (layers // 2) * TILE
        y_end, d_end = PAIRS * ring, PAIRS // 2 * TILE
        y_ref, d_ref = y_halos[0]
        sets = [
            (blocks, 0, None),
            (even, end, px == 0),
            (odd, end, px == 1),
            (y_ref, y_end, None),
            (y_ref, y_end + n_rows, px == 0),
            (d_ref, d_end, px == 1),
        ]
        gather_sources(sets, px, me, source, n_adj)
    else:
        source[...] = given[...]

    place = lane % SLOT
    odd_half = (row[0:TILE] >= REACH) == (px == 0)
    for q in range(PAIRS):
        arrived = []
        for y_ref, d_ref in y_halos:
            corner = d_ref[q // 2 * TILE : (q // 2 + 1) * TILE, :]
            corner = jnp.where(px == q % 2, pltpu.roll(corner, REACH, 0), corner)
            last = y_ref[q * ring + cells_x : (q + 1) * ring, :]
            arrived.append(
                jnp.concatenate(
                    [y_ref[q * ring : q * ring + cells_x, :], jnp.where(odd_half, corner, last)], 0
                )
            )
        before = jnp.zeros(full, jnp.float32)
        after = jnp.zeros(full, jnp.float32)
        for k, block in enumerate(arrived):
            is_next = me % 2 == k
            after = jnp.where(is_next, block, after)
            before = jnp.where(is_next, before, block)
        for b in range(2):
            c = 2 * q + b
            if c >= PARTS:
                continue
            halo = (
                pltpu.roll(before, width - 4, 1) if b else before,
                pltpu.roll(after, 1 if b else 5, 1),
            )
            for side in (0, 1):
                total = jnp.zeros(full, jnp.float32)
                for z in range(layers):
                    block = grid[c, z] if c < 6 else coeffs[z]
                    shift = (SLOT * z + (5 if side else 3)) % width
                    total = jnp.where(lane // SLOT == z, pltpu.roll(block, shift, 1), total)
                total = jnp.where((place >= 5) if side else (place < 3), halo[side], total)
                if c < 6:
                    strip[side, c] = total
                else:
                    strip_coeffs[side] = total

    no_prev_x = (row >= ring - REACH) & (lax.axis_index("xs") == 0)
    step_main = jnp.where(no_prev_x, 0.0, time_step)
    step_strip = (
        jnp.where((place < 3) & (me == 0), 0.0, step_main),
        step_main,
    )

    def next_x(v):
        return pltpu.roll(v, ring - 1, 0)

    def prev_x(v):
        return pltpu.roll(v, 1, 0)

    for step in range(STEPS):
        for side in (0, 1):
            ex, ey, ez, hx, hy, hz = [strip[side, c] for c in range(6)]
            dt, co = step_strip[side], strip_coeffs[side]
            if side:
                edge_e[step, 0], edge_e[step, 1] = ex, ez

            def next_y(v):
                return pltpu.roll(v, width - 1, 1)

            def prev_y(v):
                return pltpu.roll(v, 1, 1)

            def next_z(v):
                return jnp.where(lane < width - SLOT, pltpu.roll(v, width - SLOT, 1), 0.0)

            def prev_z(v):
                return jnp.where(lane >= SLOT, pltpu.roll(v, SLOT, 1), 0.0)

            hx = hx - dt * (next_y(ez) - ez - (next_z(ey) - ey))
            hy = hy - dt * (next_z(ex) - ex - (next_x(ez) - ez))
            hz = hz - dt * (next_x(ey) - ey - (next_y(ex) - ex))
            if not side:
                edge_h[step, 0], edge_h[step, 1] = hx, hz
            if step + 1 == STEPS:
                continue
            ex = ex + co * (hz - prev_y(hz) - (hy - prev_z(hy)))
            ey = ey + co * (hx - prev_z(hx) - (hz - prev_x(hz)))
            ez = ez + co * (hy - prev_x(hy) - (hx - prev_y(hx)) - source[1 + side])
            for c, v in enumerate((ex, ey, ez, hx, hy, hz)):
                strip[side, c] = v

    for step in range(STEPS):
        final = step + 1 == STEPS
        below = (None, None)
        for z in range(layers):
            ex, ey, ez, hx, hy, hz = [grid[c, z] for c in range(6)]
            co = coeffs[z]
            if z + 1 < layers:
                ex_z, ey_z = grid[0, z + 1] - ex, grid[1, z + 1] - ey
            else:
                ex_z, ey_z = 0.0 - ex, 0.0 - ey

            def next_y(v, edge):
                shift = (width - 1 - (SLOT * z + 5)) % width
                return jnp.where(
                    lane == width - 1, pltpu.roll(edge, shift, 1), pltpu.roll(v, width - 1, 1)
                )

            def prev_y(v, edge):
                shift = (width - (SLOT * z + 2)) % width
                return jnp.where(lane == 0, pltpu.roll(edge, shift, 1), pltpu.roll(v, 1, 1))

            hx = hx - step_main * (next_y(ez, edge_e[step, 1]) - ez - ey_z)
            hy = hy - step_main * (ex_z - (next_x(ez) - ez))
            hz = hz - step_main * (next_x(ey) - ey - (next_y(ex, edge_e[step, 0]) - ex))
            hx_z = hx - below[0] if z else hx
            hy_z = hy - below[1] if z else hy
            hx_y = hx - prev_y(hx, edge_h[step, 0])
            ex = ex + co * (hz - prev_y(hz, edge_h[step, 1]) - hy_z)
            ey = ey + co * (hx_z - (hz - prev_x(hz)))
            ez_change = hy - prev_x(hy) - hx_y
            if z == ZS:
                ez_change = ez_change - source[0]
            ez = ez + co * ez_change
            below = (hx, hy)
            for c, v in enumerate((ex, ey, ez, hx, hy, hz)):
                if final:
                    out[c, z] = v[0:cells_x]
                else:
                    grid[c, z] = v
            if final and z == ZS:
                for k, v in enumerate((-hy, hx, ey, -ex)):
                    tile[:, k * width : (k + 1) * width] = v[0:cells_x]


def multiply(weights, own, other, keep, send):
    tiles = jnp.concatenate([own[...], other[...]], 0)
    total = jnp.dot(
        weights[...],
        tiles,
        precision=lax.Precision.HIGHEST,
        preferred_element_type=jnp.float32,
    )
    half = keep.shape[0]
    keep[...] = total[0:half]
    send[...] = total[half:]


def add_split(first, second, keep, send):
    half = keep.shape[0]
    keep[...] = first[0:half, :] + second[0:half, :]
    send[...] = first[half:, :] + second[half:, :]


def shape_of(*dims):
    return jax.ShapeDtypeStruct(dims, jnp.float32)


def far_field_weights(angle_wave, xs_size, cells_x):
    me = lax.axis_index("xs")
    bits = xs_size.bit_length() - 1
    per_block = angle_wave.shape[0] // xs_size
    view = angle_wave.reshape((2,) * bits + (per_block,))
    for k in range(bits):
        bit = (me >> (bits - 1 - k)) & 1
        view = jnp.where(bit == 1, jnp.flip(view, k), view)
    view = view[(slice(None),) * (bits - 1) + (0,)]
    order = tuple(range(bits - 2, -1, -1)) + (bits - 1,)
    angles = view.transpose(order).reshape(-1)
    within = jnp.arange(cells_x, dtype=jnp.int32)
    positions = X0 + jnp.concatenate([me * cells_x + within, (me ^ 1) * cells_x + within])
    phase = angles[:, None] * positions[None, :] % GRID_X
    angle = phase.astype(jnp.float32) * (2.0 * math.pi / GRID_X)
    scale = 1.0 / math.sqrt(cells_x * xs_size)
    both = jnp.stack([jnp.cos(angle) * scale, -jnp.sin(angle) * scale], axis=1)
    return both.reshape(-1, 2 * cells_x)


def far_field_exchange(tile, angle_wave, xs_size):
    cells_x, columns = tile.shape
    bits = xs_size.bit_length() - 1
    weights = far_field_weights(angle_wave, xs_size, cells_x)

    def across(block, mask):
        return lax.ppermute(block, "xs", [(i, i ^ mask) for i in range(xs_size)])

    other = across(tile, 1)
    half = weights.shape[0] // 2
    keep, send = pl.pallas_call(
        multiply,
        out_shape=(shape_of(half, columns),) * 2,
        in_specs=[VMEM] * 3,
        out_specs=(VMEM, VMEM),
        compiler_params=PARAMS,
        name="partial_spectrum",
    )(weights, tile, other)
    for k in range(1, bits):
        arrived = across(send, 1 << k)
        if k + 1 == bits:
            return keep + arrived
        half = half // 2
        keep, send = pl.pallas_call(
            add_split,
            out_shape=(shape_of(half, columns),) * 2,
            in_specs=[VMEM] * 2,
            out_specs=(VMEM, VMEM),
            compiler_params=PARAMS,
            name="add_arrived",
        )(keep, arrived)


def gathered_sources(adj_values, adj_owner, adj_row, cells_x, cells_y):
    groups = lax.axis_size("ys")
    owners = adj_owner[:, 0]
    hits = (owners[:, None] == jnp.arange(groups, dtype=jnp.int32)[None, :]).astype(jnp.int32)
    before = jnp.cumsum(hits, axis=0) - hits
    slot_index = owners * CAP + jnp.sum(before * hits, axis=1)
    placing = (jnp.arange(groups * CAP, dtype=jnp.int32)[:, None] == slot_index[None, :]).astype(
        jnp.float32
    )
    rows = jnp.broadcast_to(adj_row.astype(jnp.float32)[:, None], (adj_row.shape[0], 1))
    outgoing = jnp.dot(
        placing, jnp.concatenate([adj_values, rows], 1), precision=lax.Precision.HIGHEST
    ).reshape(groups, CAP, cells_y + 1)
    incoming = lax.all_to_all(outgoing, "ys", split_axis=0, concat_axis=0, tiled=True)
    incoming = incoming.reshape(groups * CAP, cells_y + 1)
    landing = (
        jnp.arange(cells_x, dtype=jnp.float32)[:, None] == incoming[:, cells_y][None, :]
    ).astype(jnp.float32)
    current = jnp.dot(landing, incoming[:, :cells_y], precision=lax.Precision.HIGHEST)

    def shifted(block, axis, distance):
        size = lax.axis_size(axis)
        route = [(i, i + distance) for i in range(size) if 0 <= i + distance < size]
        return lax.ppermute(block, axis, route)

    after = shifted(current[:REACH], "xs", -1)
    before = shifted(current[-REACH:], "xs", 1)
    ringed = jnp.concatenate([current, after, before], 0)
    right = shifted(ringed[:, :3], "ys", -1)
    left = shifted(ringed[:, -3:], "ys", 1)
    start, end = SLOT * ZS, cells_y - SLOT * (ZS + 1)
    first = jnp.pad(jnp.concatenate([left, ringed[:, :5]], 1), ((0, 0), (start, end)))
    second = jnp.pad(jnp.concatenate([ringed[:, -5:], right], 1), ((0, 0), (start, end)))
    return jnp.stack([ringed, first, second])


def on_device(fields, permittivity, adj_values, adj_owner, adj_row, angle_wave):
    layers, cells_x, cells_y = fields.shape[1:]
    xs_size, ys_size = lax.axis_size("xs"), lax.axis_size("ys")
    raw = ys_size == 2
    n_adj = adj_values.shape[0] if raw else 0
    n_rows = -(-3 * n_adj // TILE) * TILE
    ring = cells_x + TILE
    x_rows = PARTS * (layers // 2) * TILE + n_rows
    y_rows = PAIRS * ring + 2 * n_rows
    d_rows = PAIRS // 2 * TILE + n_rows

    lo = pl.BlockSpec((6, layers, TILE, cells_y), lambda i: (0, 0, 0, 0))
    hi = pl.BlockSpec((6, layers, TILE, cells_y), lambda i: (0, 0, cells_x // TILE - 1, 0))
    p_lo = pl.BlockSpec((layers, TILE, cells_y), lambda i: (0, 0, 0))
    p_hi = pl.BlockSpec((layers, TILE, cells_y), lambda i: (0, cells_x // TILE - 1, 0))
    extra = (adj_values, adj_row, adj_owner) if raw else ()
    packed = pl.pallas_call(
        functools.partial(pack_x, n_adj=n_adj),
        grid=(1,),
        out_shape=(shape_of(x_rows, cells_y),) * 2 + ((shape_of(n_rows, cells_y),) if raw else ()),
        in_specs=[lo, hi, p_lo, p_hi] + ([VMEM, SMEM, SMEM] if raw else []),
        out_specs=(VMEM,) * (3 if raw else 2),
        compiler_params=PARAMS,
        name="pack_x_edges",
    )(fields, fields, permittivity, permittivity, *extra)
    blocks = packed[2:]
    x_even, x_odd = swaps(xs_size)
    from_even = lax.ppermute(packed[0], "xs", x_even)
    from_odd = lax.ppermute(packed[1], "xs", x_odd)

    y_halos = []
    y_swaps = swaps(ys_size)
    for k, route in enumerate(y_swaps):
        to_y, to_diag = pl.pallas_call(
            functools.partial(pack_y, n_rows=n_rows, swap=k),
            out_shape=(shape_of(y_rows, cells_y), shape_of(d_rows, cells_y)),
            in_specs=[VMEM] * (3 + len(blocks)),
            out_specs=(VMEM, VMEM),
            compiler_params=PARAMS,
            name="pack_y_edges",
        )(fields, permittivity, from_even, *blocks)
        diagonal = [(a * ys_size + c, b * ys_size + d) for a, b in x_odd for c, d in route]
        y_halos += [
            lax.ppermute(to_y, "ys", route),
            lax.ppermute(to_diag, ("xs", "ys"), diagonal),
        ]

    if raw:
        sources = blocks
    else:
        sources = (gathered_sources(adj_values, adj_owner, adj_row, cells_x, cells_y),)

    new_fields, tile = pl.pallas_call(
        functools.partial(evolve, n_adj=n_adj, n_rows=n_rows, n_swaps=len(y_swaps)),
        out_shape=(shape_of(*fields.shape), shape_of(cells_x, 4 * cells_y)),
        in_specs=[VMEM] * (4 + len(y_halos) + 1),
        out_specs=(VMEM, VMEM),
        scratch_shapes=[
            pltpu.VMEM((6, layers, ring, cells_y), jnp.float32),
            pltpu.VMEM((layers, ring, cells_y), jnp.float32),
            pltpu.VMEM((2, 6, ring, cells_y), jnp.float32),
            pltpu.VMEM((2, ring, cells_y), jnp.float32),
            pltpu.VMEM((3, ring, cells_y), jnp.float32),
            pltpu.VMEM((STEPS, 2, ring, cells_y), jnp.float32),
            pltpu.VMEM((STEPS, 2, ring, cells_y), jnp.float32),
        ],
        compiler_params=PARAMS,
        name="time_steps",
    )(fields, permittivity, from_even, from_odd, *y_halos, *sources)
    far = far_field_exchange(tile, angle_wave, xs_size)
    per_block = angle_wave.shape[0] // xs_size
    return (new_fields, far.reshape(per_block, 2, 4, cells_y))


def solution(mesh):
    placed = (
        P(None, None, "xs", "ys"),
        P(None, "xs", "ys"),
        P(("xs", "ys"), None),
        P(("xs", "ys"), None),
        P(("xs", "ys")),
        P(),
    )
    return jax.shard_map(
        on_device,
        mesh=mesh,
        in_specs=placed,
        out_specs=(P(None, None, "xs", "ys"), P("xs", None, None, "ys")),
        check_vma=False,
    )
```

```python
import functools
import math

import jax
import jax.numpy as jnp
from jax import lax
from jax.experimental import pallas as pl
from jax.experimental.pallas import tpu as pltpu
from jax.sharding import PartitionSpec as P

STEPS = 3
CAP = 4
GRID_X = 5000
X0 = 2000
ZS = 8

time_step = 0.5

TILE = 8
REACH = 4
SLOT = 8
PARTS = 7
PAIRS = (PARTS + 1) // 2

VMEM = pl.BlockSpec(memory_space=pltpu.VMEM)
HBM = pl.BlockSpec(memory_space=pl.ANY)
PARAMS = pltpu.CompilerParams(vmem_limit_bytes=24 * 1024 * 1024)


def lanes_of(shape):
    return lax.broadcasted_iota(jnp.int32, shape, len(shape) - 1)


def rows_of(shape):
    return lax.broadcasted_iota(jnp.int32, shape, len(shape) - 2)


def swaps(size):
    found = []
    for first in (0, 1):
        pairs = [(i, i + 1) for i in range(first, size - 1, 2)]
        if pairs:
            found.append(pairs + [(j, i) for i, j in pairs])
    return found


def halo_tile(even, odd, px, c, z, layers):
    at = pl.ds((c * (layers // 2) + z // 2) * TILE, TILE)
    from_even, from_odd = even[at, :], odd[at, :]
    same = px == z % 2
    from_even = jnp.where(same, from_even, pltpu.roll(from_even, REACH, 0))
    from_odd = jnp.where(same, pltpu.roll(from_odd, REACH, 0), from_odd)
    odd_half = (rows_of(from_even.shape) >= REACH) == (px == 0)
    return jnp.where(odd_half, from_odd, from_even)


def pack_x(*refs, n_adj):
    fields, permittivity = refs[:2]
    if n_adj:
        values, rows, owners, to_even, to_odd, blocks = refs[2:8]
        edges, edge_perm, rows_s, owners_s, sems = refs[8:]
    else:
        to_even, to_odd, edges, edge_perm, sems = refs[2:]
    px = lax.axis_index("xs") % 2
    layers, cells_x = fields.shape[1:3]
    copies = []
    for k, start in enumerate((0, cells_x - TILE)):
        rows_at = pl.ds(start, TILE)
        copies.append((fields.at[:, :, rows_at, :], edges.at[k]))
        copies.append((permittivity.at[:, rows_at, :], edge_perm.at[k]))
    if n_adj:
        blocks[...] = jnp.zeros(blocks.shape, jnp.float32)
        copies.append((values, blocks.at[pl.ds(0, n_adj), :]))
        copies.append((rows, rows_s))
        copies.append((owners, owners_s))
    copies = [pltpu.make_async_copy(s, d, sems.at[k]) for k, (s, d) in enumerate(copies)]
    for copy in copies:
        copy.start()
    for copy in copies:
        copy.wait()
    for c in range(PARTS):
        for pair in range(layers // 2):
            if c < 6:
                lo = [edges[0, c, 2 * pair + k] for k in (0, 1)]
                hi = [edges[1, c, 2 * pair + k] for k in (0, 1)]
            else:
                lo = [time_step / edge_perm[0, 2 * pair + k] for k in (0, 1)]
                hi = [time_step / edge_perm[1, 2 * pair + k] for k in (0, 1)]
            upper = rows_of(lo[0].shape) >= REACH
            first = jnp.where(upper, pltpu.roll(lo[1], REACH, 0), lo[0])
            last = jnp.where(upper, hi[1], pltpu.roll(hi[0], REACH, 0))
            at = pl.ds((c * (layers // 2) + pair) * TILE, TILE)
            to_even[at, :] = jnp.where(px == 0, last, first)
            to_odd[at, :] = jnp.where(px == 0, first, last)
    if n_adj:
        for b in range(n_adj):
            one = (1, blocks.shape[1])
            row, owner = n_adj + b, 2 * n_adj + b
            blocks[row : row + 1, :] = jnp.full(one, rows_s[b], jnp.int32).astype(jnp.float32)
            blocks[owner : owner + 1, :] = jnp.full(one, owners_s[b], jnp.int32).astype(
                jnp.float32
            )
        end = PARTS * (layers // 2) * TILE
        to_even[end:, :] = blocks[...]
        to_odd[end:, :] = blocks[...]


def pack_columns(tile_of, layers, offset, width):
    quad = ((lanes_of((TILE, width)) + offset) % width) // 4
    total = jnp.zeros((TILE, width), jnp.float32)
    for b in range(2):
        for z in range(layers):
            block = tile_of(b, z)
            if block is None:
                continue
            shift = SLOT * z + 4 * b
            if shift:
                block = pltpu.roll(block, shift, 1)
            total = jnp.where(quad == 2 * z + b, block, total)
    return pltpu.roll(total, offset, 1)


def column_offset(swap):
    return jnp.where(lax.axis_index("ys") % 2 == swap, 3, 0)


def pack_y(fields, permittivity, to_y, *, swap):
    layers, cells_x, width = fields.shape[1:]
    ring = cells_x + TILE
    offset = column_offset(swap)
    for q in range(PAIRS):
        for r in range(cells_x // TILE):
            rows = slice(r * TILE, (r + 1) * TILE)

            def tile_of(b, z):
                c = 2 * q + b
                if c < 6:
                    return fields[c, z, rows, :]
                return time_step / permittivity[z, rows, :] if c < PARTS else None

            at = slice(q * ring + r * TILE, q * ring + (r + 1) * TILE)
            to_y[at, :] = pack_columns(tile_of, layers, offset, width)


def pack_corners(unused, even, odd, *rest, layers, n_rows, swap):
    blocks, to_y = rest if n_rows else (None, rest[0])
    px = lax.axis_index("xs") % 2
    offset = column_offset(swap)
    width = to_y.shape[1]
    ring = (to_y.shape[0] - 3 * n_rows) // PAIRS
    for q in range(PAIRS):

        def tile_of(b, z):
            c = 2 * q + b
            return halo_tile(even, odd, px, c, z, layers) if c < PARTS else None

        to_y[(q + 1) * ring - TILE : (q + 1) * ring, :] = pack_columns(
            tile_of, layers, offset, width
        )
    if n_rows:
        end = PAIRS * ring
        x_end = PARTS * (layers // 2) * TILE
        to_y[end : end + n_rows, :] = blocks[...]
        to_y[end + n_rows : end + 2 * n_rows, :] = even[x_end:, :]
        to_y[end + 2 * n_rows : end + 3 * n_rows, :] = odd[x_end:, :]


def gather_sources(sets, px, me, source, n_adj):
    ring, width = source.shape[1:]
    row_at = rows_of((ring, width)).astype(jnp.float32)
    mine = jnp.zeros((ring, width), jnp.float32)
    other = jnp.zeros((ring, width), jnp.float32)
    own_index = jnp.where(me == 0, 0.0, 1.0)
    cells_x = ring - TILE
    for ref, start, is_next in sets:
        for b in range(n_adj):
            value = ref[start + b : start + b + 1, :]
            row = ref[start + n_adj + b : start + n_adj + b + 1, :]
            owner = ref[start + 2 * n_adj + b : start + 2 * n_adj + b + 1, :]
            if is_next is not None:
                after = jnp.where(row < REACH, row + cells_x, -1.0)
                before = jnp.where(row >= cells_x - REACH, row + TILE, -1.0)
                row = jnp.where(is_next, after, before)
            is_mine = owner == own_index
            mine = mine + jnp.where(row_at == jnp.where(is_mine, row, -1.0), value, 0.0)
            other = other + jnp.where(row_at == jnp.where(is_mine, -1.0, row), value, 0.0)
    lane = lanes_of((ring, width))
    slot = (lane >= SLOT * ZS) & (lane < SLOT * (ZS + 1))
    place = lane - SLOT * ZS
    shift = SLOT * ZS + 3
    before = jnp.where(me == 0, 0.0, pltpu.roll(other, shift, 1))
    source[0] = mine
    source[1] = jnp.where(slot, jnp.where(place < 3, before, pltpu.roll(mine, shift, 1)), 0.0)
    shift = SLOT * ZS + 5
    after = jnp.where(me == 0, pltpu.roll(other, shift, 1), 0.0)
    source[2] = jnp.where(slot, jnp.where(place < 5, pltpu.roll(mine, shift, 1), after), 0.0)


def evolve(*refs, n_adj, n_rows, n_swaps, surface):
    fields, permittivity, even, odd = refs[:4]
    y_halos = refs[4 : 4 + n_swaps]
    given, out, grid, coeffs, strip, strip_coeffs, source, edge_e, edge_h = refs[-9:]
    px = lax.axis_index("xs") % 2
    me = lax.axis_index("ys")
    layers, cells_x, width = fields.shape[1:]
    ring = cells_x + TILE
    full = (ring, width)
    lane, row = lanes_of(full), rows_of(full)
    used = range(layers)
    if surface:
        used = range(max(ZS - STEPS, 0), min(ZS + STEPS + 1, layers))

    for z in used:
        for c in range(6):
            grid[c, z, 0:cells_x, :] = fields[c, z]
            grid[c, z, cells_x:ring, :] = halo_tile(even, odd, px, c, z, layers)
        coeffs[z, 0:cells_x, :] = time_step / permittivity[z]
        coeffs[z, cells_x:ring, :] = halo_tile(even, odd, px, 6, z, layers)

    if n_adj:
        end = PARTS * (layers // 2) * TILE
        y_end = PAIRS * ring
        sets = [
            (given, 0, None),
            (even, end, px == 0),
            (odd, end, px == 1),
            (y_halos[0], y_end, None),
            (y_halos[0], y_end + n_rows, px == 0),
            (y_halos[0], y_end + 2 * n_rows, px == 1),
        ]
        gather_sources(sets, px, me, source, n_adj)
    else:
        source[...] = given[...]

    place = lane % SLOT
    for q in range(PAIRS):
        before = jnp.zeros(full, jnp.float32)
        after = jnp.zeros(full, jnp.float32)
        for k, y_ref in enumerate(y_halos):
            block = y_ref[q * ring : (q + 1) * ring, :]
            is_next = me % 2 == k
            after = jnp.where(is_next, block, after)
            before = jnp.where(is_next, before, block)
        for b in range(2):
            c = 2 * q + b
            if c >= PARTS:
                continue
            halo = (
                pltpu.roll(before, width - 4, 1) if b else before,
                pltpu.roll(after, 1 if b else 5, 1),
            )
            for side in (0, 1):
                total = jnp.zeros(full, jnp.float32)
                for z in used:
                    block = grid[c, z] if c < 6 else coeffs[z]
                    shift = (SLOT * z + (5 if side else 3)) % width
                    total = jnp.where(lane // SLOT == z, pltpu.roll(block, shift, 1), total)
                total = jnp.where((place >= 5) if side else (place < 3), halo[side], total)
                if c < 6:
                    strip[side, c] = total
                else:
                    strip_coeffs[side] = total

    no_prev_x = (row >= ring - REACH) & (lax.axis_index("xs") == 0)
    step_main = jnp.where(no_prev_x, 0.0, time_step)
    step_strip = (
        jnp.where((place < 3) & (me == 0), 0.0, step_main),
        step_main,
    )

    def next_x(v):
        return pltpu.roll(v, ring - 1, 0)

    def prev_x(v):
        return pltpu.roll(v, 1, 0)

    for step in range(STEPS):
        for side in (0, 1):
            ex, ey, ez, hx, hy, hz = [strip[side, c] for c in range(6)]
            dt, co = step_strip[side], strip_coeffs[side]
            if side:
                edge_e[step, 0], edge_e[step, 1] = ex, ez

            def next_y(v):
                return pltpu.roll(v, width - 1, 1)

            def prev_y(v):
                return pltpu.roll(v, 1, 1)

            def next_z(v):
                return jnp.where(lane < width - SLOT, pltpu.roll(v, width - SLOT, 1), 0.0)

            def prev_z(v):
                return jnp.where(lane >= SLOT, pltpu.roll(v, SLOT, 1), 0.0)

            hx = hx - dt * (next_y(ez) - ez - (next_z(ey) - ey))
            hy = hy - dt * (next_z(ex) - ex - (next_x(ez) - ez))
            hz = hz - dt * (next_x(ey) - ey - (next_y(ex) - ex))
            if not side:
                edge_h[step, 0], edge_h[step, 1] = hx, hz
            if step + 1 == STEPS:
                continue
            ex = ex + co * (hz - prev_y(hz) - (hy - prev_z(hy)))
            ey = ey + co * (hx - prev_z(hx) - (hz - prev_x(hz)))
            ez = ez + co * (hy - prev_x(hy) - (hx - prev_y(hx)) - source[1 + side])
            for c, v in enumerate((ex, ey, ez, hx, hy, hz)):
                strip[side, c] = v

    for step in range(STEPS):
        final = step + 1 == STEPS
        low, high = 0, layers - 1
        if surface:
            low, high = max(ZS - STEPS + step, 0), min(ZS + STEPS - 1 - step, layers - 1)
        below = None
        for z in range(low, high + 1):
            ex, ey, ez, hx, hy, hz = [grid[c, z] for c in range(6)]
            co = coeffs[z]
            if z + 1 < layers:
                ex_z, ey_z = grid[0, z + 1] - ex, grid[1, z + 1] - ey
            else:
                ex_z, ey_z = 0.0 - ex, 0.0 - ey

            def next_y(v, edge):
                shift = (width - 1 - (SLOT * z + 5)) % width
                return jnp.where(
                    lane == width - 1, pltpu.roll(edge, shift, 1), pltpu.roll(v, width - 1, 1)
                )

            def prev_y(v, edge):
                shift = (width - (SLOT * z + 2)) % width
                return jnp.where(lane == 0, pltpu.roll(edge, shift, 1), pltpu.roll(v, 1, 1))

            hx = hx - step_main * (next_y(ez, edge_e[step, 1]) - ez - ey_z)
            hy = hy - step_main * (ex_z - (next_x(ez) - ez))
            hz = hz - step_main * (next_x(ey) - ey - (next_y(ex, edge_e[step, 0]) - ex))
            if z == 0 or below:
                hx_z = hx - below[0] if z else hx
                hy_z = hy - below[1] if z else hy
                hx_y = hx - prev_y(hx, edge_h[step, 0])
                ex = ex + co * (hz - prev_y(hz, edge_h[step, 1]) - hy_z)
                ey = ey + co * (hx_z - (hz - prev_x(hz)))
                ez_change = hy - prev_x(hy) - hx_y
                if z == ZS:
                    ez_change = ez_change - source[0]
                ez = ez + co * ez_change
            below = (hx, hy)
            if not final:
                for c, v in enumerate((ex, ey, ez, hx, hy, hz)):
                    grid[c, z] = v
            elif not surface:
                for c, v in enumerate((ex, ey, ez, hx, hy, hz)):
                    out[c, z] = v[0:cells_x]
            elif z == ZS:
                for k, v in enumerate((-hy, hx, ey, -ex)):
                    out[:, k * width : (k + 1) * width] = v[0:cells_x]


def multiply(weights, *refs, n_tiles):
    tiles, parts = refs[:n_tiles], refs[n_tiles:]
    total = jnp.dot(
        weights[...],
        jnp.concatenate([tile[...] for tile in tiles], 0),
        precision=lax.Precision.HIGHEST,
        preferred_element_type=jnp.float32,
    )
    rows = parts[0].shape[0]
    for k, part in enumerate(parts):
        part[...] = total[k * rows : (k + 1) * rows]


def add_parts(*refs):
    parts, out = refs[:-1], refs[-1]
    total = parts[0][...]
    for part in parts[1:]:
        total = total + part[...]
    width = out.shape[2]
    for k in range(out.shape[1]):
        out[:, k, :] = total[:, k * width : (k + 1) * width]


def shape_of(*dims):
    return jax.ShapeDtypeStruct(dims, jnp.float32)


def far_field_weights(angle_wave, xs_size, cells_x, near):
    me = lax.axis_index("xs")
    per_block = angle_wave.shape[0] // xs_size
    far = xs_size // near
    bits = far.bit_length() - 1
    view = angle_wave.reshape(far, near, per_block)
    pick = jnp.arange(near, dtype=jnp.int32)[None, :, None] == me % near
    view = jnp.sum(jnp.where(pick, view, 0), axis=1).reshape((2,) * bits + (per_block,))
    for k in range(bits):
        bit = (me // near >> (bits - 1 - k)) & 1
        view = jnp.where(bit == 1, jnp.flip(view, k), view)
    angles = view.reshape(-1)
    owners = me ^ jnp.arange(near, dtype=jnp.int32)
    within = jnp.arange(cells_x, dtype=jnp.int32)
    positions = X0 + (owners[:, None] * cells_x + within[None, :]).reshape(-1)
    phase = angles[:, None] * positions[None, :] % GRID_X
    angle = phase.astype(jnp.float32) * (2.0 * math.pi / GRID_X)
    scale = 1.0 / math.sqrt(cells_x * xs_size)
    both = jnp.stack([jnp.cos(angle) * scale, -jnp.sin(angle) * scale], axis=1)
    return both.reshape(-1, near * cells_x)


def far_field_exchange(tile, angle_wave, xs_size):
    cells_x, columns = tile.shape
    near = 4
    weights = far_field_weights(angle_wave, xs_size, cells_x, near)

    def across(block, mask):
        return lax.ppermute(block, "xs", [(i, i ^ mask) for i in range(xs_size)])

    third = across(tile, 2)
    second = across(tile, 1)
    fourth = across(third, 1)
    far = xs_size // near
    rows = weights.shape[0] // far
    parts = pl.pallas_call(
        functools.partial(multiply, n_tiles=near),
        out_shape=(shape_of(rows, columns),) * far,
        in_specs=[VMEM] * (near + 1),
        out_specs=(VMEM,) * far,
        compiler_params=PARAMS,
        name="partial_spectrum",
    )(weights, tile, second, third, fourth)
    arrived = [across(parts[k], k * near) for k in range(far - 1, 0, -1)]
    return pl.pallas_call(
        add_parts,
        out_shape=shape_of(rows, 4, columns // 4),
        in_specs=[VMEM] * far,
        out_specs=VMEM,
        compiler_params=PARAMS,
        name="add_arrived",
    )(parts[0], *arrived)


def gathered_sources(adj_values, adj_owner, adj_row, cells_x, cells_y):
    groups = lax.axis_size("ys")
    owners = adj_owner[:, 0]
    hits = (owners[:, None] == jnp.arange(groups, dtype=jnp.int32)[None, :]).astype(jnp.int32)
    before = jnp.cumsum(hits, axis=0) - hits
    slot_index = owners * CAP + jnp.sum(before * hits, axis=1)
    placing = (jnp.arange(groups * CAP, dtype=jnp.int32)[:, None] == slot_index[None, :]).astype(
        jnp.float32
    )
    rows = jnp.broadcast_to(adj_row.astype(jnp.float32)[:, None], (adj_row.shape[0], 1))
    outgoing = jnp.dot(
        placing, jnp.concatenate([adj_values, rows], 1), precision=lax.Precision.HIGHEST
    ).reshape(groups, CAP, cells_y + 1)
    incoming = lax.all_to_all(outgoing, "ys", split_axis=0, concat_axis=0, tiled=True)
    incoming = incoming.reshape(groups * CAP, cells_y + 1)
    landing = (
        jnp.arange(cells_x, dtype=jnp.float32)[:, None] == incoming[:, cells_y][None, :]
    ).astype(jnp.float32)
    current = jnp.dot(landing, incoming[:, :cells_y], precision=lax.Precision.HIGHEST)

    def shifted(block, axis, distance):
        size = lax.axis_size(axis)
        route = [(i, i + distance) for i in range(size) if 0 <= i + distance < size]
        return lax.ppermute(block, axis, route)

    after = shifted(current[:REACH], "xs", -1)
    before = shifted(current[-REACH:], "xs", 1)
    ringed = jnp.concatenate([current, after, before], 0)
    right = shifted(ringed[:, :3], "ys", -1)
    left = shifted(ringed[:, -3:], "ys", 1)
    start, end = SLOT * ZS, cells_y - SLOT * (ZS + 1)
    first = jnp.pad(jnp.concatenate([left, ringed[:, :5]], 1), ((0, 0), (start, end)))
    second = jnp.pad(jnp.concatenate([ringed[:, -5:], right], 1), ((0, 0), (start, end)))
    return jnp.stack([ringed, first, second])


def on_device(fields, permittivity, adj_values, adj_owner, adj_row, angle_wave):
    layers, cells_x, cells_y = fields.shape[1:]
    xs_size, ys_size = lax.axis_size("xs"), lax.axis_size("ys")
    raw = ys_size == 2
    n_adj = adj_values.shape[0] if raw else 0
    n_rows = -(-3 * n_adj // TILE) * TILE
    ring = cells_x + TILE
    x_rows = PARTS * (layers // 2) * TILE + n_rows
    y_rows = PAIRS * ring + 3 * n_rows

    extra = (adj_values, adj_row, adj_owner.reshape(-1)) if raw else ()
    packed = pl.pallas_call(
        functools.partial(pack_x, n_adj=n_adj),
        out_shape=(shape_of(x_rows, cells_y),) * 2 + ((shape_of(n_rows, cells_y),) if raw else ()),
        in_specs=[HBM] * (2 + len(extra)),
        out_specs=(VMEM,) * (3 if raw else 2),
        scratch_shapes=[
            pltpu.VMEM((2, 6, layers, TILE, cells_y), jnp.float32),
            pltpu.VMEM((2, layers, TILE, cells_y), jnp.float32),
        ]
        + ([pltpu.SMEM((n_adj,), jnp.int32)] * 2 if raw else [])
        + [pltpu.SemaphoreType.DMA((4 + len(extra),))],
        compiler_params=PARAMS,
        name="pack_x_edges",
    )(*[pltpu.with_memory_space_constraint(x, pltpu.HBM) for x in (fields, permittivity, *extra)])
    blocks = packed[2:]
    x_even, x_odd = swaps(xs_size)
    from_even = lax.ppermute(packed[0], "xs", x_even)
    from_odd = lax.ppermute(packed[1], "xs", x_odd)

    y_halos = []
    y_swaps = swaps(ys_size)
    for k, route in enumerate(y_swaps):
        to_y = pl.pallas_call(
            functools.partial(pack_y, swap=k),
            out_shape=shape_of(y_rows, cells_y),
            in_specs=[VMEM] * 2,
            out_specs=VMEM,
            compiler_params=PARAMS,
            name="pack_y_edges",
        )(fields, permittivity)
        to_y = pl.pallas_call(
            functools.partial(pack_corners, layers=layers, n_rows=n_rows, swap=k),
            out_shape=shape_of(y_rows, cells_y),
            in_specs=[VMEM] * (3 + len(blocks)),
            out_specs=VMEM,
            input_output_aliases={0: 0},
            compiler_params=PARAMS,
            name="pack_corners",
        )(to_y, from_even, from_odd, *blocks)
        y_halos.append(lax.ppermute(to_y, "ys", route))

    if raw:
        sources = blocks
    else:
        sources = (gathered_sources(adj_values, adj_owner, adj_row, cells_x, cells_y),)

    def steps(surface, shape, name, *after):
        return pl.pallas_call(
            lambda *refs: evolve(
                *refs[: len(operands)],
                *refs[len(operands) + len(after) :],
                n_adj=n_adj,
                n_rows=n_rows,
                n_swaps=len(y_swaps),
                surface=surface,
            ),
            out_shape=shape,
            in_specs=[VMEM] * len(operands) + [pl.BlockSpec(memory_space=pl.ANY)] * len(after),
            out_specs=VMEM,
            scratch_shapes=[
                pltpu.VMEM((6, layers, ring, cells_y), jnp.float32),
                pltpu.VMEM((layers, ring, cells_y), jnp.float32),
                pltpu.VMEM((2, 6, ring, cells_y), jnp.float32),
                pltpu.VMEM((2, ring, cells_y), jnp.float32),
                pltpu.VMEM((3, ring, cells_y), jnp.float32),
                pltpu.VMEM((STEPS, 2, ring, cells_y), jnp.float32),
                pltpu.VMEM((STEPS, 2, ring, cells_y), jnp.float32),
            ],
            compiler_params=PARAMS,
            name=name,
        )(*operands, *after)

    operands = (fields, permittivity, from_even, from_odd, *y_halos, *sources)
    tile = steps(True, shape_of(cells_x, 4 * cells_y), "surface_steps")
    new_fields = steps(False, shape_of(*fields.shape), "time_steps", tile)
    far = far_field_exchange(tile, angle_wave, xs_size)
    per_block = angle_wave.shape[0] // xs_size
    return (new_fields, far.reshape(per_block, 2, 4, cells_y))


def solution(mesh):
    placed = (
        P(None, None, "xs", "ys"),
        P(None, "xs", "ys"),
        P(("xs", "ys"), None),
        P(("xs", "ys"), None),
        P(("xs", "ys")),
        P(),
    )
    return jax.shard_map(
        on_device,
        mesh=mesh,
        in_specs=placed,
        out_specs=(P(None, None, "xs", "ys"), P("xs", None, None, "ys")),
        check_vma=False,
    )
```

```python
import functools
import math

import jax
import jax.numpy as jnp
from jax import lax
from jax.experimental import pallas as pl
from jax.experimental.pallas import tpu as pltpu
from jax.sharding import PartitionSpec as P

STEPS = 3
CAP = 4
GRID_X = 5000
X0 = 2000
ZS = 8

time_step = 0.5

TILE = 8
REACH = 4
SLOT = 8
PARTS = 7
PAIRS = (PARTS + 1) // 2
TOGETHER = 8

VMEM = pl.BlockSpec(memory_space=pltpu.VMEM)
ANY = pl.BlockSpec(memory_space=pl.ANY)
PARAMS = pltpu.CompilerParams(vmem_limit_bytes=24 * 1024 * 1024)


def lanes_of(shape):
    return lax.broadcasted_iota(jnp.int32, shape, len(shape) - 1)


def rows_of(shape):
    return lax.broadcasted_iota(jnp.int32, shape, len(shape) - 2)


def swaps(size):
    found = []
    for first in (0, 1):
        pairs = [(i, i + 1) for i in range(first, size - 1, 2)]
        if pairs:
            found.append(pairs + [(j, i) for i, j in pairs])
    return found


def halo_tile(even, odd, px, c, z, layers):
    at = pl.ds(pl.multiple_of((c * (layers // 2) + z // 2) * TILE, TILE), TILE)
    from_even, from_odd = even[at, :], odd[at, :]
    same = px == z % 2
    turned_even, turned_odd = pltpu.roll(from_even, REACH, 0), pltpu.roll(from_odd, REACH, 0)
    odd_half = (rows_of(from_even.shape) >= REACH) == (px == 0)
    return jnp.where(
        same,
        jnp.where(odd_half, turned_odd, from_even),
        jnp.where(odd_half, from_odd, turned_even),
    )


def repeat(first, last, body, together=1):
    count = last - first
    if together >= count:
        for i in range(first, last):
            body(i)
        return
    rounds = count // together

    def several(n, _):
        for k in range(together):
            body(first + n * together + k)

    lax.fori_loop(0, rounds, several, None)
    for i in range(first + rounds * together, last):
        body(i)


def pack_x(*refs, n_adj):
    fields, permittivity = refs[:2]
    if n_adj:
        values, rows, owners, to_even, to_odd, blocks = refs[2:8]
        edges, edge_perm, rows_s, owners_s, sems = refs[8:]
    else:
        to_even, to_odd, edges, edge_perm, sems = refs[2:]
    px = lax.axis_index("xs") % 2
    layers, cells_x = fields.shape[1:3]
    copies = []
    for k, start in enumerate((0, cells_x - TILE)):
        rows_at = pl.ds(start, TILE)
        copies.append((fields.at[:, :, rows_at, :], edges.at[k]))
        copies.append((permittivity.at[:, rows_at, :], edge_perm.at[k]))
    if n_adj:
        blocks[...] = jnp.zeros(blocks.shape, jnp.float32)
        copies.append((values, blocks.at[pl.ds(0, n_adj), :]))
        copies.append((rows, rows_s))
        copies.append((owners, owners_s))
    copies = [pltpu.make_async_copy(s, d, sems.at[k]) for k, (s, d) in enumerate(copies)]
    for copy in copies:
        copy.start()
    for copy in copies:
        copy.wait()
    for c in range(PARTS):
        for pair in range(layers // 2):
            if c < 6:
                lo = [edges[0, c, 2 * pair + k] for k in (0, 1)]
                hi = [edges[1, c, 2 * pair + k] for k in (0, 1)]
            else:
                lo = [time_step / edge_perm[0, 2 * pair + k] for k in (0, 1)]
                hi = [time_step / edge_perm[1, 2 * pair + k] for k in (0, 1)]
            upper = rows_of(lo[0].shape) >= REACH
            first = jnp.where(upper, pltpu.roll(lo[1], REACH, 0), lo[0])
            last = jnp.where(upper, hi[1], pltpu.roll(hi[0], REACH, 0))
            at = pl.ds((c * (layers // 2) + pair) * TILE, TILE)
            to_even[at, :] = jnp.where(px == 0, last, first)
            to_odd[at, :] = jnp.where(px == 0, first, last)
    if n_adj:
        for b in range(n_adj):
            one = (1, blocks.shape[1])
            row, owner = n_adj + b, 2 * n_adj + b
            blocks[row : row + 1, :] = jnp.full(one, rows_s[b], jnp.int32).astype(jnp.float32)
            blocks[owner : owner + 1, :] = jnp.full(one, owners_s[b], jnp.int32).astype(
                jnp.float32
            )
        end = PARTS * (layers // 2) * TILE
        to_even[end:, :] = blocks[...]
        to_odd[end:, :] = blocks[...]


def pack_strips(tile_of, layers):
    first = second = None
    for z in layers:
        block = tile_of(z)
        here = lanes_of(block.shape) // SLOT == z
        lower = pltpu.roll(block, (SLOT * z + 3) % block.shape[1], 1)
        upper = pltpu.roll(block, (SLOT * z + 5) % block.shape[1], 1)
        first = lower if first is None else jnp.where(here, lower, first)
        second = upper if second is None else jnp.where(here, upper, second)
    return first, second


def pack_pair(first, second, to_next):
    edges = [jnp.where(to_next, second[b], first[b]) for b in range(len(first))]
    width = edges[0].shape[1]
    total = pltpu.roll(edges[0], jnp.where(to_next, width - 2, width - 3), 1)
    if len(edges) > 1:
        other = pltpu.roll(edges[1], jnp.where(to_next, 2, 1), 1)
        total = jnp.where(lanes_of(total.shape) % SLOT < 4, total, other)
    return total


def pack_y(fields, permittivity, strips, *to_y):
    layers, cells_x, width = fields.shape[1:]
    ring = cells_x + TILE
    for r in range(cells_x // TILE):
        rows = slice(r * TILE, (r + 1) * TILE)
        for q in range(PAIRS):
            pair = []
            for c in range(2 * q, min(2 * q + 2, PARTS)):

                def tile_of(z):
                    return fields[c, z, rows, :] if c < 6 else time_step / permittivity[z, rows, :]

                pair.append(pack_strips(tile_of, range(layers)))
                for side in (0, 1):
                    strips[side, c, rows, :] = pair[-1][side]
            for swap, message in enumerate(to_y):
                to_next = lax.axis_index("ys") % 2 == swap
                at = slice(q * ring + r * TILE, q * ring + (r + 1) * TILE)
                message[at, :] = pack_pair([p[0] for p in pair], [p[1] for p in pair], to_next)


def pack_corners(*refs, layers, n_rows, n_swaps):
    even, odd = refs[1 + n_swaps : 3 + n_swaps]
    strips, to_y = refs[-1 - n_swaps], refs[-n_swaps:]
    px = lax.axis_index("xs") % 2
    ring = (to_y[0].shape[0] - 3 * n_rows) // PAIRS
    for q in range(PAIRS):
        pair = []
        for c in range(2 * q, min(2 * q + 2, PARTS)):

            def tile_of(z):
                return halo_tile(even, odd, px, c, z, layers)

            pair.append(pack_strips(tile_of, range(layers)))
            for side in (0, 1):
                strips[side, c, ring - TILE : ring, :] = pair[-1][side]
        for swap, message in enumerate(to_y):
            to_next = lax.axis_index("ys") % 2 == swap
            at = slice((q + 1) * ring - TILE, (q + 1) * ring)
            message[at, :] = pack_pair([p[0] for p in pair], [p[1] for p in pair], to_next)
    if n_rows:
        blocks = refs[3 + n_swaps]
        end = PAIRS * ring
        x_end = PARTS * (layers // 2) * TILE
        to_y[0][end : end + n_rows, :] = blocks[...]
        to_y[0][end + n_rows : end + 2 * n_rows, :] = even[x_end:, :]
        to_y[0][end + 2 * n_rows : end + 3 * n_rows, :] = odd[x_end:, :]


def row_index(shape):
    fold = lax.broadcasted_iota(jnp.int32, shape, 0)
    return lax.broadcasted_iota(jnp.int32, shape, 1) * shape[0] + fold


def gather_sources(sets, px, me, source, n_adj, cells_x):
    full = source.shape[1:]
    row_at = row_index(full).astype(jnp.float32)
    mine = jnp.zeros(full, jnp.float32)
    other = jnp.zeros(full, jnp.float32)
    own_index = jnp.where(me == 0, 0.0, 1.0)
    for ref, start, is_next in sets:
        for b in range(n_adj):
            value = ref[start + b : start + b + 1, :]
            row = ref[start + n_adj + b : start + n_adj + b + 1, :]
            owner = ref[start + 2 * n_adj + b : start + 2 * n_adj + b + 1, :]
            if is_next is not None:
                after = jnp.where(row < REACH, row + cells_x, -1.0)
                before = jnp.where(row >= cells_x - REACH, row + TILE, -1.0)
                row = jnp.where(is_next, after, before)
            is_mine = owner == own_index
            mine = mine + jnp.where(row_at == jnp.where(is_mine, row, -1.0), value, 0.0)
            other = other + jnp.where(row_at == jnp.where(is_mine, -1.0, row), value, 0.0)
    lane = lanes_of(full)
    slot = (lane >= SLOT * ZS) & (lane < SLOT * (ZS + 1))
    place = lane - SLOT * ZS
    shift = SLOT * ZS + 3
    before = jnp.where(me == 0, 0.0, pltpu.roll(other, shift, 2))
    source[0] = mine
    source[1] = jnp.where(slot, jnp.where(place < 3, before, pltpu.roll(mine, shift, 2)), 0.0)
    shift = SLOT * ZS + 5
    after = jnp.where(me == 0, pltpu.roll(other, shift, 2), 0.0)
    source[2] = jnp.where(slot, jnp.where(place < 5, pltpu.roll(mine, shift, 2), after), 0.0)


def next_x(v):
    return jnp.concatenate([v[1:], pltpu.roll(v[0:1], v.shape[1] - 1, 1)], 0)


def prev_x(v):
    return jnp.concatenate([pltpu.roll(v[-1:], 1, 1), v[:-1]], 0)


def lane_roll(v, shift):
    return pltpu.roll(v, shift % v.shape[2], 2)


def zeros(shape):
    return jnp.zeros(shape, jnp.float32)


def unfold(ref, fold):
    return jnp.stack([ref[pl.ds(j, TILE, stride=fold), :] for j in range(fold)])


def fold_back(ref, v):
    for j in range(v.shape[0]):
        ref[pl.ds(j, TILE, stride=v.shape[0]), :] = v[j]


def step_size(full):
    outside = (row_index(full) >= full[0] * TILE - REACH) & (lax.axis_index("xs") == 0)
    return jnp.where(outside, 0.0, time_step)


def evolve_strips(strips, y_halos, source, strip, edge_e, edge_h):
    me = lax.axis_index("ys")
    ring, width = strips.shape[2:]
    fold = ring // TILE
    full = (fold, TILE, width)
    for q in range(PAIRS):
        for r in range(fold):
            before = jnp.zeros((TILE, width), jnp.float32)
            after = jnp.zeros((TILE, width), jnp.float32)
            at = q * ring + r * TILE
            for k, y_ref in enumerate(y_halos):
                block = y_ref[at : at + TILE, :]
                is_next = me % 2 == k
                after = jnp.where(is_next, block, after)
                before = jnp.where(is_next, before, block)
            place = lanes_of(before.shape) % SLOT
            rows = slice(r * TILE, (r + 1) * TILE)
            for c in range(2 * q, min(2 * q + 2, PARTS)):
                b = c % 2
                lower = pltpu.roll(before, width - 4, 1) if b else before
                upper = pltpu.roll(after, 1 if b else 5, 1)
                strip[0, c, rows, :] = jnp.where(place < 3, lower, strips[0, c, rows, :])
                strip[1, c, rows, :] = jnp.where(place >= 5, upper, strips[1, c, rows, :])
    lane = lanes_of(full)
    place = lane % SLOT
    for side in (0, 1):
        ex, ey, ez, hx, hy, hz, co = [unfold(strip.at[side, c], fold) for c in range(PARTS)]
        dt = step_size(full)
        if not side:
            dt = jnp.where((place < 3) & (me == 0), 0.0, dt)
        for step in range(STEPS):

            def next_z(v):
                return jnp.where(lane < width - SLOT, lane_roll(v, -SLOT), 0.0)

            def prev_z(v):
                return jnp.where(lane >= SLOT, lane_roll(v, SLOT), 0.0)

            if side:
                edge_e[step] = jnp.where(place == 5, ex, lane_roll(ez, 1))
                if step + 1 == STEPS:
                    continue
            hx = hx - dt * (lane_roll(ez, -1) - ez - (next_z(ey) - ey))
            hy = hy - dt * (next_z(ex) - ex - (next_x(ez) - ez))
            hz = hz - dt * (next_x(ey) - ey - (lane_roll(ex, -1) - ex))
            if not side:
                edge_h[step] = jnp.where(place == 2, hz, lane_roll(hx, 1))
                if step + 1 == STEPS:
                    continue
            ex = ex + co * (hz - lane_roll(hz, 1) - (hy - prev_z(hy)))
            ey = ey + co * (hx - prev_z(hx) - (hz - prev_x(hz)))
            ez = ez + co * (hy - prev_x(hy) - (hx - lane_roll(hx, 1)) - source[1 + side])


def surface_steps(*refs, n_adj, n_rows, n_swaps):
    fields, permittivity, even, odd = refs[:4]
    strips, y_halos, given = refs[4], refs[5 : 5 + n_swaps], refs[5 + n_swaps]
    out, source, edge_e, edge_h, grid, coeffs, state, strip = refs[6 + n_swaps :]
    px = lax.axis_index("xs") % 2
    layers, cells_x, width = fields.shape[1:]
    ring = cells_x + TILE
    fold = ring // TILE
    full = (fold, TILE, width)
    lane = lanes_of(full)
    used = range(max(ZS - STEPS, 0), min(ZS + STEPS + 1, layers))

    for z in used:
        for c in range(PARTS):
            ref = grid.at[c, z] if c < 6 else coeffs.at[z]
            ref[0:cells_x, :] = fields[c, z] if c < 6 else time_step / permittivity[z]
            ref[cells_x:ring, :] = halo_tile(even, odd, px, c, z, layers)

    if n_adj:
        end = PARTS * (layers // 2) * TILE
        y_end = PAIRS * ring
        sets = [
            (given, 0, None),
            (even, end, px == 0),
            (odd, end, px == 1),
            (y_halos[0], y_end, None),
            (y_halos[0], y_end + n_rows, px == 0),
            (y_halos[0], y_end + 2 * n_rows, px == 1),
        ]
        gather_sources(sets, px, lax.axis_index("ys"), source, n_adj, cells_x)
    else:
        source[...] = given[...]
    evolve_strips(strips, y_halos, source, strip, edge_e, edge_h)

    dt = step_size(full)
    for step in range(STEPS):
        final = step + 1 == STEPS
        low, high = max(ZS - STEPS + step, 0), min(ZS + STEPS - 1 - step, layers - 1)

        def load(c, z):
            return state[c, z] if step else unfold(grid.at[c, z], fold)

        def store(c, z, v):
            if final:
                fold_back(grid.at[c, z], v)
            else:
                state[c, z] = v

        below = None
        ex, ey = load(0, low), load(1, low)
        for z in range(low, high + 1):
            ez, hx, hy, hz = [load(c, z) for c in range(2, 6)]
            if z + 1 < layers:
                ex_above, ey_above = load(0, z + 1), load(1, z + 1)
            else:
                ex_above, ey_above = jnp.zeros(full, jnp.float32), jnp.zeros(full, jnp.float32)
            edge = lane_roll(edge_e[step], width - 1 - (SLOT * z + 5))
            ex_y = jnp.where(lane == width - 1, edge, lane_roll(ex, -1))
            ez_y = lane_roll(jnp.where(lane == 0, edge, ez), -1)
            hx = hx - dt * (ez_y - ez - (ey_above - ey))
            hy = hy - dt * (ex_above - ex - (next_x(ez) - ez))
            hz = hz - dt * (next_x(ey) - ey - (ex_y - ex))
            for c, v in ((3, hx), (4, hy), (5, hz)):
                store(c, z, v)
            if z == 0 or below:
                if step:
                    co = coeffs[z, 0:ring, :].reshape(full)
                else:
                    co = unfold(coeffs.at[z], fold)
                    coeffs[z, 0:ring, :] = co.reshape(ring, width)
                hx_z = hx - below[0] if z else hx
                hy_z = hy - below[1] if z else hy
                edge = lane_roll(edge_h[step], width - 1 - (SLOT * z + 2))
                hx_y = jnp.where(lane == 0, edge, lane_roll(hx, 1))
                hz_y = lane_roll(jnp.where(lane == width - 1, edge, hz), 1)
                store(0, z, ex + co * (hz - hz_y - hy_z))
                store(1, z, ey + co * (hx_z - (hz - prev_x(hz))))
                change = hy - prev_x(hy) - (hx - hx_y)
                if z == ZS:
                    change = change - source[0]
                store(2, z, ez + co * change)
            below = (hx, hy)
            ex, ey = ex_above, ey_above
    for k, (c, sign) in enumerate(((4, -1.0), (3, 1.0), (1, 1.0), (0, -1.0))):
        out[:, k * width : (k + 1) * width] = sign * grid[c, ZS, 0:cells_x, :]


def take_steps(first, last, layers, refs, load, store, load_coeff, after_layer=None):
    source, edge_e, edge_h = refs
    full = source.shape[1:]
    width = full[2]
    lane = lanes_of(full)
    dt = step_size(full)
    for step in range(first, last):

        def advance_h(z):
            ex, ey, ez, hx, hy, hz = [load(step, c, z) for c in range(6)]
            edge = lane_roll(edge_e[step], 2 * width - 1 - (SLOT * z + 5))
            ex_y = jnp.where(lane == width - 1, edge, lane_roll(ex, -1))
            ez_y = lane_roll(jnp.where(lane == 0, edge, ez), -1)
            store(step, 3, z, hx - dt * (ez_y - ez - (load(step, 1, z + 1) - ey)))
            store(step, 4, z, hy - dt * (load(step, 0, z + 1) - ex - (next_x(ez) - ez)))
            store(step, 5, z, hz - dt * (next_x(ey) - ey - (ex_y - ex)))

        def advance_e(z):
            hx, hy, hz = [load(step + 1, c, z) for c in range(3, 6)]
            co = load_coeff(z)
            edge = lane_roll(edge_h[step], 2 * width - 1 - (SLOT * z + 2))
            hx_y = jnp.where(lane == 0, edge, lane_roll(hx, 1))
            hz_y = lane_roll(jnp.where(lane == width - 1, edge, hz), 1)
            change = hz - hz_y - (hy - load(step + 1, 4, z - 1))
            store(step, 0, z, load(step, 0, z) + co * change)
            change = hx - load(step + 1, 3, z - 1) - (hz - prev_x(hz))
            store(step, 1, z, load(step, 1, z) + co * change)
            change = hy - prev_x(hy) - (hx - hx_y) - jnp.where(z == ZS, source[0], 0.0)
            store(step, 2, z, load(step, 2, z) + co * change)
            if after_layer and step + 1 == last:
                after_layer(z)

        repeat(0, layers, advance_h, TOGETHER)
        repeat(0, layers, advance_e, TOGETHER)


def zero_outside(ref, layers):
    for c in (0, 1):
        ref[c, layers + 1] = zeros(ref.shape[2:])
        ref[c + 3, 0] = zeros(ref.shape[2:])


def first_step(*refs):
    fields, permittivity, even, odd, *carried = refs[:7]
    state, coeffs, grid, coeff_rows = refs[7:]
    px = lax.axis_index("xs") % 2
    layers, cells_x, width = fields.shape[1:]
    ring = cells_x + TILE
    fold = ring // TILE

    def build(z):
        for c in range(PARTS):
            ref = grid.at[c, z + 1] if c < 6 else coeff_rows.at[z]
            ref[0:cells_x, :] = fields[c, z] if c < 6 else time_step / permittivity[z]
            ref[cells_x:ring, :] = halo_tile(even, odd, px, c, z, layers)
        coeffs[z] = unfold(coeff_rows.at[z], fold)

    repeat(0, layers, build, TOGETHER // 2)
    for c in (0, 1):
        grid[c, layers + 1] = zeros((ring, width))
    zero_outside(state, layers)

    def load(step, c, z):
        return state[c, z + 1] if step else unfold(grid.at[c, z + 1], fold)

    def store(step, c, z, v):
        state[c, z + 1] = v

    take_steps(0, 1, layers, carried, load, store, lambda z: coeffs[z])


def later_steps(*refs):
    before, coeffs, *carried = refs[:5]
    out, state, grid, sems = refs[5:]
    layers, cells_x = out.shape[1:3]

    def copy_out(z):
        done = grid.at[:, z, pl.ds(0, cells_x), :]
        return pltpu.make_async_copy(done, out.at[:, z], sems.at[z])

    zero_outside(state, layers)

    def load(step, c, z):
        return (before if step == 1 else state)[c, z + 1]

    def store(step, c, z, v):
        if step + 1 < STEPS or c >= 3:
            state[c, z + 1] = v
        if step + 1 == STEPS:
            fold_back(grid.at[c, z], v)

    take_steps(
        1,
        STEPS,
        layers,
        carried,
        lambda step, c, z: load(1 if step == 1 else 2, c, z),
        store,
        lambda z: coeffs[z],
        lambda z: copy_out(z).start(),
    )
    repeat(0, layers, lambda z: copy_out(z).wait())


def multiply(weights, *refs, n_tiles):
    tiles, parts = refs[:n_tiles], refs[n_tiles:]
    total = jnp.dot(
        weights[...],
        jnp.concatenate([tile[...] for tile in tiles], 0),
        precision=lax.Precision.HIGHEST,
        preferred_element_type=jnp.float32,
    )
    rows = parts[0].shape[0]
    for k, part in enumerate(parts):
        part[...] = total[k * rows : (k + 1) * rows]


def add_parts(*refs):
    parts, out = refs[:-1], refs[-1]
    total = parts[0][...]
    for part in parts[1:]:
        total = total + part[...]
    width = out.shape[2]
    for k in range(out.shape[1]):
        out[:, k, :] = total[:, k * width : (k + 1) * width]


def shape_of(*dims):
    return jax.ShapeDtypeStruct(dims, jnp.float32)


def far_field_weights(angle_wave, xs_size, cells_x, near):
    me = lax.axis_index("xs")
    per_block = angle_wave.shape[0] // xs_size
    far = xs_size // near
    bits = far.bit_length() - 1
    view = angle_wave.reshape(far, near, per_block)
    pick = jnp.arange(near, dtype=jnp.int32)[None, :, None] == me % near
    view = jnp.sum(jnp.where(pick, view, 0), axis=1).reshape((2,) * bits + (per_block,))
    for k in range(bits):
        bit = (me // near >> (bits - 1 - k)) & 1
        view = jnp.where(bit == 1, jnp.flip(view, k), view)
    angles = view.reshape(-1)
    owners = me ^ jnp.arange(near, dtype=jnp.int32)
    within = jnp.arange(cells_x, dtype=jnp.int32)
    positions = X0 + (owners[:, None] * cells_x + within[None, :]).reshape(-1)
    phase = angles[:, None] * positions[None, :] % GRID_X
    angle = phase.astype(jnp.float32) * (2.0 * math.pi / GRID_X)
    scale = 1.0 / math.sqrt(cells_x * xs_size)
    both = jnp.stack([jnp.cos(angle) * scale, -jnp.sin(angle) * scale], axis=1)
    return both.reshape(-1, near * cells_x)


def far_field_exchange(tile, angle_wave, xs_size, beside, finish):
    cells_x, columns = tile.shape
    near = 4
    weights = far_field_weights(angle_wave, xs_size, cells_x, near)

    def across(block, mask):
        return lax.ppermute(block, "xs", [(i, i ^ mask) for i in range(xs_size)])

    third = across(tile, 2)
    second = across(tile, 1)
    third, beside = lax.optimization_barrier((third, beside))
    fourth = across(third, 1)
    far = xs_size // near
    rows = weights.shape[0] // far
    parts = pl.pallas_call(
        functools.partial(multiply, n_tiles=near),
        out_shape=(shape_of(rows, columns),) * far,
        in_specs=[VMEM] * (near + 1),
        out_specs=(VMEM,) * far,
        compiler_params=PARAMS,
        name="partial_spectrum",
    )(weights, tile, second, third, fourth)
    arrived = [across(parts[k], k * near) for k in range(far - 1, 0, -1)]
    finished = finish(beside)
    far_field = pl.pallas_call(
        add_parts,
        out_shape=shape_of(rows, 4, columns // 4),
        in_specs=[VMEM] * far,
        out_specs=VMEM,
        compiler_params=PARAMS,
        name="add_arrived",
    )(parts[0], *arrived)
    return far_field, finished


def gathered_sources(adj_values, adj_owner, adj_row, cells_x, cells_y):
    groups = lax.axis_size("ys")
    owners = adj_owner[:, 0]
    hits = (owners[:, None] == jnp.arange(groups, dtype=jnp.int32)[None, :]).astype(jnp.int32)
    before = jnp.cumsum(hits, axis=0) - hits
    slot_index = owners * CAP + jnp.sum(before * hits, axis=1)
    placing = (jnp.arange(groups * CAP, dtype=jnp.int32)[:, None] == slot_index[None, :]).astype(
        jnp.float32
    )
    rows = jnp.broadcast_to(adj_row.astype(jnp.float32)[:, None], (adj_row.shape[0], 1))
    outgoing = jnp.dot(
        placing, jnp.concatenate([adj_values, rows], 1), precision=lax.Precision.HIGHEST
    ).reshape(groups, CAP, cells_y + 1)
    incoming = lax.all_to_all(outgoing, "ys", split_axis=0, concat_axis=0, tiled=True)
    incoming = incoming.reshape(groups * CAP, cells_y + 1)
    landing = (
        jnp.arange(cells_x, dtype=jnp.float32)[:, None] == incoming[:, cells_y][None, :]
    ).astype(jnp.float32)
    current = jnp.dot(landing, incoming[:, :cells_y], precision=lax.Precision.HIGHEST)

    def shifted(block, axis, distance):
        size = lax.axis_size(axis)
        route = [(i, i + distance) for i in range(size) if 0 <= i + distance < size]
        return lax.ppermute(block, axis, route)

    after = shifted(current[:REACH], "xs", -1)
    before = shifted(current[-REACH:], "xs", 1)
    ringed = jnp.concatenate([current, after, before], 0)
    right = shifted(ringed[:, :3], "ys", -1)
    left = shifted(ringed[:, -3:], "ys", 1)
    start, end = SLOT * ZS, cells_y - SLOT * (ZS + 1)
    first = jnp.pad(jnp.concatenate([left, ringed[:, :5]], 1), ((0, 0), (start, end)))
    second = jnp.pad(jnp.concatenate([ringed[:, -5:], right], 1), ((0, 0), (start, end)))
    folded = jnp.stack([ringed, first, second]).reshape(3, TILE, -1, cells_y)
    return folded.transpose(0, 2, 1, 3)


def on_device(fields, permittivity, adj_values, adj_owner, adj_row, angle_wave):
    layers, cells_x, cells_y = fields.shape[1:]
    xs_size, ys_size = lax.axis_size("xs"), lax.axis_size("ys")
    raw = ys_size == 2
    n_adj = adj_values.shape[0] if raw else 0
    n_rows = -(-3 * n_adj // TILE) * TILE
    ring = cells_x + TILE
    x_rows = PARTS * (layers // 2) * TILE + n_rows
    y_rows = PAIRS * ring + 3 * n_rows

    extra = (adj_values, adj_row, adj_owner.reshape(-1)) if raw else ()
    packed = pl.pallas_call(
        functools.partial(pack_x, n_adj=n_adj),
        out_shape=(shape_of(x_rows, cells_y),) * 2 + ((shape_of(n_rows, cells_y),) if raw else ()),
        in_specs=[ANY] * (2 + len(extra)),
        out_specs=(VMEM,) * (3 if raw else 2),
        scratch_shapes=[
            pltpu.VMEM((2, 6, layers, TILE, cells_y), jnp.float32),
            pltpu.VMEM((2, layers, TILE, cells_y), jnp.float32),
        ]
        + ([pltpu.SMEM((n_adj,), jnp.int32)] * 2 if raw else [])
        + [pltpu.SemaphoreType.DMA((4 + len(extra),))],
        compiler_params=PARAMS,
        name="pack_x_edges",
    )(*[pltpu.with_memory_space_constraint(x, pltpu.HBM) for x in (fields, permittivity, *extra)])
    blocks = packed[2:]
    x_even, x_odd = swaps(xs_size)
    from_even = lax.ppermute(packed[0], "xs", x_even)
    from_odd = lax.ppermute(packed[1], "xs", x_odd)

    y_swaps = swaps(ys_size)
    strips_shape = shape_of(2, PARTS, ring, cells_y)
    made = (strips_shape,) + (shape_of(y_rows, cells_y),) * len(y_swaps)
    packed = pl.pallas_call(
        pack_y,
        out_shape=made,
        in_specs=[VMEM] * 2,
        out_specs=(VMEM,) * len(made),
        compiler_params=PARAMS,
        name="pack_y_edges",
    )(fields, permittivity)
    strips, *to_y = pl.pallas_call(
        functools.partial(pack_corners, layers=layers, n_rows=n_rows, n_swaps=len(y_swaps)),
        out_shape=made,
        in_specs=[VMEM] * (len(made) + 2 + len(blocks)),
        out_specs=(VMEM,) * len(made),
        input_output_aliases={k: k for k in range(len(made))},
        compiler_params=PARAMS,
        name="pack_corners",
    )(*packed, from_even, from_odd, *blocks)
    y_halos = [lax.ppermute(message, "ys", route) for message, route in zip(to_y, y_swaps)]

    if raw:
        sources = blocks
    else:
        sources = (gathered_sources(adj_values, adj_owner, adj_row, cells_x, cells_y),)

    fold = ring // TILE
    folded = (fold, TILE, cells_y)
    operands = (fields, permittivity, from_even, from_odd, strips, *y_halos, *sources)
    tile, *carried = pl.pallas_call(
        functools.partial(surface_steps, n_adj=n_adj, n_rows=n_rows, n_swaps=len(y_swaps)),
        out_shape=(
            shape_of(cells_x, 4 * cells_y),
            shape_of(3, *folded),
            shape_of(STEPS, *folded),
            shape_of(STEPS, *folded),
        ),
        in_specs=[VMEM] * len(operands),
        out_specs=(VMEM,) * 4,
        scratch_shapes=[
            pltpu.VMEM((6, layers, ring, cells_y), jnp.float32),
            pltpu.VMEM((layers, ring, cells_y), jnp.float32),
            pltpu.VMEM((6, layers, *folded), jnp.float32),
            pltpu.VMEM((2, PARTS, ring, cells_y), jnp.float32),
        ],
        compiler_params=PARAMS,
        name="surface_steps",
    )(*operands)

    state_shape = (6, layers + 2, *folded)
    operands = (fields, permittivity, from_even, from_odd, *carried)
    stepped = pl.pallas_call(
        first_step,
        out_shape=(shape_of(*state_shape), shape_of(layers, *folded)),
        in_specs=[VMEM] * len(operands),
        out_specs=(VMEM, VMEM),
        scratch_shapes=[
            pltpu.VMEM((6, layers + 2, ring, cells_y), jnp.float32),
            pltpu.VMEM((layers, ring, cells_y), jnp.float32),
        ],
        compiler_params=PARAMS,
        name="first_step",
    )(*operands)

    def finish(stepped):
        return pl.pallas_call(
            later_steps,
            out_shape=shape_of(*fields.shape),
            in_specs=[VMEM] * 5,
            out_specs=ANY,
            scratch_shapes=[
                pltpu.VMEM(state_shape, jnp.float32),
                pltpu.VMEM((6, layers, ring, cells_y), jnp.float32),
                pltpu.SemaphoreType.DMA((layers,)),
            ],
            compiler_params=PARAMS,
            name="later_steps",
        )(*stepped, *carried)

    far, new_fields = far_field_exchange(tile, angle_wave, xs_size, stepped, finish)
    per_block = angle_wave.shape[0] // xs_size
    return (new_fields, far.reshape(per_block, 2, 4, cells_y))


def solution(mesh):
    placed = (
        P(None, None, "xs", "ys"),
        P(None, "xs", "ys"),
        P(("xs", "ys"), None),
        P(("xs", "ys"), None),
        P(("xs", "ys")),
        P(),
    )
    return jax.shard_map(
        on_device,
        mesh=mesh,
        in_specs=placed,
        out_specs=(P(None, None, "xs", "ys"), P("xs", None, None, "ys")),
        check_vma=False,
    )
```

```python
import functools
import math

import jax
import jax.numpy as jnp
from jax import lax
from jax.experimental import pallas as pl
from jax.experimental.pallas import tpu as pltpu
from jax.sharding import PartitionSpec as P

STEPS = 3
CAP = 4
GRID_X = 5000
X0 = 2000
ZS = 8

time_step = 0.5

TILE = 8
REACH = 4
SLOT = 8
PARTS = 7
X_GROUPS = ((0, 1, 3), (2, 4, 6), (5,))
Y_GROUPS = ((0, 2, 4), (1, 3, 6), (5,))
TOGETHER = 8

VMEM = pl.BlockSpec(memory_space=pltpu.VMEM)
ANY = pl.BlockSpec(memory_space=pl.ANY)
PARAMS = pltpu.CompilerParams(vmem_limit_bytes=24 * 1024 * 1024)


def lanes_of(shape):
    return lax.broadcasted_iota(jnp.int32, shape, len(shape) - 1)


def rows_of(shape):
    return lax.broadcasted_iota(jnp.int32, shape, len(shape) - 2)


def swaps(size):
    found = []
    for first in (0, 1):
        pairs = [(i, i + 1) for i in range(first, size - 1, 2)]
        if pairs:
            found.append(pairs + [(j, i) for i, j in pairs])
    return found


def x_message_rows(layers):
    return (2 * layers + layers // 2) * TILE


def halo_tile(even, odd, px, c, z, layers):
    group = [c in parts for parts in X_GROUPS].index(True)
    slot = X_GROUPS[group].index(c)
    tile = 2 * z + group if group < 2 else 2 * layers + z // 2
    at = pl.ds(tile * TILE if isinstance(z, int) else pl.multiple_of(tile * TILE, TILE), TILE)
    from_even, from_odd = even[at, :], odd[at, :]
    after = jnp.where(px == 0, from_even, from_odd)
    before = jnp.where(px == 0, from_odd, from_even)
    lower = rows_of(after.shape) < REACH

    def placed(first, count):
        back = (TILE - first) % TILE
        to_end = (TILE - count - first) % TILE
        return jnp.where(
            lower,
            pltpu.roll(after, back, 0) if back else after,
            pltpu.roll(before, to_end, 0) if to_end else before,
        )

    if group < 2:
        return placed(3 * slot, 3 if slot < 2 else 2)
    if isinstance(z, int):
        return placed(4 * (z % 2), 3)
    return jnp.where(z % 2 == 0, placed(0, 3), placed(4, 3))


def repeat(first, last, body, together=1):
    count = last - first
    if together >= count:
        for i in range(first, last):
            body(i)
        return
    rounds = count // together

    def several(n, _):
        for k in range(together):
            body(first + n * together + k)

    lax.fori_loop(0, rounds, several, None)
    for i in range(first + rounds * together, last):
        body(i)


def pack_x(*refs, n_adj):
    fields, permittivity = refs[:2]
    if n_adj:
        values, rows, owners, to_even, to_odd, blocks = refs[2:8]
        edges, edge_perm, rows_s, owners_s, sems = refs[8:]
    else:
        to_even, to_odd, edges, edge_perm, sems = refs[2:]
    px = lax.axis_index("xs") % 2
    layers, cells_x = fields.shape[1:3]
    copies = []
    for k, start in enumerate((0, cells_x - TILE)):
        rows_at = pl.ds(start, TILE)
        copies.append((fields.at[:, :, rows_at, :], edges.at[k]))
        copies.append((permittivity.at[:, rows_at, :], edge_perm.at[k]))
    if n_adj:
        blocks[...] = jnp.zeros(blocks.shape, jnp.float32)
        copies.append((values, blocks.at[pl.ds(0, n_adj), :]))
        copies.append((rows, rows_s))
        copies.append((owners, owners_s))
    copies = [pltpu.make_async_copy(s, d, sems.at[k]) for k, (s, d) in enumerate(copies)]
    for copy in copies:
        copy.start()
    for copy in copies:
        copy.wait()

    def both(c, z):
        if c < 6:
            return edges[0, c, z], edges[1, c, z]
        return time_step / edge_perm[0, z], time_step / edge_perm[1, z]

    def send(tile, first, last):
        at = slice(tile * TILE, (tile + 1) * TILE)
        to_even[at, :] = jnp.where(px == 0, last, first)
        to_odd[at, :] = jnp.where(px == 0, first, last)

    def turn(v, shift):
        return pltpu.roll(v, shift, 0)

    row = rows_of((TILE, fields.shape[3]))
    for z in range(layers):
        for g in range(2):
            (lo0, hi0), (lo1, hi1), (lo2, hi2) = [both(c, z) for c in X_GROUPS[g]]
            first = jnp.where(row < 3, lo0, jnp.where(row < 6, turn(lo1, 3), turn(lo2, 6)))
            last = jnp.where(row < 3, turn(hi0, 3), jnp.where(row < 6, turn(hi1, 6), hi2))
            send(2 * z + g, first, last)
    for pair in range(layers // 2):
        (lo0, hi0), (lo1, hi1) = [both(X_GROUPS[2][0], 2 * pair + k) for k in (0, 1)]
        first = jnp.where(row < 4, lo0, turn(lo1, 4))
        last = jnp.where(row < 4, turn(hi0, 3), turn(hi1, 7))
        send(2 * layers + pair, first, last)
    if n_adj:
        for b in range(n_adj):
            one = (1, blocks.shape[1])
            row, owner = n_adj + b, 2 * n_adj + b
            blocks[row : row + 1, :] = jnp.full(one, rows_s[b], jnp.int32).astype(jnp.float32)
            blocks[owner : owner + 1, :] = jnp.full(one, owners_s[b], jnp.int32).astype(
                jnp.float32
            )
        end = x_message_rows(layers)
        to_even[end:, :] = blocks[...]
        to_odd[end:, :] = blocks[...]


def pack_strips(tile_of, layers):
    first = second = None
    for z in layers:
        block = tile_of(z)
        here = lanes_of(block.shape) // SLOT == z
        lower = pltpu.roll(block, (SLOT * z + 3) % block.shape[1], 1)
        upper = pltpu.roll(block, (SLOT * z + 5) % block.shape[1], 1)
        first = lower if first is None else jnp.where(here, lower, first)
        second = upper if second is None else jnp.where(here, upper, second)
    return first, second


def pack_group(first, second, to_next):
    edges = [jnp.where(to_next, upper, lower) for lower, upper in zip(first, second)]
    width = edges[0].shape[1]
    place = lanes_of(edges[0].shape) % SLOT
    total = pltpu.roll(edges[0], jnp.where(to_next, width - 2, width - 3), 1)
    if len(edges) > 1:
        middle = pltpu.roll(edges[1], jnp.where(to_next, 1, 0), 1)
        total = jnp.where(place < 3, total, jnp.where(place < 6, middle, pltpu.roll(edges[2], 3, 1)))
    return total


def place_group(before, after, slot):
    width = before.shape[1]
    lower, upper = ((0, 5), (width - 3, 2), (width - 5, width - 1))[slot]
    return (pltpu.roll(before, lower, 1) if lower else before), pltpu.roll(after, upper, 1)


def pack_y(fields, permittivity, strips, *to_y):
    layers, cells_x, width = fields.shape[1:]
    ring = cells_x + TILE
    for r in range(cells_x // TILE):
        rows = slice(r * TILE, (r + 1) * TILE)
        for g, parts in enumerate(Y_GROUPS):
            packed = []
            for c in parts:

                def tile_of(z):
                    return fields[c, z, rows, :] if c < 6 else time_step / permittivity[z, rows, :]

                packed.append(pack_strips(tile_of, range(layers)))
                for side in (0, 1):
                    strips[side, c, rows, :] = packed[-1][side]
            for swap, message in enumerate(to_y):
                to_next = lax.axis_index("ys") % 2 == swap
                at = slice(g * ring + r * TILE, g * ring + (r + 1) * TILE)
                message[at, :] = pack_group([p[0] for p in packed], [p[1] for p in packed], to_next)


def pack_corners(*refs, layers, n_rows, n_swaps):
    even, odd = refs[1 + n_swaps : 3 + n_swaps]
    strips, to_y = refs[-1 - n_swaps], refs[-n_swaps:]
    px = lax.axis_index("xs") % 2
    ring = (to_y[0].shape[0] - 3 * n_rows) // len(Y_GROUPS)
    for g, parts in enumerate(Y_GROUPS):
        packed = []
        for c in parts:

            def tile_of(z):
                return halo_tile(even, odd, px, c, z, layers)

            packed.append(pack_strips(tile_of, range(layers)))
            for side in (0, 1):
                strips[side, c, ring - TILE : ring, :] = packed[-1][side]
        for swap, message in enumerate(to_y):
            to_next = lax.axis_index("ys") % 2 == swap
            at = slice((g + 1) * ring - TILE, (g + 1) * ring)
            message[at, :] = pack_group([p[0] for p in packed], [p[1] for p in packed], to_next)
    if n_rows:
        blocks = refs[3 + n_swaps]
        end = len(Y_GROUPS) * ring
        x_end = x_message_rows(layers)
        to_y[0][end : end + n_rows, :] = blocks[...]
        to_y[0][end + n_rows : end + 2 * n_rows, :] = even[x_end:, :]
        to_y[0][end + 2 * n_rows : end + 3 * n_rows, :] = odd[x_end:, :]


def row_index(shape):
    fold = lax.broadcasted_iota(jnp.int32, shape, 0)
    return lax.broadcasted_iota(jnp.int32, shape, 1) * shape[0] + fold


def gather_sources(sets, px, me, source, n_adj, cells_x):
    full = source.shape[1:]
    row_at = row_index(full).astype(jnp.float32)
    mine = jnp.zeros(full, jnp.float32)
    other = jnp.zeros(full, jnp.float32)
    own_index = jnp.where(me == 0, 0.0, 1.0)
    for ref, start, is_next in sets:
        for b in range(n_adj):
            value = ref[start + b : start + b + 1, :]
            row = ref[start + n_adj + b : start + n_adj + b + 1, :]
            owner = ref[start + 2 * n_adj + b : start + 2 * n_adj + b + 1, :]
            if is_next is not None:
                after = jnp.where(row < REACH, row + cells_x, -1.0)
                before = jnp.where(row >= cells_x - REACH, row + TILE, -1.0)
                row = jnp.where(is_next, after, before)
            is_mine = owner == own_index
            mine = mine + jnp.where(row_at == jnp.where(is_mine, row, -1.0), value, 0.0)
            other = other + jnp.where(row_at == jnp.where(is_mine, -1.0, row), value, 0.0)
    lane = lanes_of(full)
    slot = (lane >= SLOT * ZS) & (lane < SLOT * (ZS + 1))
    place = lane - SLOT * ZS
    shift = SLOT * ZS + 3
    before = jnp.where(me == 0, 0.0, pltpu.roll(other, shift, 2))
    source[0] = mine
    source[1] = jnp.where(slot, jnp.where(place < 3, before, pltpu.roll(mine, shift, 2)), 0.0)
    shift = SLOT * ZS + 5
    after = jnp.where(me == 0, pltpu.roll(other, shift, 2), 0.0)
    source[2] = jnp.where(slot, jnp.where(place < 5, pltpu.roll(mine, shift, 2), after), 0.0)


def next_x(v):
    return jnp.concatenate([v[1:], pltpu.roll(v[0:1], v.shape[1] - 1, 1)], 0)


def prev_x(v):
    return jnp.concatenate([pltpu.roll(v[-1:], 1, 1), v[:-1]], 0)


def lane_roll(v, shift):
    return pltpu.roll(v, shift % v.shape[2], 2)


def zeros(shape):
    return jnp.zeros(shape, jnp.float32)


def unfold(ref, fold):
    return jnp.stack([ref[pl.ds(j, TILE, stride=fold), :] for j in range(fold)])


def fold_back(ref, v):
    for j in range(v.shape[0]):
        ref[pl.ds(j, TILE, stride=v.shape[0]), :] = v[j]


def step_size(full):
    outside = (row_index(full) >= full[0] * TILE - REACH) & (lax.axis_index("xs") == 0)
    return jnp.where(outside, 0.0, time_step)


def evolve_strips(strips, y_halos, source, strip, edge_e, edge_h):
    me = lax.axis_index("ys")
    ring, width = strips.shape[2:]
    fold = ring // TILE
    full = (fold, TILE, width)
    for g, parts in enumerate(Y_GROUPS):
        for r in range(fold):
            before, after = zeros((TILE, width)), zeros((TILE, width))
            at = g * ring + r * TILE
            for k, y_ref in enumerate(y_halos):
                block = y_ref[at : at + TILE, :]
                is_next = me % 2 == k
                after = jnp.where(is_next, block, after)
                before = jnp.where(is_next, before, block)
            place = lanes_of(before.shape) % SLOT
            rows = slice(r * TILE, (r + 1) * TILE)
            for slot, c in enumerate(parts):
                lower, upper = place_group(before, after, slot)
                strip[0, c, rows, :] = jnp.where(place < 3, lower, strips[0, c, rows, :])
                strip[1, c, rows, :] = jnp.where(place >= 5, upper, strips[1, c, rows, :])
    lane = lanes_of(full)
    place = lane % SLOT
    for side in (0, 1):
        ex, ey, ez, hx, hy, hz, co = [unfold(strip.at[side, c], fold) for c in range(PARTS)]
        dt = step_size(full)
        if not side:
            dt = jnp.where((place < 3) & (me == 0), 0.0, dt)
        for step in range(STEPS):

            def next_z(v):
                return jnp.where(lane < width - SLOT, lane_roll(v, -SLOT), 0.0)

            def prev_z(v):
                return jnp.where(lane >= SLOT, lane_roll(v, SLOT), 0.0)

            if side:
                edge_e[step] = jnp.where(place == 5, ex, lane_roll(ez, 1))
                if step + 1 == STEPS:
                    continue
            hx = hx - dt * (lane_roll(ez, -1) - ez - (next_z(ey) - ey))
            hy = hy - dt * (next_z(ex) - ex - (next_x(ez) - ez))
            hz = hz - dt * (next_x(ey) - ey - (lane_roll(ex, -1) - ex))
            if not side:
                edge_h[step] = jnp.where(place == 2, hz, lane_roll(hx, 1))
                if step + 1 == STEPS:
                    continue
            ex = ex + co * (hz - lane_roll(hz, 1) - (hy - prev_z(hy)))
            ey = ey + co * (hx - prev_z(hx) - (hz - prev_x(hz)))
            ez = ez + co * (hy - prev_x(hy) - (hx - lane_roll(hx, 1)) - source[1 + side])


def surface_steps(*refs, n_adj, n_rows, n_swaps):
    fields, permittivity, even, odd = refs[:4]
    strips, y_halos, given = refs[4], refs[5 : 5 + n_swaps], refs[5 + n_swaps]
    out, source, edge_e, edge_h, grid, coeffs, state, strip = refs[6 + n_swaps :]
    px = lax.axis_index("xs") % 2
    layers, cells_x, width = fields.shape[1:]
    ring = cells_x + TILE
    fold = ring // TILE
    full = (fold, TILE, width)
    lane = lanes_of(full)
    used = range(max(ZS - STEPS, 0), min(ZS + STEPS + 1, layers))

    for z in used:
        for c in range(PARTS):
            ref = grid.at[c, z] if c < 6 else coeffs.at[z]
            ref[0:cells_x, :] = fields[c, z] if c < 6 else time_step / permittivity[z]
            ref[cells_x:ring, :] = halo_tile(even, odd, px, c, z, layers)

    if n_adj:
        end = x_message_rows(layers)
        y_end = len(Y_GROUPS) * ring
        sets = [
            (given, 0, None),
            (even, end, px == 0),
            (odd, end, px == 1),
            (y_halos[0], y_end, None),
            (y_halos[0], y_end + n_rows, px == 0),
            (y_halos[0], y_end + 2 * n_rows, px == 1),
        ]
        gather_sources(sets, px, lax.axis_index("ys"), source, n_adj, cells_x)
    else:
        source[...] = given[...]
    evolve_strips(strips, y_halos, source, strip, edge_e, edge_h)

    dt = step_size(full)
    for step in range(STEPS):
        final = step + 1 == STEPS
        low, high = max(ZS - STEPS + step, 0), min(ZS + STEPS - 1 - step, layers - 1)

        def load(c, z):
            return state[c, z] if step else unfold(grid.at[c, z], fold)

        def store(c, z, v):
            if final:
                fold_back(grid.at[c, z], v)
            else:
                state[c, z] = v

        below = None
        ex, ey = load(0, low), load(1, low)
        for z in range(low, high + 1):
            ez, hx, hy, hz = [load(c, z) for c in range(2, 6)]
            if z + 1 < layers:
                ex_above, ey_above = load(0, z + 1), load(1, z + 1)
            else:
                ex_above, ey_above = jnp.zeros(full, jnp.float32), jnp.zeros(full, jnp.float32)
            edge = lane_roll(edge_e[step], width - 1 - (SLOT * z + 5))
            ex_y = jnp.where(lane == width - 1, edge, lane_roll(ex, -1))
            ez_y = lane_roll(jnp.where(lane == 0, edge, ez), -1)
            hx = hx - dt * (ez_y - ez - (ey_above - ey))
            hy = hy - dt * (ex_above - ex - (next_x(ez) - ez))
            hz = hz - dt * (next_x(ey) - ey - (ex_y - ex))
            for c, v in ((3, hx), (4, hy), (5, hz)):
                store(c, z, v)
            if z == 0 or below:
                if step:
                    co = coeffs[z, 0:ring, :].reshape(full)
                else:
                    co = unfold(coeffs.at[z], fold)
                    coeffs[z, 0:ring, :] = co.reshape(ring, width)
                hx_z = hx - below[0] if z else hx
                hy_z = hy - below[1] if z else hy
                edge = lane_roll(edge_h[step], width - 1 - (SLOT * z + 2))
                hx_y = jnp.where(lane == 0, edge, lane_roll(hx, 1))
                hz_y = lane_roll(jnp.where(lane == width - 1, edge, hz), 1)
                store(0, z, ex + co * (hz - hz_y - hy_z))
                store(1, z, ey + co * (hx_z - (hz - prev_x(hz))))
                change = hy - prev_x(hy) - (hx - hx_y)
                if z == ZS:
                    change = change - source[0]
                store(2, z, ez + co * change)
            below = (hx, hy)
            ex, ey = ex_above, ey_above
    for k, (c, sign) in enumerate(((4, -1.0), (3, 1.0), (1, 1.0), (0, -1.0))):
        out[:, k * width : (k + 1) * width] = sign * grid[c, ZS, 0:cells_x, :]


def take_steps(first, last, layers, refs, load, store, load_coeff, after_layer=None):
    source, edge_e, edge_h = refs
    full = source.shape[1:]
    width = full[2]
    lane = lanes_of(full)
    dt = step_size(full)
    for step in range(first, last):

        def advance_h(z):
            ex, ey, ez, hx, hy, hz = [load(step, c, z) for c in range(6)]
            edge = lane_roll(edge_e[step], 2 * width - 1 - (SLOT * z + 5))
            ex_y = jnp.where(lane == width - 1, edge, lane_roll(ex, -1))
            ez_y = lane_roll(jnp.where(lane == 0, edge, ez), -1)
            store(step, 3, z, hx - dt * (ez_y - ez - (load(step, 1, z + 1) - ey)))
            store(step, 4, z, hy - dt * (load(step, 0, z + 1) - ex - (next_x(ez) - ez)))
            store(step, 5, z, hz - dt * (next_x(ey) - ey - (ex_y - ex)))

        def advance_e(z):
            hx, hy, hz = [load(step + 1, c, z) for c in range(3, 6)]
            co = load_coeff(z)
            edge = lane_roll(edge_h[step], 2 * width - 1 - (SLOT * z + 2))
            hx_y = jnp.where(lane == 0, edge, lane_roll(hx, 1))
            hz_y = lane_roll(jnp.where(lane == width - 1, edge, hz), 1)
            change = hz - hz_y - (hy - load(step + 1, 4, z - 1))
            store(step, 0, z, load(step, 0, z) + co * change)
            change = hx - load(step + 1, 3, z - 1) - (hz - prev_x(hz))
            store(step, 1, z, load(step, 1, z) + co * change)
            change = hy - prev_x(hy) - (hx - hx_y) - jnp.where(z == ZS, source[0], 0.0)
            store(step, 2, z, load(step, 2, z) + co * change)
            if after_layer and step + 1 == last:
                after_layer(z)

        repeat(0, layers, advance_h, TOGETHER)
        repeat(0, layers, advance_e, TOGETHER)


def zero_outside(ref, layers):
    for c in (0, 1):
        ref[c, layers + 1] = zeros(ref.shape[2:])
        ref[c + 3, 0] = zeros(ref.shape[2:])


def first_step(*refs):
    fields, permittivity, even, odd, *carried = refs[:7]
    state, coeffs, grid, coeff_rows = refs[7:]
    px = lax.axis_index("xs") % 2
    layers, cells_x, width = fields.shape[1:]
    ring = cells_x + TILE
    fold = ring // TILE

    def build(z):
        for c in range(PARTS):
            ref = grid.at[c, z + 1] if c < 6 else coeff_rows.at[z]
            ref[0:cells_x, :] = fields[c, z] if c < 6 else time_step / permittivity[z]
            ref[cells_x:ring, :] = halo_tile(even, odd, px, c, z, layers)
        coeffs[z] = unfold(coeff_rows.at[z], fold)

    repeat(0, layers, build, TOGETHER // 2)
    for c in (0, 1):
        grid[c, layers + 1] = zeros((ring, width))
    zero_outside(state, layers)

    def load(step, c, z):
        return state[c, z + 1] if step else unfold(grid.at[c, z + 1], fold)

    def store(step, c, z, v):
        state[c, z + 1] = v

    take_steps(0, 1, layers, carried, load, store, lambda z: coeffs[z])


def later_steps(*refs):
    before, coeffs, *carried = refs[:5]
    out, state, grid, sems = refs[5:]
    layers, cells_x = out.shape[1:3]

    def copy_out(z):
        done = grid.at[:, z, pl.ds(0, cells_x), :]
        return pltpu.make_async_copy(done, out.at[:, z], sems.at[z])

    zero_outside(state, layers)

    def load(step, c, z):
        return (before if step == 1 else state)[c, z + 1]

    def store(step, c, z, v):
        if step + 1 < STEPS or c >= 3:
            state[c, z + 1] = v
        if step + 1 == STEPS:
            fold_back(grid.at[c, z], v)

    take_steps(
        1,
        STEPS,
        layers,
        carried,
        lambda step, c, z: load(1 if step == 1 else 2, c, z),
        store,
        lambda z: coeffs[z],
        lambda z: copy_out(z).start(),
    )
    repeat(0, layers, lambda z: copy_out(z).wait())


def multiply(weights, *refs, n_tiles):
    tiles, parts = refs[:n_tiles], refs[n_tiles:]
    total = jnp.dot(
        weights[...],
        jnp.concatenate([tile[...] for tile in tiles], 0),
        precision=lax.Precision.HIGHEST,
        preferred_element_type=jnp.float32,
    )
    rows = parts[0].shape[0]
    for k, part in enumerate(parts):
        part[...] = total[k * rows : (k + 1) * rows]


def add_parts(*refs):
    parts, out = refs[:-1], refs[-1]
    total = parts[0][...]
    for part in parts[1:]:
        total = total + part[...]
    width = out.shape[2]
    for k in range(out.shape[1]):
        out[:, k, :] = total[:, k * width : (k + 1) * width]


def shape_of(*dims):
    return jax.ShapeDtypeStruct(dims, jnp.float32)


def far_field_weights(angle_wave, xs_size, cells_x, near):
    me = lax.axis_index("xs")
    per_block = angle_wave.shape[0] // xs_size
    far = xs_size // near
    bits = far.bit_length() - 1
    view = angle_wave.reshape(far, near, per_block)
    pick = jnp.arange(near, dtype=jnp.int32)[None, :, None] == me % near
    view = jnp.sum(jnp.where(pick, view, 0), axis=1).reshape((2,) * bits + (per_block,))
    for k in range(bits):
        bit = (me // near >> (bits - 1 - k)) & 1
        view = jnp.where(bit == 1, jnp.flip(view, k), view)
    angles = view.reshape(-1)
    owners = me ^ jnp.arange(near, dtype=jnp.int32)
    within = jnp.arange(cells_x, dtype=jnp.int32)
    positions = X0 + (owners[:, None] * cells_x + within[None, :]).reshape(-1)
    phase = angles[:, None] * positions[None, :] % GRID_X
    angle = phase.astype(jnp.float32) * (2.0 * math.pi / GRID_X)
    scale = 1.0 / math.sqrt(cells_x * xs_size)
    both = jnp.stack([jnp.cos(angle) * scale, -jnp.sin(angle) * scale], axis=1)
    return both.reshape(-1, near * cells_x)


def far_field_exchange(tile, angle_wave, xs_size, beside, finish):
    cells_x, columns = tile.shape
    near = 4
    weights = far_field_weights(angle_wave, xs_size, cells_x, near)

    def across(block, mask):
        return lax.ppermute(block, "xs", [(i, i ^ mask) for i in range(xs_size)])

    third = across(tile, 2)
    second = across(tile, 1)
    third, beside = lax.optimization_barrier((third, beside))
    fourth = across(third, 1)
    far = xs_size // near
    rows = weights.shape[0] // far
    parts = pl.pallas_call(
        functools.partial(multiply, n_tiles=near),
        out_shape=(shape_of(rows, columns),) * far,
        in_specs=[VMEM] * (near + 1),
        out_specs=(VMEM,) * far,
        compiler_params=PARAMS,
        name="partial_spectrum",
    )(weights, tile, second, third, fourth)
    arrived = [across(parts[k], k * near) for k in range(far - 1, 0, -1)]
    finished = finish(beside)
    far_field = pl.pallas_call(
        add_parts,
        out_shape=shape_of(rows, 4, columns // 4),
        in_specs=[VMEM] * far,
        out_specs=VMEM,
        compiler_params=PARAMS,
        name="add_arrived",
    )(parts[0], *arrived)
    return far_field, finished


def gathered_sources(adj_values, adj_owner, adj_row, cells_x, cells_y):
    groups = lax.axis_size("ys")
    owners = adj_owner[:, 0]
    hits = (owners[:, None] == jnp.arange(groups, dtype=jnp.int32)[None, :]).astype(jnp.int32)
    before = jnp.cumsum(hits, axis=0) - hits
    slot_index = owners * CAP + jnp.sum(before * hits, axis=1)
    placing = (jnp.arange(groups * CAP, dtype=jnp.int32)[:, None] == slot_index[None, :]).astype(
        jnp.float32
    )
    rows = jnp.broadcast_to(adj_row.astype(jnp.float32)[:, None], (adj_row.shape[0], 1))
    outgoing = jnp.dot(
        placing, jnp.concatenate([adj_values, rows], 1), precision=lax.Precision.HIGHEST
    ).reshape(groups, CAP, cells_y + 1)
    incoming = lax.all_to_all(outgoing, "ys", split_axis=0, concat_axis=0, tiled=True)
    incoming = incoming.reshape(groups * CAP, cells_y + 1)
    landing = (
        jnp.arange(cells_x, dtype=jnp.float32)[:, None] == incoming[:, cells_y][None, :]
    ).astype(jnp.float32)
    current = jnp.dot(landing, incoming[:, :cells_y], precision=lax.Precision.HIGHEST)

    def shifted(block, axis, distance):
        size = lax.axis_size(axis)
        route = [(i, i + distance) for i in range(size) if 0 <= i + distance < size]
        return lax.ppermute(block, axis, route)

    after = shifted(current[:REACH], "xs", -1)
    before = shifted(current[-REACH:], "xs", 1)
    ringed = jnp.concatenate([current, after, before], 0)
    right = shifted(ringed[:, :3], "ys", -1)
    left = shifted(ringed[:, -3:], "ys", 1)
    start, end = SLOT * ZS, cells_y - SLOT * (ZS + 1)
    first = jnp.pad(jnp.concatenate([left, ringed[:, :5]], 1), ((0, 0), (start, end)))
    second = jnp.pad(jnp.concatenate([ringed[:, -5:], right], 1), ((0, 0), (start, end)))
    folded = jnp.stack([ringed, first, second]).reshape(3, TILE, -1, cells_y)
    return folded.transpose(0, 2, 1, 3)


def on_device(fields, permittivity, adj_values, adj_owner, adj_row, angle_wave):
    layers, cells_x, cells_y = fields.shape[1:]
    xs_size, ys_size = lax.axis_size("xs"), lax.axis_size("ys")
    raw = ys_size == 2
    n_adj = adj_values.shape[0] if raw else 0
    n_rows = -(-3 * n_adj // TILE) * TILE
    ring = cells_x + TILE
    x_rows = x_message_rows(layers) + n_rows
    y_rows = len(Y_GROUPS) * ring + 3 * n_rows

    extra = (adj_values, adj_row, adj_owner.reshape(-1)) if raw else ()
    packed = pl.pallas_call(
        functools.partial(pack_x, n_adj=n_adj),
        out_shape=(shape_of(x_rows, cells_y),) * 2 + ((shape_of(n_rows, cells_y),) if raw else ()),
        in_specs=[ANY] * (2 + len(extra)),
        out_specs=(VMEM,) * (3 if raw else 2),
        scratch_shapes=[
            pltpu.VMEM((2, 6, layers, TILE, cells_y), jnp.float32),
            pltpu.VMEM((2, layers, TILE, cells_y), jnp.float32),
        ]
        + ([pltpu.SMEM((n_adj,), jnp.int32)] * 2 if raw else [])
        + [pltpu.SemaphoreType.DMA((4 + len(extra),))],
        compiler_params=PARAMS,
        name="pack_x_edges",
    )(*[pltpu.with_memory_space_constraint(x, pltpu.HBM) for x in (fields, permittivity, *extra)])
    blocks = packed[2:]
    x_even, x_odd = swaps(xs_size)
    from_odd = lax.ppermute(packed[1], "xs", x_odd)
    from_even = lax.ppermute(packed[0], "xs", x_even)

    y_swaps = swaps(ys_size)
    strips_shape = shape_of(2, PARTS, ring, cells_y)
    made = (strips_shape,) + (shape_of(y_rows, cells_y),) * len(y_swaps)
    packed = pl.pallas_call(
        pack_y,
        out_shape=made,
        in_specs=[VMEM] * 2,
        out_specs=(VMEM,) * len(made),
        compiler_params=PARAMS,
        name="pack_y_edges",
    )(fields, permittivity)
    strips, *to_y = pl.pallas_call(
        functools.partial(pack_corners, layers=layers, n_rows=n_rows, n_swaps=len(y_swaps)),
        out_shape=made,
        in_specs=[VMEM] * (len(made) + 2 + len(blocks)),
        out_specs=(VMEM,) * len(made),
        input_output_aliases={k: k for k in range(len(made))},
        compiler_params=PARAMS,
        name="pack_corners",
    )(*packed, from_even, from_odd, *blocks)
    y_halos = [lax.ppermute(message, "ys", route) for message, route in zip(to_y, y_swaps)]

    if raw:
        sources = blocks
    else:
        sources = (gathered_sources(adj_values, adj_owner, adj_row, cells_x, cells_y),)

    fold = ring // TILE
    folded = (fold, TILE, cells_y)
    operands = (fields, permittivity, from_even, from_odd, strips, *y_halos, *sources)
    tile, *carried = pl.pallas_call(
        functools.partial(surface_steps, n_adj=n_adj, n_rows=n_rows, n_swaps=len(y_swaps)),
        out_shape=(
            shape_of(cells_x, 4 * cells_y),
            shape_of(3, *folded),
            shape_of(STEPS, *folded),
            shape_of(STEPS, *folded),
        ),
        in_specs=[VMEM] * len(operands),
        out_specs=(VMEM,) * 4,
        scratch_shapes=[
            pltpu.VMEM((6, layers, ring, cells_y), jnp.float32),
            pltpu.VMEM((layers, ring, cells_y), jnp.float32),
            pltpu.VMEM((6, layers, *folded), jnp.float32),
            pltpu.VMEM((2, PARTS, ring, cells_y), jnp.float32),
        ],
        compiler_params=PARAMS,
        name="surface_steps",
    )(*operands)

    state_shape = (6, layers + 2, *folded)
    operands = (fields, permittivity, from_even, from_odd, *carried)
    stepped = pl.pallas_call(
        first_step,
        out_shape=(shape_of(*state_shape), shape_of(layers, *folded)),
        in_specs=[VMEM] * len(operands),
        out_specs=(VMEM, VMEM),
        scratch_shapes=[
            pltpu.VMEM((6, layers + 2, ring, cells_y), jnp.float32),
            pltpu.VMEM((layers, ring, cells_y), jnp.float32),
        ],
        compiler_params=PARAMS,
        name="first_step",
    )(*operands)

    def finish(stepped):
        return pl.pallas_call(
            later_steps,
            out_shape=shape_of(*fields.shape),
            in_specs=[VMEM] * 5,
            out_specs=ANY,
            scratch_shapes=[
                pltpu.VMEM(state_shape, jnp.float32),
                pltpu.VMEM((6, layers, ring, cells_y), jnp.float32),
                pltpu.SemaphoreType.DMA((layers,)),
            ],
            compiler_params=PARAMS,
            name="later_steps",
        )(*stepped, *carried)

    far, new_fields = far_field_exchange(tile, angle_wave, xs_size, stepped, finish)
    per_block = angle_wave.shape[0] // xs_size
    return (new_fields, far.reshape(per_block, 2, 4, cells_y))


def solution(mesh):
    placed = (
        P(None, None, "xs", "ys"),
        P(None, "xs", "ys"),
        P(("xs", "ys"), None),
        P(("xs", "ys"), None),
        P(("xs", "ys")),
        P(),
    )
    return jax.shard_map(
        on_device,
        mesh=mesh,
        in_specs=placed,
        out_specs=(P(None, None, "xs", "ys"), P("xs", None, None, "ys")),
        check_vma=False,
    )
```

```python
import functools
import math

import jax
import jax.numpy as jnp
from jax import lax
from jax.experimental import pallas as pl
from jax.experimental.pallas import tpu as pltpu
from jax.sharding import PartitionSpec as P

STEPS = 3
CAP = 4
GRID_X = 5000
X0 = 2000
ZS = 8

time_step = 0.5

TILE = 8
REACH = 4
SLOT = 8
PARTS = 7
X_GROUPS = ((0, 1, 3), (2, 4, 6), (5,))
Y_GROUPS = ((0, 2, 4), (1, 3, 6), (5,))
TOGETHER = 8
EARLY = 2

VMEM = pl.BlockSpec(memory_space=pltpu.VMEM)
ANY = pl.BlockSpec(memory_space=pl.ANY)
PARAMS = pltpu.CompilerParams(vmem_limit_bytes=24 * 1024 * 1024)


def lanes_of(shape):
    return lax.broadcasted_iota(jnp.int32, shape, len(shape) - 1)


def rows_of(shape):
    return lax.broadcasted_iota(jnp.int32, shape, len(shape) - 2)


def swaps(size):
    found = []
    for first in (0, 1):
        pairs = [(i, i + 1) for i in range(first, size - 1, 2)]
        if pairs:
            found.append(pairs + [(j, i) for i, j in pairs])
    return found


def x_message_rows(layers):
    return (2 * layers + layers // 2) * TILE


def halo_tile(even, odd, px, c, z, layers):
    group = [c in parts for parts in X_GROUPS].index(True)
    slot = X_GROUPS[group].index(c)
    tile = 2 * z + group if group < 2 else 2 * layers + z // 2
    at = pl.ds(tile * TILE if isinstance(z, int) else pl.multiple_of(tile * TILE, TILE), TILE)
    from_even, from_odd = even[at, :], odd[at, :]
    after = jnp.where(px == 0, from_even, from_odd)
    before = jnp.where(px == 0, from_odd, from_even)
    lower = rows_of(after.shape) < REACH

    def placed(first, count):
        back = (TILE - first) % TILE
        to_end = (TILE - count - first) % TILE
        return jnp.where(
            lower,
            pltpu.roll(after, back, 0) if back else after,
            pltpu.roll(before, to_end, 0) if to_end else before,
        )

    if group < 2:
        return placed(3 * slot, 3 if slot < 2 else 2)
    if isinstance(z, int):
        return placed(4 * (z % 2), 3)
    return jnp.where(z % 2 == 0, placed(0, 3), placed(4, 3))


def repeat(first, last, body, together=1):
    count = last - first
    if together >= count:
        for i in range(first, last):
            body(i)
        return
    rounds = count // together

    def several(n, _):
        for k in range(together):
            body(first + n * together + k)

    lax.fori_loop(0, rounds, several, None)
    for i in range(first + rounds * together, last):
        body(i)


def pack_edge(tile_of, message, layers, last):
    def turn(v, shift):
        return pltpu.roll(v, shift, 0) if shift else v

    def send(tile, v):
        message[tile * TILE : (tile + 1) * TILE, :] = v

    row = rows_of((TILE, message.shape[1]))
    shifts = (3, 6, 0) if last else (0, 3, 6)
    for z in range(layers):
        for g in range(2):
            a, b, c = [turn(tile_of(c, z), shift) for c, shift in zip(X_GROUPS[g], shifts)]
            send(2 * z + g, jnp.where(row < 3, a, jnp.where(row < 6, b, c)))
    shifts = (3, 7) if last else (0, 4)
    for pair in range(layers // 2):
        a, b = [turn(tile_of(X_GROUPS[2][0], 2 * pair + k), shifts[k]) for k in (0, 1)]
        send(2 * layers + pair, jnp.where(row < REACH, a, b))


def pack_x(*refs, n_adj):
    fields, permittivity = refs[:2]
    if n_adj:
        values, rows, owners, to_even, to_odd, blocks = refs[2:8]
        edges, edge_perm, rows_s, owners_s, sems = refs[8:]
    else:
        to_even, to_odd, edges, edge_perm, sems = refs[2:]
    px = lax.axis_index("xs") % 2
    layers, cells_x = fields.shape[1:3]
    copies = []
    for k, start in enumerate((0, cells_x - TILE)):
        rows_at = pl.ds(start, TILE)
        copies.append((fields.at[:, :, rows_at, :], edges.at[k]))
        copies.append((permittivity.at[:, rows_at, :], edge_perm.at[k]))
    if n_adj:
        blocks[...] = jnp.zeros(blocks.shape, jnp.float32)
        copies.append((values, blocks.at[pl.ds(0, n_adj), :]))
        copies.append((rows, rows_s))
        copies.append((owners, owners_s))
    copies = [pltpu.make_async_copy(s, d, sems.at[k]) for k, (s, d) in enumerate(copies)]
    for copy in copies:
        copy.start()
    for copy in copies:
        copy.wait()

    def edge_of(k):
        return lambda c, z: edges[k, c, z] if c < 6 else time_step / edge_perm[k, z]

    def pack(first, last):
        pack_edge(edge_of(0), first, layers, False)
        pack_edge(edge_of(1), last, layers, True)

    pl.when(px == 0)(lambda: pack(to_odd, to_even))
    pl.when(px == 1)(lambda: pack(to_even, to_odd))
    if n_adj:
        for b in range(n_adj):
            code = rows_s[b] + cells_x * owners_s[b]
            blocks[n_adj + b : n_adj + b + 1, :] = jnp.full(
                (1, blocks.shape[1]), code, jnp.int32
            ).astype(jnp.float32)
        to_even[x_message_rows(layers) :, :] = blocks[...]
        to_odd[x_message_rows(layers) :, :] = blocks[...]


def pack_strip(tile_of, layers, shift):
    total = None
    for z in range(layers):
        block = tile_of(z)
        moved = pltpu.roll(block, (SLOT * z + shift) % block.shape[1], 1)
        total = moved if z == 0 else jnp.where(lanes_of(block.shape) // SLOT == z, moved, total)
    return total


def pack_strips(tile_of, layers):
    tiles = [tile_of(z) for z in range(layers)]
    return [pack_strip(lambda z: tiles[z], layers, shift) for shift in (3, 5)]


def pack_group(edges, to_next):
    width = edges[0].shape[1]
    place = lanes_of(edges[0].shape) % SLOT
    total = pltpu.roll(edges[0], width - 2 if to_next else width - 3, 1)
    if len(edges) > 1:
        middle = pltpu.roll(edges[1], 1, 1) if to_next else edges[1]
        total = jnp.where(place < 3, total, jnp.where(place < 6, middle, pltpu.roll(edges[2], 3, 1)))
    return total


def place_group(before, after, slot):
    width = before.shape[1]
    lower, upper = ((0, 5), (width - 3, 2), (width - 5, width - 1))[slot]
    return (pltpu.roll(before, lower, 1) if lower else before), pltpu.roll(after, upper, 1)


def pack_y(fields, permittivity, strips, *to_y):
    layers, cells_x, width = fields.shape[1:]
    ring = cells_x + TILE
    for r in range(cells_x // TILE):
        rows = slice(r * TILE, (r + 1) * TILE)
        for g, parts in enumerate(Y_GROUPS):
            packed = []
            for c in parts:

                def tile_of(z):
                    return fields[c, z, rows, :] if c < 6 else time_step / permittivity[z, rows, :]

                packed.append(pack_strips(tile_of, layers))
                for side in (0, 1):
                    strips[side, c, rows, :] = packed[-1][side]
            for swap, message in enumerate(to_y):
                to_next = lax.axis_index("ys") % 2 == swap
                at = slice(g * ring + r * TILE, g * ring + (r + 1) * TILE)
                message[at, :] = jnp.where(
                    to_next,
                    pack_group([p[1] for p in packed], True),
                    pack_group([p[0] for p in packed], False),
                )


def pack_corners(*refs, layers, n_rows, n_swaps):
    even, odd = refs[n_swaps : 2 + n_swaps]
    to_y = refs[-n_swaps:]
    px = lax.axis_index("xs") % 2
    ring = (to_y[0].shape[0] - 3 * n_rows) // len(Y_GROUPS)

    def fill(message, to_next):
        for g, parts in enumerate(Y_GROUPS):
            packed = [
                pack_strip(
                    lambda z: halo_tile(even, odd, px, c, z, layers), layers, 5 if to_next else 3
                )
                for c in parts
            ]
            message[(g + 1) * ring - TILE : (g + 1) * ring, :] = pack_group(packed, to_next)

    for swap, message in enumerate(to_y):
        is_next = lax.axis_index("ys") % 2 == swap
        for to_next in (False, True):
            pl.when(is_next == to_next)(functools.partial(fill, message, to_next))
    if n_rows:
        blocks = refs[2 + n_swaps]
        end = len(Y_GROUPS) * ring
        x_end = x_message_rows(layers)
        to_y[0][end : end + n_rows, :] = blocks[...]
        to_y[0][end + n_rows : end + 2 * n_rows, :] = even[x_end:, :]
        to_y[0][end + 2 * n_rows : end + 3 * n_rows, :] = odd[x_end:, :]


def row_index(shape):
    fold = lax.broadcasted_iota(jnp.int32, shape, 0)
    return lax.broadcasted_iota(jnp.int32, shape, 1) * shape[0] + fold


def gather_sources(sets, px, me, totals, n_adj, cells_x):
    mine, other = totals[0], totals[1]
    row_at = row_index(mine.shape).astype(jnp.float32)
    own_index = jnp.where(me == 0, 0.0, 1.0)
    for ref, start, is_next in sets:
        for b in range(n_adj):
            value = ref[start + b : start + b + 1, :]
            code = ref[start + n_adj + b : start + n_adj + b + 1, :]
            owner = jnp.where(code >= cells_x, 1.0, 0.0)
            row = code - cells_x * owner
            if is_next is not None:
                after = jnp.where(row < REACH, row + cells_x, -1.0)
                before = jnp.where(row >= cells_x - REACH, row + TILE, -1.0)
                row = jnp.where(is_next, after, before)
            is_mine = owner == own_index
            mine = mine + jnp.where(row_at == jnp.where(is_mine, row, -1.0), value, 0.0)
            other = other + jnp.where(row_at == jnp.where(is_mine, -1.0, row), value, 0.0)
    totals[0], totals[1] = mine, other


def place_sources(totals, me, source):
    mine, other = totals[0], totals[1]
    lane = lanes_of(mine.shape)
    slot = (lane >= SLOT * ZS) & (lane < SLOT * (ZS + 1))
    place = lane - SLOT * ZS
    shift = SLOT * ZS + 3
    before = jnp.where(me == 0, 0.0, pltpu.roll(other, shift, 2))
    source[0] = mine
    source[1] = jnp.where(slot, jnp.where(place < 3, before, pltpu.roll(mine, shift, 2)), 0.0)
    shift = SLOT * ZS + 5
    after = jnp.where(me == 0, pltpu.roll(other, shift, 2), 0.0)
    source[2] = jnp.where(slot, jnp.where(place < 5, pltpu.roll(mine, shift, 2), after), 0.0)


def next_x(v):
    return jnp.concatenate([v[1:], pltpu.roll(v[0:1], v.shape[1] - 1, 1)], 0)


def prev_x(v):
    return jnp.concatenate([pltpu.roll(v[-1:], 1, 1), v[:-1]], 0)


def lane_roll(v, shift):
    return pltpu.roll(v, shift % v.shape[2], 2)


def zeros(shape):
    return jnp.zeros(shape, jnp.float32)


def unfold(ref, fold):
    return jnp.stack([ref[pl.ds(j, TILE, stride=fold), :] for j in range(fold)])


def fold_back(ref, v):
    for j in range(v.shape[0]):
        ref[pl.ds(j, TILE, stride=v.shape[0]), :] = v[j]


def step_size(full):
    outside = (row_index(full) >= full[0] * TILE - REACH) & (lax.axis_index("xs") == 0)
    return jnp.where(outside, 0.0, time_step)


def evolve_strips(strips, halo_strips, y_halos, source, strip, edge_e, edge_h):
    me = lax.axis_index("ys")
    ring, width = strips.shape[2] + TILE, strips.shape[3]
    fold = ring // TILE
    full = (fold, TILE, width)
    for g, parts in enumerate(Y_GROUPS):
        for r in range(fold):
            before, after = zeros((TILE, width)), zeros((TILE, width))
            at = g * ring + r * TILE
            for k, y_ref in enumerate(y_halos):
                block = y_ref[at : at + TILE, :]
                is_next = me % 2 == k
                after = jnp.where(is_next, block, after)
                before = jnp.where(is_next, before, block)
            place = lanes_of(before.shape) % SLOT
            rows = slice(r * TILE, (r + 1) * TILE)
            for slot, c in enumerate(parts):
                lower, upper = place_group(before, after, slot)
                own = [strips[k, c, rows, :] if r + 1 < fold else halo_strips[k, c] for k in (0, 1)]
                strip[0, c, rows, :] = jnp.where(place < 3, lower, own[0])
                strip[1, c, rows, :] = jnp.where(place >= 5, upper, own[1])
    lane = lanes_of(full)
    place = lane % SLOT
    for side in (0, 1):
        ex, ey, ez, hx, hy, hz, co = [unfold(strip.at[side, c], fold) for c in range(PARTS)]
        dt = step_size(full)
        if not side:
            dt = jnp.where((place < 3) & (me == 0), 0.0, dt)
        for step in range(STEPS):

            def next_z(v):
                return jnp.where(lane < width - SLOT, lane_roll(v, -SLOT), 0.0)

            def prev_z(v):
                return jnp.where(lane >= SLOT, lane_roll(v, SLOT), 0.0)

            if side:
                edge_e[step] = jnp.where(place == 5, ex, lane_roll(ez, 1))
                if step + 1 == STEPS:
                    continue
            hx = hx - dt * (lane_roll(ez, -1) - ez - (next_z(ey) - ey))
            hy = hy - dt * (next_z(ex) - ex - (next_x(ez) - ez))
            hz = hz - dt * (next_x(ey) - ey - (lane_roll(ex, -1) - ex))
            if not side:
                edge_h[step] = jnp.where(place == 2, hz, lane_roll(hx, 1))
                if step + 1 == STEPS:
                    continue
            ex = ex + co * (hz - lane_roll(hz, 1) - (hy - prev_z(hy)))
            ey = ey + co * (hx - prev_z(hx) - (hz - prev_x(hz)))
            ez = ez + co * (hy - prev_x(hy) - (hx - lane_roll(hx, 1)) - source[1 + side])


def surface_layers(layers):
    return range(max(ZS - STEPS, 0), min(ZS + STEPS + 1, layers))


def prepare_surface(*refs, n_adj, n_rows):
    fields, permittivity, even, odd = refs[:4]
    state, coeffs, halo_strips = refs[4 + bool(n_adj) : 7 + bool(n_adj)]
    rows = refs[-1]
    px = lax.axis_index("xs") % 2
    layers, cells_x, width = fields.shape[1:]
    ring = cells_x + TILE
    fold = ring // TILE
    for c in range(PARTS):
        halos = [halo_tile(even, odd, px, c, z, layers) for z in range(layers)]
        for side, tile in enumerate(pack_strips(lambda z: halos[z], layers)):
            halo_strips[side, c] = tile
        for z in surface_layers(layers):
            rows[c, z, 0:cells_x, :] = fields[c, z] if c < 6 else time_step / permittivity[z]
            rows[c, z, cells_x:ring, :] = halos[z]
            folded = unfold(rows.at[c, z], fold)
            if c < 6:
                state[c, z] = folded
            else:
                coeffs[z] = folded
    if n_adj:
        blocks, totals = refs[4], refs[8]
        totals[...] = zeros(totals.shape)
        end = x_message_rows(layers)
        sets = [(blocks, 0, None), (even, end, px == 0), (odd, end, px == 1)]
        gather_sources(sets, px, lax.axis_index("ys"), totals, n_adj, cells_x)


def surface_steps(*refs, n_adj, n_rows, n_swaps):
    before, coeffs, halo_strips, strips = refs[:4]
    y_halos, given = refs[4 : 4 + n_swaps], refs[4 + n_swaps]
    out, source, edge_e, edge_h, rows, state, strip, totals = refs[5 + n_swaps :]
    px = lax.axis_index("xs") % 2
    me = lax.axis_index("ys")
    layers = before.shape[1]
    full = before.shape[2:]
    fold, width = full[0], full[2]
    cells_x = (fold - 1) * TILE
    lane = lanes_of(full)

    if n_adj:
        end = len(Y_GROUPS) * fold * TILE
        sets = [
            (y_halos[0], end, None),
            (y_halos[0], end + n_rows, px == 0),
            (y_halos[0], end + 2 * n_rows, px == 1),
        ]
        totals[...] = given[...]
        gather_sources(sets, px, me, totals, n_adj, cells_x)
        place_sources(totals, me, source)
    else:
        source[...] = given[...]
    evolve_strips(strips, halo_strips, y_halos, source, strip, edge_e, edge_h)

    dt = step_size(full)
    for step in range(STEPS):
        final = step + 1 == STEPS
        low, high = max(ZS - STEPS + step, 0), min(ZS + STEPS - 1 - step, layers - 1)

        def load(c, z):
            return state[c, z] if step else before[c, z]

        def store(c, z, v):
            if not final:
                state[c, z] = v
            elif z == ZS and c in (0, 1, 3, 4):
                fold_back(rows.at[c], v)

        below = None
        ex, ey = load(0, low), load(1, low)
        for z in range(low, high + 1):
            ez, hx, hy, hz = [load(c, z) for c in range(2, 6)]
            if z + 1 < layers:
                ex_above, ey_above = load(0, z + 1), load(1, z + 1)
            else:
                ex_above, ey_above = jnp.zeros(full, jnp.float32), jnp.zeros(full, jnp.float32)
            edge = lane_roll(edge_e[step], width - 1 - (SLOT * z + 5))
            ex_y = jnp.where(lane == width - 1, edge, lane_roll(ex, -1))
            ez_y = lane_roll(jnp.where(lane == 0, edge, ez), -1)
            hx = hx - dt * (ez_y - ez - (ey_above - ey))
            hy = hy - dt * (ex_above - ex - (next_x(ez) - ez))
            hz = hz - dt * (next_x(ey) - ey - (ex_y - ex))
            for c, v in ((3, hx), (4, hy), (5, hz)):
                store(c, z, v)
            if z == 0 or below:
                co = coeffs[z]
                hx_z = hx - below[0] if z else hx
                hy_z = hy - below[1] if z else hy
                edge = lane_roll(edge_h[step], width - 1 - (SLOT * z + 2))
                hx_y = jnp.where(lane == 0, edge, lane_roll(hx, 1))
                hz_y = lane_roll(jnp.where(lane == width - 1, edge, hz), 1)
                store(0, z, ex + co * (hz - hz_y - hy_z))
                store(1, z, ey + co * (hx_z - (hz - prev_x(hz))))
                change = hy - prev_x(hy) - (hx - hx_y)
                if z == ZS:
                    change = change - source[0]
                store(2, z, ez + co * change)
            below = (hx, hy)
            ex, ey = ex_above, ey_above
    for k, (c, sign) in enumerate(((4, -1.0), (3, 1.0), (1, 1.0), (0, -1.0))):
        out[:, k * width : (k + 1) * width] = sign * rows[c, 0:cells_x, :]


def take_steps(first, last, layers, refs, load, store, load_coeff, after_layer=None):
    source, edge_e, edge_h = refs
    full = source.shape[1:]
    width = full[2]
    lane = lanes_of(full)
    dt = step_size(full)
    for step in range(first, last):

        def advance_h(z):
            ex, ey, ez, hx, hy, hz = [load(step, c, z) for c in range(6)]
            edge = lane_roll(edge_e[step], 2 * width - 1 - (SLOT * z + 5))
            ex_y = jnp.where(lane == width - 1, edge, lane_roll(ex, -1))
            ez_y = lane_roll(jnp.where(lane == 0, edge, ez), -1)
            store(step, 3, z, hx - dt * (ez_y - ez - (load(step, 1, z + 1) - ey)))
            store(step, 4, z, hy - dt * (load(step, 0, z + 1) - ex - (next_x(ez) - ez)))
            store(step, 5, z, hz - dt * (next_x(ey) - ey - (ex_y - ex)))

        def advance_e(z):
            hx, hy, hz = [load(step + 1, c, z) for c in range(3, 6)]
            co = load_coeff(z)
            edge = lane_roll(edge_h[step], 2 * width - 1 - (SLOT * z + 2))
            hx_y = jnp.where(lane == 0, edge, lane_roll(hx, 1))
            hz_y = lane_roll(jnp.where(lane == width - 1, edge, hz), 1)
            change = hz - hz_y - (hy - load(step + 1, 4, z - 1))
            store(step, 0, z, load(step, 0, z) + co * change)
            change = hx - load(step + 1, 3, z - 1) - (hz - prev_x(hz))
            store(step, 1, z, load(step, 1, z) + co * change)
            change = hy - prev_x(hy) - (hx - hx_y) - jnp.where(z == ZS, source[0], 0.0)
            store(step, 2, z, load(step, 2, z) + co * change)
            if after_layer and step + 1 == last:
                after_layer(z)

        repeat(0, layers, advance_h, TOGETHER)
        repeat(0, layers, advance_e, TOGETHER)


def zero_outside(ref, layers):
    for c in (0, 1):
        ref[c, layers + 1] = zeros(ref.shape[2:])
        ref[c + 3, 0] = zeros(ref.shape[2:])


def early_steps(*refs):
    fields, permittivity, even, odd, *carried = refs[:7]
    state, coeffs, grid, coeff_rows = refs[7:]
    px = lax.axis_index("xs") % 2
    layers, cells_x, width = fields.shape[1:]
    ring = cells_x + TILE
    fold = ring // TILE

    def build(z):
        for c in range(PARTS):
            ref = grid.at[c, z + 1] if c < 6 else coeff_rows.at[z]
            ref[0:cells_x, :] = fields[c, z] if c < 6 else time_step / permittivity[z]
            ref[cells_x:ring, :] = halo_tile(even, odd, px, c, z, layers)
        coeffs[z] = unfold(coeff_rows.at[z], fold)

    repeat(0, layers, build, TOGETHER // 2)
    for c in (0, 1):
        grid[c, layers + 1] = zeros((ring, width))
    zero_outside(state, layers)

    def load(step, c, z):
        return state[c, z + 1] if step else unfold(grid.at[c, z + 1], fold)

    def store(step, c, z, v):
        state[c, z + 1] = v

    take_steps(0, EARLY, layers, carried, load, store, lambda z: coeffs[z])


def later_steps(*refs):
    before, coeffs, *carried = refs[:5]
    out, state, grid, sems = refs[5:]
    layers, cells_x = out.shape[1:3]

    def copy_out(z):
        done = grid.at[:, z, pl.ds(0, cells_x), :]
        return pltpu.make_async_copy(done, out.at[:, z], sems.at[z])

    zero_outside(state, layers)

    def load(step, c, z):
        return (before if step == EARLY else state)[c, z + 1]

    def store(step, c, z, v):
        if step + 1 < STEPS or c >= 3:
            state[c, z + 1] = v
        if step + 1 == STEPS:
            fold_back(grid.at[c, z], v)

    take_steps(
        EARLY,
        STEPS,
        layers,
        carried,
        load,
        store,
        lambda z: coeffs[z],
        lambda z: copy_out(z).start(),
    )
    repeat(0, layers, lambda z: copy_out(z).wait())


def multiply(weights, *refs, n_tiles):
    tiles, parts = refs[:n_tiles], refs[n_tiles:]
    total = jnp.dot(
        weights[...],
        jnp.concatenate([tile[...] for tile in tiles], 0),
        precision=lax.Precision.HIGHEST,
        preferred_element_type=jnp.float32,
    )
    rows = parts[0].shape[0]
    for k, part in enumerate(parts):
        part[...] = total[k * rows : (k + 1) * rows]


def add_parts(*refs):
    parts, out = refs[:-1], refs[-1]
    total = parts[0][...]
    for part in parts[1:]:
        total = total + part[...]
    width = out.shape[2]
    for k in range(out.shape[1]):
        out[:, k, :] = total[:, k * width : (k + 1) * width]


def shape_of(*dims):
    return jax.ShapeDtypeStruct(dims, jnp.float32)


def far_field_weights(angle_wave, xs_size, cells_x, near):
    me = lax.axis_index("xs")
    per_block = angle_wave.shape[0] // xs_size
    far = xs_size // near
    bits = far.bit_length() - 1
    view = angle_wave.reshape(far, near, per_block)
    pick = jnp.arange(near, dtype=jnp.int32)[None, :, None] == me % near
    view = jnp.sum(jnp.where(pick, view, 0), axis=1).reshape((2,) * bits + (per_block,))
    for k in range(bits):
        bit = (me // near >> (bits - 1 - k)) & 1
        view = jnp.where(bit == 1, jnp.flip(view, k), view)
    angles = view.reshape(-1)
    owners = me ^ jnp.arange(near, dtype=jnp.int32)
    within = jnp.arange(cells_x, dtype=jnp.int32)
    positions = X0 + (owners[:, None] * cells_x + within[None, :]).reshape(-1)
    phase = angles[:, None] * positions[None, :] % GRID_X
    angle = phase.astype(jnp.float32) * (2.0 * math.pi / GRID_X)
    scale = 1.0 / math.sqrt(cells_x * xs_size)
    both = jnp.stack([jnp.cos(angle) * scale, -jnp.sin(angle) * scale], axis=1)
    return both.reshape(-1, near * cells_x)


def far_field_exchange(tile, angle_wave, xs_size, beside, finish):
    cells_x, columns = tile.shape
    near = 4
    weights = far_field_weights(angle_wave, xs_size, cells_x, near)

    def across(block, mask):
        return lax.ppermute(block, "xs", [(i, i ^ mask) for i in range(xs_size)])

    third = across(tile, 2)
    second = across(tile, 1)
    third, beside = lax.optimization_barrier((third, beside))
    fourth = across(third, 1)
    far = xs_size // near
    rows = weights.shape[0] // far
    parts = pl.pallas_call(
        functools.partial(multiply, n_tiles=near),
        out_shape=(shape_of(rows, columns),) * far,
        in_specs=[VMEM] * (near + 1),
        out_specs=(VMEM,) * far,
        compiler_params=PARAMS,
        name="partial_spectrum",
    )(weights, tile, second, third, fourth)
    arrived = [across(parts[k], k * near) for k in range(far - 1, 0, -1)]
    finished = finish(beside)
    far_field = pl.pallas_call(
        add_parts,
        out_shape=shape_of(rows, 4, columns // 4),
        in_specs=[VMEM] * far,
        out_specs=VMEM,
        compiler_params=PARAMS,
        name="add_arrived",
    )(parts[0], *arrived)
    return far_field, finished


def gathered_sources(adj_values, adj_owner, adj_row, cells_x, cells_y):
    groups = lax.axis_size("ys")
    owners = adj_owner[:, 0]
    hits = (owners[:, None] == jnp.arange(groups, dtype=jnp.int32)[None, :]).astype(jnp.int32)
    before = jnp.cumsum(hits, axis=0) - hits
    slot_index = owners * CAP + jnp.sum(before * hits, axis=1)
    placing = (jnp.arange(groups * CAP, dtype=jnp.int32)[:, None] == slot_index[None, :]).astype(
        jnp.float32
    )
    rows = jnp.broadcast_to(adj_row.astype(jnp.float32)[:, None], (adj_row.shape[0], 1))
    outgoing = jnp.dot(
        placing, jnp.concatenate([adj_values, rows], 1), precision=lax.Precision.HIGHEST
    ).reshape(groups, CAP, cells_y + 1)
    incoming = lax.all_to_all(outgoing, "ys", split_axis=0, concat_axis=0, tiled=True)
    incoming = incoming.reshape(groups * CAP, cells_y + 1)
    landing = (
        jnp.arange(cells_x, dtype=jnp.float32)[:, None] == incoming[:, cells_y][None, :]
    ).astype(jnp.float32)
    current = jnp.dot(landing, incoming[:, :cells_y], precision=lax.Precision.HIGHEST)

    def shifted(block, axis, distance):
        size = lax.axis_size(axis)
        route = [(i, i + distance) for i in range(size) if 0 <= i + distance < size]
        return lax.ppermute(block, axis, route)

    after = shifted(current[:REACH], "xs", -1)
    before = shifted(current[-REACH:], "xs", 1)
    ringed = jnp.concatenate([current, after, before], 0)
    right = shifted(ringed[:, :3], "ys", -1)
    left = shifted(ringed[:, -3:], "ys", 1)
    start, end = SLOT * ZS, cells_y - SLOT * (ZS + 1)
    first = jnp.pad(jnp.concatenate([left, ringed[:, :5]], 1), ((0, 0), (start, end)))
    second = jnp.pad(jnp.concatenate([ringed[:, -5:], right], 1), ((0, 0), (start, end)))
    folded = jnp.stack([ringed, first, second]).reshape(3, TILE, -1, cells_y)
    return folded.transpose(0, 2, 1, 3)


def on_device(fields, permittivity, adj_values, adj_owner, adj_row, angle_wave):
    layers, cells_x, cells_y = fields.shape[1:]
    xs_size, ys_size = lax.axis_size("xs"), lax.axis_size("ys")
    raw = ys_size == 2
    n_adj = adj_values.shape[0] if raw else 0
    n_rows = -(-2 * n_adj // TILE) * TILE
    ring = cells_x + TILE
    x_rows = x_message_rows(layers) + n_rows
    y_rows = len(Y_GROUPS) * ring + 3 * n_rows

    extra = (adj_values, adj_row, adj_owner.reshape(-1)) if raw else ()
    x_message = shape_of(x_rows, cells_y)
    to_even, to_odd, *blocks = pl.pallas_call(
        functools.partial(pack_x, n_adj=n_adj),
        out_shape=(x_message,) * 2 + ((shape_of(n_rows, cells_y),) if raw else ()),
        in_specs=[ANY] * (2 + len(extra)),
        out_specs=(VMEM,) * (3 if raw else 2),
        scratch_shapes=[
            pltpu.VMEM((2, 6, layers, TILE, cells_y), jnp.float32),
            pltpu.VMEM((2, layers, TILE, cells_y), jnp.float32),
        ]
        + ([pltpu.SMEM((n_adj,), jnp.int32)] * 2 if raw else [])
        + [pltpu.SemaphoreType.DMA((4 + len(extra),))],
        compiler_params=PARAMS,
        name="pack_x_edges",
    )(*[pltpu.with_memory_space_constraint(x, pltpu.HBM) for x in (fields, permittivity, *extra)])
    x_even, x_odd = swaps(xs_size)
    from_even = lax.ppermute(to_even, "xs", x_even)
    from_odd = lax.ppermute(to_odd, "xs", x_odd)

    y_swaps = swaps(ys_size)
    messages = (shape_of(y_rows, cells_y),) * len(y_swaps)
    strips, *to_y = pl.pallas_call(
        pack_y,
        out_shape=(shape_of(2, PARTS, cells_x, cells_y),) + messages,
        in_specs=[VMEM] * 2,
        out_specs=(VMEM,) * (1 + len(messages)),
        compiler_params=PARAMS,
        name="pack_y_edges",
    )(fields, permittivity)
    to_y = pl.pallas_call(
        functools.partial(pack_corners, layers=layers, n_rows=n_rows, n_swaps=len(y_swaps)),
        out_shape=messages,
        in_specs=[VMEM] * (len(messages) + 2 + len(blocks)),
        out_specs=(VMEM,) * len(messages),
        input_output_aliases={k: k for k in range(len(messages))},
        compiler_params=PARAMS,
        name="pack_corners",
    )(*to_y, from_even, from_odd, *blocks)
    y_halos = [lax.ppermute(message, "ys", route) for message, route in zip(to_y, y_swaps)]

    fold = ring // TILE
    folded = (fold, TILE, cells_y)
    made = (
        shape_of(6, layers, *folded),
        shape_of(layers, *folded),
        shape_of(2, PARTS, TILE, cells_y),
    ) + ((shape_of(2, *folded),) if raw else ())
    prepared = pl.pallas_call(
        functools.partial(prepare_surface, n_adj=n_adj, n_rows=n_rows),
        out_shape=made,
        in_specs=[VMEM] * (4 + len(blocks)),
        out_specs=(VMEM,) * len(made),
        scratch_shapes=[pltpu.VMEM((PARTS, layers, ring, cells_y), jnp.float32)],
        compiler_params=PARAMS,
        name="prepare_surface",
    )(fields, permittivity, from_even, from_odd, *blocks)
    if raw:
        sources = prepared[3:]
    else:
        sources = (gathered_sources(adj_values, adj_owner, adj_row, cells_x, cells_y),)
    operands = (*prepared[:3], strips, *y_halos, *sources)
    tile, *carried = pl.pallas_call(
        functools.partial(surface_steps, n_adj=n_adj, n_rows=n_rows, n_swaps=len(y_swaps)),
        out_shape=(
            shape_of(cells_x, 4 * cells_y),
            shape_of(3, *folded),
            shape_of(STEPS, *folded),
            shape_of(STEPS, *folded),
        ),
        in_specs=[VMEM] * len(operands),
        out_specs=(VMEM,) * 4,
        scratch_shapes=[
            pltpu.VMEM((6, ring, cells_y), jnp.float32),
            pltpu.VMEM((6, layers, *folded), jnp.float32),
            pltpu.VMEM((2, PARTS, ring, cells_y), jnp.float32),
            pltpu.VMEM((2, *folded), jnp.float32),
        ],
        compiler_params=PARAMS,
        name="surface_steps",
    )(*operands)

    state_shape = (6, layers + 2, *folded)
    operands = (fields, permittivity, from_even, from_odd, *carried)
    stepped = pl.pallas_call(
        early_steps,
        out_shape=(shape_of(*state_shape), shape_of(layers, *folded)),
        in_specs=[VMEM] * len(operands),
        out_specs=(VMEM, VMEM),
        scratch_shapes=[
            pltpu.VMEM((6, layers + 2, ring, cells_y), jnp.float32),
            pltpu.VMEM((layers, ring, cells_y), jnp.float32),
        ],
        compiler_params=PARAMS,
        name="early_steps",
    )(*operands)

    def finish(stepped):
        return pl.pallas_call(
            later_steps,
            out_shape=shape_of(*fields.shape),
            in_specs=[VMEM] * 5,
            out_specs=ANY,
            scratch_shapes=[
                pltpu.VMEM(state_shape, jnp.float32),
                pltpu.VMEM((6, layers, ring, cells_y), jnp.float32),
                pltpu.SemaphoreType.DMA((layers,)),
            ],
            compiler_params=PARAMS,
            name="later_steps",
        )(*stepped, *carried)

    far, new_fields = far_field_exchange(tile, angle_wave, xs_size, stepped, finish)
    per_block = angle_wave.shape[0] // xs_size
    return (new_fields, far.reshape(per_block, 2, 4, cells_y))


def solution(mesh):
    placed = (
        P(None, None, "xs", "ys"),
        P(None, "xs", "ys"),
        P(("xs", "ys"), None),
        P(("xs", "ys"), None),
        P(("xs", "ys")),
        P(),
    )
    return jax.shard_map(
        on_device,
        mesh=mesh,
        in_specs=placed,
        out_specs=(P(None, None, "xs", "ys"), P("xs", None, None, "ys")),
        check_vma=False,
    )
```

```python
import functools
import math

import jax
import jax.numpy as jnp
from jax import lax
from jax.experimental import pallas as pl
from jax.experimental.pallas import tpu as pltpu
from jax.sharding import PartitionSpec as P

STEPS = 3
CAP = 4
GRID_X = 5000
X0 = 2000
ZS = 8

time_step = 0.5

TILE = 8
REACH = 4
SLOT = 8
PARTS = 7
X_GROUPS = ((0, 1, 3), (2, 4, 6), (5,))
Y_GROUPS = ((0, 2, 4), (1, 3, 6), (5,))
TOGETHER = 8
EARLY = 2
NEAR = 4

VMEM = pl.BlockSpec(memory_space=pltpu.VMEM)
ANY = pl.BlockSpec(memory_space=pl.ANY)
PARAMS = pltpu.CompilerParams(vmem_limit_bytes=24 * 1024 * 1024)


def lanes_of(shape):
    return lax.broadcasted_iota(jnp.int32, shape, len(shape) - 1)


def rows_of(shape):
    return lax.broadcasted_iota(jnp.int32, shape, len(shape) - 2)


def swaps(size):
    found = []
    for first in (0, 1):
        pairs = [(i, i + 1) for i in range(first, size - 1, 2)]
        if first and size > 2 and size % 2 == 0:
            pairs.append((size - 1, 0))
        if pairs:
            found.append(pairs + [(j, i) for i, j in pairs])
    return found


def odd_route(xs_size, ys_size, y_route):
    ends = [0] + ([xs_size - 1] if xs_size % 2 == 0 else [])
    pairs = [(i, i + 1) for i in range(1, xs_size - 1, 2)]
    pairs += [(j, i) for i, j in pairs]
    route = [(a * ys_size + s, b * ys_size + t) for a, b in pairs for s, t in y_route]
    near = swaps(ys_size)[0]
    return route + [(e * ys_size + s, e * ys_size + t) for e in ends for s, t in near]


def at_end(axis):
    index = lax.axis_index(axis)
    return (index == 0) | (index == lax.axis_size(axis) - 1)


def x_message_rows(layers):
    return (2 * layers + layers // 2) * TILE


def halo_tile(even, odd, px, c, z, layers):
    group = [c in parts for parts in X_GROUPS].index(True)
    slot = X_GROUPS[group].index(c)
    tile = 2 * z + group if group < 2 else 2 * layers + z // 2
    at = pl.ds(tile * TILE if isinstance(z, int) else pl.multiple_of(tile * TILE, TILE), TILE)
    from_even, from_odd = even[at, :], jnp.where(at_end("xs"), 0.0, odd[at, :])
    after = jnp.where(px == 0, from_even, from_odd)
    before = jnp.where(px == 0, from_odd, from_even)
    lower = rows_of(after.shape) < REACH

    def placed(first, count):
        back = (TILE - first) % TILE
        to_end = (TILE - count - first) % TILE
        return jnp.where(
            lower,
            pltpu.roll(after, back, 0) if back else after,
            pltpu.roll(before, to_end, 0) if to_end else before,
        )

    if group < 2:
        return placed(3 * slot, 3 if slot < 2 else 2)
    if isinstance(z, int):
        return placed(4 * (z % 2), 3)
    return jnp.where(z % 2 == 0, placed(0, 3), placed(4, 3))


def repeat(first, last, body, together=1):
    count = last - first
    if together >= count:
        for i in range(first, last):
            body(i)
        return
    rounds = count // together

    def several(n, _):
        for k in range(together):
            body(first + n * together + k)

    lax.fori_loop(0, rounds, several, None)
    for i in range(first + rounds * together, last):
        body(i)


def pack_edge(tile_of, message, layers, last):
    def turn(v, shift):
        return pltpu.roll(v, shift, 0) if shift else v

    def send(tile, v):
        message[tile * TILE : (tile + 1) * TILE, :] = v

    row = rows_of((TILE, message.shape[1]))
    shifts = (3, 6, 0) if last else (0, 3, 6)
    for z in range(layers):
        for g in range(2):
            a, b, c = [turn(tile_of(c, z), shift) for c, shift in zip(X_GROUPS[g], shifts)]
            send(2 * z + g, jnp.where(row < 3, a, jnp.where(row < 6, b, c)))
    shifts = (3, 7) if last else (0, 4)
    for pair in range(layers // 2):
        a, b = [turn(tile_of(X_GROUPS[2][0], 2 * pair + k), shifts[k]) for k in (0, 1)]
        send(2 * layers + pair, jnp.where(row < REACH, a, b))


def pack_x(*refs, n_adj, n_swaps):
    fields, permittivity = refs[:2]
    if n_adj:
        values, rows, owners, to_even, to_odd, blocks = refs[2:8]
        to_diag = refs[8 : 8 + n_swaps]
        edges, edge_perm, rows_s, owners_s, sems = refs[8 + n_swaps :]
    else:
        to_even, to_odd = refs[2:4]
        to_diag = refs[4 : 4 + n_swaps]
        edges, edge_perm, sems = refs[4 + n_swaps :]
    px = lax.axis_index("xs") % 2
    layers, cells_x = fields.shape[1:3]
    copies = []
    for k, start in enumerate((0, cells_x - TILE)):
        rows_at = pl.ds(start, TILE)
        copies.append((fields.at[:, :, rows_at, :], edges.at[k]))
        copies.append((permittivity.at[:, rows_at, :], edge_perm.at[k]))
    if n_adj:
        blocks[...] = jnp.zeros(blocks.shape, jnp.float32)
        copies.append((values, blocks.at[pl.ds(0, n_adj), :]))
        copies.append((rows, rows_s))
        copies.append((owners, owners_s))
    copies = [pltpu.make_async_copy(s, d, sems.at[k]) for k, (s, d) in enumerate(copies)]
    for copy in copies:
        copy.start()
    for copy in copies:
        copy.wait()

    def edge_of(k):
        return lambda c, z: edges[k, c, z] if c < 6 else time_step / edge_perm[k, z]

    def pack(first, last):
        pack_edge(edge_of(0), first, layers, False)
        pack_edge(edge_of(1), last, layers, True)

    pl.when(px == 0)(lambda: pack(to_odd, to_even))
    pl.when(px == 1)(lambda: pack(to_even, to_odd))

    def pack_corner(message, k, to_next):
        for g, parts in enumerate(Y_GROUPS):
            packed = [
                pack_strip(lambda z: edge_of(k)(c, z), layers, 5 if to_next else 3) for c in parts
            ]
            message[g * TILE : (g + 1) * TILE, :] = pack_group(packed, to_next)

    for swap, message in enumerate(to_diag):
        is_next = lax.axis_index("ys") % 2 == swap
        for k in (0, 1):
            for to_next in (False, True):
                pl.when((px == k) & (is_next == to_next))(
                    functools.partial(pack_corner, message, k, to_next)
                )
    if n_adj:
        for b in range(n_adj):
            code = rows_s[b] + cells_x * owners_s[b]
            blocks[n_adj + b : n_adj + b + 1, :] = jnp.full(
                (1, blocks.shape[1]), code, jnp.int32
            ).astype(jnp.float32)
        to_even[x_message_rows(layers) :, :] = blocks[...]
        to_odd[x_message_rows(layers) :, :] = blocks[...]
        to_diag[0][len(Y_GROUPS) * TILE :, :] = blocks[...]


def pack_strip(tile_of, layers, shift):
    total = None
    for z in range(layers):
        block = tile_of(z)
        moved = pltpu.roll(block, (SLOT * z + shift) % block.shape[1], 1)
        total = moved if z == 0 else jnp.where(lanes_of(block.shape) // SLOT == z, moved, total)
    return total


def pack_strips(tile_of, layers):
    tiles = [tile_of(z) for z in range(layers)]
    return [pack_strip(lambda z: tiles[z], layers, shift) for shift in (3, 5)]


def pack_group(edges, to_next):
    width = edges[0].shape[1]
    place = lanes_of(edges[0].shape) % SLOT
    total = pltpu.roll(edges[0], width - 2 if to_next else width - 3, 1)
    if len(edges) > 1:
        middle = pltpu.roll(edges[1], 1, 1) if to_next else edges[1]
        total = jnp.where(place < 3, total, jnp.where(place < 6, middle, pltpu.roll(edges[2], 3, 1)))
    return total


def place_group(before, after, slot):
    width = before.shape[1]
    lower, upper = ((0, 5), (width - 3, 2), (width - 5, width - 1))[slot]
    return (pltpu.roll(before, lower, 1) if lower else before), pltpu.roll(after, upper, 1)


def pack_y(fields, permittivity, even, *refs, n_rows):
    blocks, refs = (refs[0], refs[1:]) if n_rows else (None, refs)
    strips, *to_y = refs
    layers, cells_x, width = fields.shape[1:]
    ring = cells_x + TILE
    px = lax.axis_index("xs") % 2

    def fill(message, to_next):
        for r in range(ring // TILE):
            rows = slice(r * TILE, (r + 1) * TILE)
            for g, parts in enumerate(Y_GROUPS):
                packed = []
                for c in parts:

                    def tile_of(z):
                        if r * TILE == cells_x:
                            return halo_tile(even, even, px, c, z, layers)
                        return own_tile(fields, permittivity, c, z, rows)

                    packed.append(pack_strip(tile_of, layers, 5 if to_next else 3))
                    if r * TILE < cells_x:
                        strips[int(to_next), c, rows, :] = packed[-1]
                at = slice(g * ring + r * TILE, g * ring + (r + 1) * TILE)
                message[at, :] = pack_group(packed, to_next)

    for swap, message in enumerate(to_y):
        is_next = lax.axis_index("ys") % 2 == swap
        for to_next in (False, True):
            pl.when(is_next == to_next)(functools.partial(fill, message, to_next))
    if n_rows:
        end = len(Y_GROUPS) * ring
        to_y[0][end : end + n_rows, :] = blocks[...]
        to_y[0][end + n_rows : end + 2 * n_rows, :] = even[x_message_rows(layers) :, :]


def own_tile(fields, permittivity, c, z, rows):
    return fields[c, z, rows, :] if c < 6 else time_step / permittivity[z, rows, :]


def row_index(shape):
    fold = lax.broadcasted_iota(jnp.int32, shape, 0)
    return lax.broadcasted_iota(jnp.int32, shape, 1) * shape[0] + fold


def gather_sources(sets, px, me, totals, n_adj, cells_x):
    mine, other = totals[0], totals[1]
    row_at = row_index(mine.shape).astype(jnp.float32)
    own_index = jnp.where(me == 0, 0.0, 1.0)
    for ref, start, is_next in sets:
        for b in range(n_adj):
            value = ref[start + b : start + b + 1, :]
            code = ref[start + n_adj + b : start + n_adj + b + 1, :]
            owner = jnp.where(code >= cells_x, 1.0, 0.0)
            row = code - cells_x * owner
            if is_next is not None:
                after = jnp.where(row < REACH, row + cells_x, -1.0)
                before = jnp.where(row >= cells_x - REACH, row + TILE, -1.0)
                row = jnp.where(is_next, after, before)
            is_mine = owner == own_index
            mine = mine + jnp.where(row_at == jnp.where(is_mine, row, -1.0), value, 0.0)
            other = other + jnp.where(row_at == jnp.where(is_mine, -1.0, row), value, 0.0)
    totals[0], totals[1] = mine, other


def place_sources(totals, me, source):
    mine, other = totals[0], totals[1]
    lane = lanes_of(mine.shape)
    slot = (lane >= SLOT * ZS) & (lane < SLOT * (ZS + 1))
    place = lane - SLOT * ZS
    shift = SLOT * ZS + 3
    before = jnp.where(me == 0, 0.0, pltpu.roll(other, shift, 2))
    source[0] = mine
    source[1] = jnp.where(slot, jnp.where(place < 3, before, pltpu.roll(mine, shift, 2)), 0.0)
    shift = SLOT * ZS + 5
    after = jnp.where(me == 0, pltpu.roll(other, shift, 2), 0.0)
    source[2] = jnp.where(slot, jnp.where(place < 5, pltpu.roll(mine, shift, 2), after), 0.0)


def next_x(v):
    return jnp.concatenate([v[1:], pltpu.roll(v[0:1], v.shape[1] - 1, 1)], 0)


def prev_x(v):
    return jnp.concatenate([pltpu.roll(v[-1:], 1, 1), v[:-1]], 0)


def lane_roll(v, shift):
    return pltpu.roll(v, shift % v.shape[2], 2)


def zeros(shape):
    return jnp.zeros(shape, jnp.float32)


def unfold(ref, fold):
    return jnp.stack([ref[pl.ds(j, TILE, stride=fold), :] for j in range(fold)])


def fold_back(ref, v):
    for j in range(v.shape[0]):
        ref[pl.ds(j, TILE, stride=v.shape[0]), :] = v[j]


def step_size(full):
    outside = (row_index(full) >= full[0] * TILE - REACH) & (lax.axis_index("xs") == 0)
    return jnp.where(outside, 0.0, time_step)


def evolve_strips(strips, halo_strips, y_halos, diag_halos, source, strip, edge_e, edge_h):
    me = lax.axis_index("ys")
    ring, width = strips.shape[2] + TILE, strips.shape[3]
    fold = ring // TILE
    full = (fold, TILE, width)
    for g, parts in enumerate(Y_GROUPS):
        for r in range(fold):
            before, after = zeros((TILE, width)), zeros((TILE, width))
            at = g * ring + r * TILE
            for k, (y_ref, d_ref) in enumerate(zip(y_halos, diag_halos)):
                block = y_ref[at : at + TILE, :]
                if r + 1 == fold:
                    odd_half = (rows_of(block.shape) >= REACH) == (lax.axis_index("xs") % 2 == 0)
                    corner = jnp.where(at_end("xs"), 0.0, d_ref[g * TILE : (g + 1) * TILE, :])
                    block = jnp.where(odd_half, corner, block)
                if k:
                    block = jnp.where(at_end("ys"), 0.0, block)
                is_next = me % 2 == k
                after = jnp.where(is_next, block, after)
                before = jnp.where(is_next, before, block)
            place = lanes_of(before.shape) % SLOT
            rows = slice(r * TILE, (r + 1) * TILE)
            for slot, c in enumerate(parts):
                lower, upper = place_group(before, after, slot)
                own = [strips[k, c, rows, :] if r + 1 < fold else halo_strips[k, c] for k in (0, 1)]
                strip[0, c, rows, :] = jnp.where(place < 3, lower, own[0])
                strip[1, c, rows, :] = jnp.where(place >= 5, upper, own[1])
    lane = lanes_of(full)
    place = lane % SLOT
    for side in (0, 1):
        ex, ey, ez, hx, hy, hz, co = [unfold(strip.at[side, c], fold) for c in range(PARTS)]
        dt = step_size(full)
        if not side:
            dt = jnp.where((place < 3) & (me == 0), 0.0, dt)
        for step in range(STEPS):

            def next_z(v):
                return jnp.where(lane < width - SLOT, lane_roll(v, -SLOT), 0.0)

            def prev_z(v):
                return jnp.where(lane >= SLOT, lane_roll(v, SLOT), 0.0)

            if side:
                edge_e[step] = jnp.where(place == 5, ex, lane_roll(ez, 1))
                if step + 1 == STEPS:
                    continue
            hx = hx - dt * (lane_roll(ez, -1) - ez - (next_z(ey) - ey))
            hy = hy - dt * (next_z(ex) - ex - (next_x(ez) - ez))
            hz = hz - dt * (next_x(ey) - ey - (lane_roll(ex, -1) - ex))
            if not side:
                edge_h[step] = jnp.where(place == 2, hz, lane_roll(hx, 1))
                if step + 1 == STEPS:
                    continue
            ex = ex + co * (hz - lane_roll(hz, 1) - (hy - prev_z(hy)))
            ey = ey + co * (hx - prev_z(hx) - (hz - prev_x(hz)))
            ez = ez + co * (hy - prev_x(hy) - (hx - lane_roll(hx, 1)) - source[1 + side])


def surface_layers(layers):
    return range(max(ZS - STEPS, 0), min(ZS + STEPS + 1, layers))


def prepare_surface(*refs, n_adj, n_rows, n_swaps):
    fields, permittivity, even, odd, angle_wave = refs[1:6]
    strips, state, coeffs, halo_strips, angles = refs[6 + bool(n_adj) : 11 + bool(n_adj)]
    rows, angles_s, sem = refs[-3:]
    fetch = pltpu.make_async_copy(angle_wave, angles_s, sem)
    fetch.start()
    px = lax.axis_index("xs") % 2
    layers, cells_x, width = fields.shape[1:]
    ring = cells_x + TILE
    fold = ring // TILE

    def fill(side):
        for c in range(PARTS):
            for r in range(cells_x // TILE):
                at = slice(r * TILE, (r + 1) * TILE)
                strips[side, c, at, :] = pack_strip(
                    lambda z: own_tile(fields, permittivity, c, z, at), layers, 5 if side else 3
                )

    if n_swaps == 1:
        for side in (0, 1):
            pl.when(lax.axis_index("ys") % 2 == side)(functools.partial(fill, side))
    for c in range(PARTS):
        halos = [halo_tile(even, odd, px, c, z, layers) for z in range(layers)]
        for side, tile in enumerate(pack_strips(lambda z: halos[z], layers)):
            halo_strips[side, c] = tile
        for z in surface_layers(layers):
            rows[c, z, 0:cells_x, :] = fields[c, z] if c < 6 else time_step / permittivity[z]
            rows[c, z, cells_x:ring, :] = halos[z]
            folded = unfold(rows.at[c, z], fold)
            if c < 6:
                state[c, z] = folded
            else:
                coeffs[z] = folded
    if n_adj:
        blocks, totals = refs[6], refs[12]
        totals[...] = zeros(totals.shape)
        end = x_message_rows(layers)
        rows[0, 0, 0:n_rows, :] = jnp.where(at_end("xs"), 0.0, odd[end:, :])
        sets = [(blocks, 0, None), (even, end, px == 0), (rows.at[0, 0], 0, px == 1)]
        gather_sources(sets, px, lax.axis_index("ys"), totals, n_adj, cells_x)
    fetch.wait()
    per_block = angle_wave.shape[0] // lax.axis_size("xs")
    for k in range(angles.shape[0]):
        owner = lax.axis_index("xs") ^ (k // per_block * NEAR)
        one = angles_s[owner * per_block + k % per_block]
        angles[k : k + 1, :] = jnp.full((1, angles.shape[1]), one, jnp.int32)


def surface_steps(*refs, n_adj, n_rows, n_swaps):
    before, coeffs, halo_strips, strips = refs[:4]
    y_halos, diag_halos = refs[4 : 4 + n_swaps], refs[4 + n_swaps : 4 + 2 * n_swaps]
    given, out, source, edge_e, edge_h, rows, state, strip, totals = refs[4 + 2 * n_swaps :]
    px = lax.axis_index("xs") % 2
    me = lax.axis_index("ys")
    layers = before.shape[1]
    full = before.shape[2:]
    fold, width = full[0], full[2]
    cells_x = (fold - 1) * TILE
    lane = lanes_of(full)

    if n_adj:
        end = len(Y_GROUPS) * fold * TILE
        sets = [
            (y_halos[0], end, None),
            (y_halos[0], end + n_rows, px == 0),
            (rows.at[0], 0, px == 1),
        ]
        corner_rows = diag_halos[0][len(Y_GROUPS) * TILE :, :]
        rows[0, 0:n_rows, :] = jnp.where(at_end("xs"), 0.0, corner_rows)
        totals[...] = given[...]
        gather_sources(sets, px, me, totals, n_adj, cells_x)
        place_sources(totals, me, source)
    else:
        source[...] = given[...]
    evolve_strips(strips, halo_strips, y_halos, diag_halos, source, strip, edge_e, edge_h)

    dt = step_size(full)
    for step in range(STEPS):
        final = step + 1 == STEPS
        low, high = max(ZS - STEPS + step, 0), min(ZS + STEPS - 1 - step, layers - 1)

        def load(c, z):
            return state[c, z] if step else before[c, z]

        def store(c, z, v):
            if not final:
                state[c, z] = v
            elif z == ZS and c in (0, 1, 3, 4):
                fold_back(rows.at[c], v)

        below = None
        ex, ey = load(0, low), load(1, low)
        for z in range(low, high + 1):
            ez, hx, hy, hz = [load(c, z) for c in range(2, 6)]
            if z + 1 < layers:
                ex_above, ey_above = load(0, z + 1), load(1, z + 1)
            else:
                ex_above, ey_above = jnp.zeros(full, jnp.float32), jnp.zeros(full, jnp.float32)
            edge = lane_roll(edge_e[step], width - 1 - (SLOT * z + 5))
            ex_y = jnp.where(lane == width - 1, edge, lane_roll(ex, -1))
            ez_y = lane_roll(jnp.where(lane == 0, edge, ez), -1)
            hx = hx - dt * (ez_y - ez - (ey_above - ey))
            hy = hy - dt * (ex_above - ex - (next_x(ez) - ez))
            hz = hz - dt * (next_x(ey) - ey - (ex_y - ex))
            for c, v in ((3, hx), (4, hy), (5, hz)):
                store(c, z, v)
            if z == 0 or below:
                co = coeffs[z]
                hx_z = hx - below[0] if z else hx
                hy_z = hy - below[1] if z else hy
                edge = lane_roll(edge_h[step], width - 1 - (SLOT * z + 2))
                hx_y = jnp.where(lane == 0, edge, lane_roll(hx, 1))
                hz_y = lane_roll(jnp.where(lane == width - 1, edge, hz), 1)
                store(0, z, ex + co * (hz - hz_y - hy_z))
                store(1, z, ey + co * (hx_z - (hz - prev_x(hz))))
                change = hy - prev_x(hy) - (hx - hx_y)
                if z == ZS:
                    change = change - source[0]
                store(2, z, ez + co * change)
            below = (hx, hy)
            ex, ey = ex_above, ey_above
    for k, (c, sign) in enumerate(((4, -1.0), (3, 1.0), (1, 1.0), (0, -1.0))):
        out[:, k * width : (k + 1) * width] = sign * rows[c, 0:cells_x, :]


def take_steps(first, last, layers, refs, load, store, load_coeff, after_layer=None):
    source, edge_e, edge_h = refs
    full = source.shape[1:]
    width = full[2]
    lane = lanes_of(full)
    dt = step_size(full)
    for step in range(first, last):

        def advance_h(z):
            ex, ey, ez, hx, hy, hz = [load(step, c, z) for c in range(6)]
            edge = lane_roll(edge_e[step], 2 * width - 1 - (SLOT * z + 5))
            ex_y = jnp.where(lane == width - 1, edge, lane_roll(ex, -1))
            ez_y = lane_roll(jnp.where(lane == 0, edge, ez), -1)
            store(step, 3, z, hx - dt * (ez_y - ez - (load(step, 1, z + 1) - ey)))
            store(step, 4, z, hy - dt * (load(step, 0, z + 1) - ex - (next_x(ez) - ez)))
            store(step, 5, z, hz - dt * (next_x(ey) - ey - (ex_y - ex)))

        def advance_e(z):
            hx, hy, hz = [load(step + 1, c, z) for c in range(3, 6)]
            co = load_coeff(z)
            edge = lane_roll(edge_h[step], 2 * width - 1 - (SLOT * z + 2))
            hx_y = jnp.where(lane == 0, edge, lane_roll(hx, 1))
            hz_y = lane_roll(jnp.where(lane == width - 1, edge, hz), 1)
            change = hz - hz_y - (hy - load(step + 1, 4, z - 1))
            store(step, 0, z, load(step, 0, z) + co * change)
            change = hx - load(step + 1, 3, z - 1) - (hz - prev_x(hz))
            store(step, 1, z, load(step, 1, z) + co * change)
            change = hy - prev_x(hy) - (hx - hx_y) - jnp.where(z == ZS, source[0], 0.0)
            store(step, 2, z, load(step, 2, z) + co * change)
            if after_layer and step + 1 == last:
                after_layer(z)

        repeat(0, layers, advance_h, TOGETHER)
        repeat(0, layers, advance_e, TOGETHER)


def zero_outside(ref, layers):
    for c in (0, 1):
        ref[c, layers + 1] = zeros(ref.shape[2:])
        ref[c + 3, 0] = zeros(ref.shape[2:])


def early_steps(*refs):
    fields, permittivity, even, odd, *carried = refs[:7]
    state, coeffs, grid, coeff_rows = refs[7:]
    px = lax.axis_index("xs") % 2
    layers, cells_x, width = fields.shape[1:]
    ring = cells_x + TILE
    fold = ring // TILE

    def build(z):
        for c in range(PARTS):
            ref = grid.at[c, z + 1] if c < 6 else coeff_rows.at[z]
            ref[0:cells_x, :] = fields[c, z] if c < 6 else time_step / permittivity[z]
            ref[cells_x:ring, :] = halo_tile(even, odd, px, c, z, layers)
        coeffs[z] = unfold(coeff_rows.at[z], fold)

    repeat(0, layers, build, TOGETHER // 2)
    for c in (0, 1):
        grid[c, layers + 1] = zeros((ring, width))
    zero_outside(state, layers)

    def load(step, c, z):
        return state[c, z + 1] if step else unfold(grid.at[c, z + 1], fold)

    def store(step, c, z, v):
        state[c, z + 1] = v

    take_steps(0, EARLY, layers, carried, load, store, lambda z: coeffs[z])


def later_steps(*refs):
    before, coeffs, *carried = refs[:5]
    out, state, grid, sems = refs[5:]
    layers, cells_x = out.shape[1:3]

    def copy_out(z):
        done = grid.at[:, z, pl.ds(0, cells_x), :]
        return pltpu.make_async_copy(done, out.at[:, z], sems.at[z])

    zero_outside(state, layers)

    def load(step, c, z):
        return (before if step == EARLY else state)[c, z + 1]

    def store(step, c, z, v):
        if step + 1 < STEPS or c >= 3:
            state[c, z + 1] = v
        if step + 1 == STEPS:
            fold_back(grid.at[c, z], v)

    take_steps(
        EARLY,
        STEPS,
        layers,
        carried,
        load,
        store,
        lambda z: coeffs[z],
        lambda z: copy_out(z).start(),
    )
    repeat(0, layers, lambda z: copy_out(z).wait())


def multiply(weights, *refs, n_tiles):
    tiles, parts = refs[:n_tiles], refs[n_tiles:]
    total = jnp.dot(
        weights[...],
        jnp.concatenate([tile[...] for tile in tiles], 0),
        precision=lax.Precision.HIGHEST,
        preferred_element_type=jnp.float32,
    )
    rows = parts[0].shape[0]
    for k, part in enumerate(parts):
        part[...] = total[k * rows : (k + 1) * rows]


def add_parts(*refs):
    parts, out = refs[:-1], refs[-1]
    total = parts[0][...]
    for part in parts[1:]:
        total = total + part[...]
    width = out.shape[2]
    for k in range(out.shape[1]):
        out[:, k, :] = total[:, k * width : (k + 1) * width]


def shape_of(*dims):
    return jax.ShapeDtypeStruct(dims, jnp.float32)


def far_field_weights(angles, xs_size, cells_x):
    column = jnp.arange(NEAR * cells_x, dtype=jnp.int32)
    owner = lax.axis_index("xs") ^ (column // cells_x)
    phase = angles * (X0 + owner * cells_x + column % cells_x)[None, :] % GRID_X
    angle = phase.astype(jnp.float32) * (2.0 * math.pi / GRID_X)
    scale = 1.0 / math.sqrt(cells_x * xs_size)
    both = jnp.stack([jnp.cos(angle) * scale, -jnp.sin(angle) * scale], axis=1)
    return both.reshape(-1, NEAR * cells_x)


def far_field_exchange(tile, angles, xs_size, beside, finish):
    cells_x, columns = tile.shape
    weights = far_field_weights(angles, xs_size, cells_x)

    def across(block, mask):
        return lax.ppermute(block, "xs", [(i, i ^ mask) for i in range(xs_size)])

    third = across(tile, 2)
    second = across(tile, 1)
    third, beside = lax.optimization_barrier((third, beside))
    fourth = across(third, 1)
    far = xs_size // NEAR
    rows = weights.shape[0] // far
    parts = pl.pallas_call(
        functools.partial(multiply, n_tiles=NEAR),
        out_shape=(shape_of(rows, columns),) * far,
        in_specs=[VMEM] * (NEAR + 1),
        out_specs=(VMEM,) * far,
        compiler_params=PARAMS,
        name="partial_spectrum",
    )(weights, tile, second, third, fourth)
    arrived = [across(parts[k], k * NEAR) for k in range(far - 1, 0, -1)]
    finished = finish(beside)
    far_field = pl.pallas_call(
        add_parts,
        out_shape=shape_of(rows, 4, columns // 4),
        in_specs=[VMEM] * far,
        out_specs=VMEM,
        compiler_params=PARAMS,
        name="add_arrived",
    )(parts[0], *arrived)
    return far_field, finished


def gathered_sources(adj_values, adj_owner, adj_row, cells_x, cells_y):
    groups = lax.axis_size("ys")
    owners = adj_owner[:, 0]
    hits = (owners[:, None] == jnp.arange(groups, dtype=jnp.int32)[None, :]).astype(jnp.int32)
    before = jnp.cumsum(hits, axis=0) - hits
    slot_index = owners * CAP + jnp.sum(before * hits, axis=1)
    placing = (jnp.arange(groups * CAP, dtype=jnp.int32)[:, None] == slot_index[None, :]).astype(
        jnp.float32
    )
    rows = jnp.broadcast_to(adj_row.astype(jnp.float32)[:, None], (adj_row.shape[0], 1))
    outgoing = jnp.dot(
        placing, jnp.concatenate([adj_values, rows], 1), precision=lax.Precision.HIGHEST
    ).reshape(groups, CAP, cells_y + 1)
    incoming = lax.all_to_all(outgoing, "ys", split_axis=0, concat_axis=0, tiled=True)
    incoming = incoming.reshape(groups * CAP, cells_y + 1)
    landing = (
        jnp.arange(cells_x, dtype=jnp.float32)[:, None] == incoming[:, cells_y][None, :]
    ).astype(jnp.float32)
    current = jnp.dot(landing, incoming[:, :cells_y], precision=lax.Precision.HIGHEST)

    def shifted(block, axis, distance):
        size = lax.axis_size(axis)
        route = [(i, i + distance) for i in range(size) if 0 <= i + distance < size]
        return lax.ppermute(block, axis, route)

    after = shifted(current[:REACH], "xs", -1)
    before = shifted(current[-REACH:], "xs", 1)
    ringed = jnp.concatenate([current, after, before], 0)
    right = shifted(ringed[:, :3], "ys", -1)
    left = shifted(ringed[:, -3:], "ys", 1)
    start, end = SLOT * ZS, cells_y - SLOT * (ZS + 1)
    first = jnp.pad(jnp.concatenate([left, ringed[:, :5]], 1), ((0, 0), (start, end)))
    second = jnp.pad(jnp.concatenate([ringed[:, -5:], right], 1), ((0, 0), (start, end)))
    folded = jnp.stack([ringed, first, second]).reshape(3, TILE, -1, cells_y)
    return folded.transpose(0, 2, 1, 3)


def on_device(fields, permittivity, adj_values, adj_owner, adj_row, angle_wave):
    layers, cells_x, cells_y = fields.shape[1:]
    xs_size, ys_size = lax.axis_size("xs"), lax.axis_size("ys")
    raw = ys_size == 2
    n_adj = adj_values.shape[0] if raw else 0
    n_rows = -(-2 * n_adj // TILE) * TILE
    ring = cells_x + TILE
    x_rows = x_message_rows(layers) + n_rows
    y_rows = len(Y_GROUPS) * ring + 2 * n_rows
    d_rows = len(Y_GROUPS) * TILE + n_rows
    y_swaps = swaps(ys_size)

    extra = (adj_values, adj_row, adj_owner.reshape(-1)) if raw else ()
    x_message = shape_of(x_rows, cells_y)
    made = (x_message,) * 2 + ((shape_of(n_rows, cells_y),) if raw else ())
    made += (shape_of(d_rows, cells_y),) * len(y_swaps)
    to_even, to_odd, *packed = pl.pallas_call(
        functools.partial(pack_x, n_adj=n_adj, n_swaps=len(y_swaps)),
        out_shape=made,
        in_specs=[ANY] * (2 + len(extra)),
        out_specs=(VMEM,) * len(made),
        scratch_shapes=[
            pltpu.VMEM((2, 6, layers, TILE, cells_y), jnp.float32),
            pltpu.VMEM((2, layers, TILE, cells_y), jnp.float32),
        ]
        + ([pltpu.SMEM((n_adj,), jnp.int32)] * 2 if raw else [])
        + [pltpu.SemaphoreType.DMA((4 + len(extra),))],
        compiler_params=PARAMS,
        name="pack_x_edges",
    )(*[pltpu.with_memory_space_constraint(x, pltpu.HBM) for x in (fields, permittivity, *extra)])
    blocks, to_diag = (packed[:1], packed[1:]) if raw else ([], packed)
    both = ("xs", "ys")
    from_even = lax.ppermute(to_even, "xs", swaps(xs_size)[0])
    straight = odd_route(xs_size, ys_size, [(i, i) for i in range(ys_size)])
    from_odd = lax.ppermute(to_odd, both, straight)
    diag_halos = [
        lax.ppermute(message, both, odd_route(xs_size, ys_size, route))
        for message, route in zip(to_diag, y_swaps)
    ]

    made = (shape_of(2, PARTS, cells_x, cells_y),) + (shape_of(y_rows, cells_y),) * len(y_swaps)
    strips, *to_y = pl.pallas_call(
        functools.partial(pack_y, n_rows=n_rows),
        out_shape=made,
        in_specs=[VMEM] * (3 + len(blocks)),
        out_specs=(VMEM,) * len(made),
        compiler_params=PARAMS,
        name="pack_y_edges",
    )(fields, permittivity, from_even, *blocks)
    y_halos = [lax.ppermute(message, "ys", route) for message, route in zip(to_y, y_swaps)]

    fold = ring // TILE
    folded = (fold, TILE, cells_y)
    n_angles = angle_wave.shape[0] // NEAR
    made = (
        strips,
        shape_of(6, layers, *folded),
        shape_of(layers, *folded),
        shape_of(2, PARTS, TILE, cells_y),
        jax.ShapeDtypeStruct((n_angles, NEAR * cells_x), jnp.int32),
    ) + ((shape_of(2, *folded),) if raw else ())
    prepared = pl.pallas_call(
        functools.partial(prepare_surface, n_adj=n_adj, n_rows=n_rows, n_swaps=len(y_swaps)),
        out_shape=[jax.ShapeDtypeStruct(x.shape, x.dtype) for x in made],
        in_specs=[VMEM] * 5 + [ANY] + [VMEM] * len(blocks),
        input_output_aliases={0: 0},
        out_specs=(VMEM,) * len(made),
        scratch_shapes=[
            pltpu.VMEM((PARTS, layers, ring, cells_y), jnp.float32),
            pltpu.SMEM(angle_wave.shape, jnp.int32),
            pltpu.SemaphoreType.DMA(()),
        ],
        compiler_params=PARAMS,
        name="prepare_surface",
    )(
        strips,
        fields,
        permittivity,
        from_even,
        from_odd,
        pltpu.with_memory_space_constraint(angle_wave, pltpu.HBM),
        *blocks,
    )
    strips, *prepared = prepared
    angles = prepared[3]
    if raw:
        sources = prepared[4:]
    else:
        sources = (gathered_sources(adj_values, adj_owner, adj_row, cells_x, cells_y),)
    operands = (*prepared[:3], strips, *y_halos, *diag_halos, *sources)
    tile, *carried = pl.pallas_call(
        functools.partial(surface_steps, n_adj=n_adj, n_rows=n_rows, n_swaps=len(y_swaps)),
        out_shape=(
            shape_of(cells_x, 4 * cells_y),
            shape_of(3, *folded),
            shape_of(STEPS, *folded),
            shape_of(STEPS, *folded),
        ),
        in_specs=[VMEM] * len(operands),
        out_specs=(VMEM,) * 4,
        scratch_shapes=[
            pltpu.VMEM((6, ring, cells_y), jnp.float32),
            pltpu.VMEM((6, layers, *folded), jnp.float32),
            pltpu.VMEM((2, PARTS, ring, cells_y), jnp.float32),
            pltpu.VMEM((2, *folded), jnp.float32),
        ],
        compiler_params=PARAMS,
        name="surface_steps",
    )(*operands)

    state_shape = (6, layers + 2, *folded)
    operands = (fields, permittivity, from_even, from_odd, *carried)
    stepped = pl.pallas_call(
        early_steps,
        out_shape=(shape_of(*state_shape), shape_of(layers, *folded)),
        in_specs=[VMEM] * len(operands),
        out_specs=(VMEM, VMEM),
        scratch_shapes=[
            pltpu.VMEM((6, layers + 2, ring, cells_y), jnp.float32),
            pltpu.VMEM((layers, ring, cells_y), jnp.float32),
        ],
        compiler_params=PARAMS,
        name="early_steps",
    )(*operands)

    def finish(stepped):
        return pl.pallas_call(
            later_steps,
            out_shape=shape_of(*fields.shape),
            in_specs=[VMEM] * 5,
            out_specs=ANY,
            scratch_shapes=[
                pltpu.VMEM(state_shape, jnp.float32),
                pltpu.VMEM((6, layers, ring, cells_y), jnp.float32),
                pltpu.SemaphoreType.DMA((layers,)),
            ],
            compiler_params=PARAMS,
            name="later_steps",
        )(*stepped, *carried)

    far, new_fields = far_field_exchange(tile, angles, xs_size, stepped, finish)
    per_block = angle_wave.shape[0] // xs_size
    return (new_fields, far.reshape(per_block, 2, 4, cells_y))


def solution(mesh):
    placed = (
        P(None, None, "xs", "ys"),
        P(None, "xs", "ys"),
        P(("xs", "ys"), None),
        P(("xs", "ys"), None),
        P(("xs", "ys")),
        P(),
    )
    return jax.shard_map(
        on_device,
        mesh=mesh,
        in_specs=placed,
        out_specs=(P(None, None, "xs", "ys"), P("xs", None, None, "ys")),
        check_vma=False,
    )
```

```python
import functools
import math

import jax
import jax.numpy as jnp
from jax import lax
from jax.experimental import pallas as pl
from jax.experimental.pallas import tpu as pltpu
from jax.sharding import PartitionSpec as P

STEPS = 3
CAP = 4
GRID_X = 5000
X0 = 2000
ZS = 8

time_step = 0.5

TILE = 8
REACH = 4
SLOT = 8
PARTS = 7
X_GROUPS = ((0, 1, 3), (2, 4, 6), (5,))
Y_GROUPS = ((0, 2, 4), (1, 3, 6), (5,))
TOGETHER = 8
EARLY = 2
NEAR = 4

VMEM = pl.BlockSpec(memory_space=pltpu.VMEM)
ANY = pl.BlockSpec(memory_space=pl.ANY)
PARAMS = pltpu.CompilerParams(vmem_limit_bytes=24 * 1024 * 1024)


def lanes_of(shape):
    return lax.broadcasted_iota(jnp.int32, shape, len(shape) - 1)


def rows_of(shape):
    return lax.broadcasted_iota(jnp.int32, shape, len(shape) - 2)


def swaps(size):
    found = []
    for first in (0, 1):
        pairs = [(i, i + 1) for i in range(first, size - 1, 2)]
        if first and size > 2 and size % 2 == 0:
            pairs.append((size - 1, 0))
        if pairs:
            found.append(pairs + [(j, i) for i, j in pairs])
    return found


def odd_route(xs_size, ys_size, y_route):
    ends = [0] + ([xs_size - 1] if xs_size % 2 == 0 else [])
    pairs = [(i, i + 1) for i in range(1, xs_size - 1, 2)]
    pairs += [(j, i) for i, j in pairs]
    route = [(a * ys_size + s, b * ys_size + t) for a, b in pairs for s, t in y_route]
    near = swaps(ys_size)[0]
    return route + [(e * ys_size + s, e * ys_size + t) for e in ends for s, t in near]


def at_end(axis):
    index = lax.axis_index(axis)
    return (index == 0) | (index == lax.axis_size(axis) - 1)


def x_message_rows(layers):
    return (2 * layers + layers // 2) * TILE


def halo_tile(even, odd, px, c, z, layers):
    group = [c in parts for parts in X_GROUPS].index(True)
    slot = X_GROUPS[group].index(c)
    tile = 2 * z + group if group < 2 else 2 * layers + z // 2
    at = pl.ds(tile * TILE if isinstance(z, int) else pl.multiple_of(tile * TILE, TILE), TILE)
    from_even, from_odd = even[at, :], jnp.where(at_end("xs"), 0.0, odd[at, :])
    after = jnp.where(px == 0, from_even, from_odd)
    before = jnp.where(px == 0, from_odd, from_even)
    lower = rows_of(after.shape) < REACH

    def placed(first, count):
        back = (TILE - first) % TILE
        to_end = (TILE - count - first) % TILE
        return jnp.where(
            lower,
            pltpu.roll(after, back, 0) if back else after,
            pltpu.roll(before, to_end, 0) if to_end else before,
        )

    if group < 2:
        return placed(3 * slot, 3 if slot < 2 else 2)
    if isinstance(z, int):
        return placed(4 * (z % 2), 3)
    return jnp.where(z % 2 == 0, placed(0, 3), placed(4, 3))


def repeat(first, last, body, together=1):
    count = last - first
    if together >= count:
        for i in range(first, last):
            body(i)
        return
    rounds = count // together

    def several(n, _):
        for k in range(together):
            body(first + n * together + k)

    lax.fori_loop(0, rounds, several, None)
    for i in range(first + rounds * together, last):
        body(i)


def pack_edge(tile_of, message, layers, last):
    def turn(v, shift):
        return pltpu.roll(v, shift, 0) if shift else v

    def send(tile, v):
        message[tile * TILE : (tile + 1) * TILE, :] = v

    row = rows_of((TILE, message.shape[1]))
    shifts = (3, 6, 0) if last else (0, 3, 6)
    for z in range(layers):
        for g in range(2):
            a, b, c = [turn(tile_of(c, z), shift) for c, shift in zip(X_GROUPS[g], shifts)]
            send(2 * z + g, jnp.where(row < 3, a, jnp.where(row < 6, b, c)))
    shifts = (3, 7) if last else (0, 4)
    for pair in range(layers // 2):
        a, b = [turn(tile_of(X_GROUPS[2][0], 2 * pair + k), shifts[k]) for k in (0, 1)]
        send(2 * layers + pair, jnp.where(row < REACH, a, b))


def pack_x(*refs, n_adj, n_swaps):
    fields, permittivity = refs[:2]
    if n_adj:
        values, rows, owners, to_even, to_odd, blocks = refs[2:8]
        to_diag = refs[8 : 8 + n_swaps]
        edges, edge_perm, rows_s, owners_s, sems = refs[8 + n_swaps :]
    else:
        to_even, to_odd = refs[2:4]
        to_diag = refs[4 : 4 + n_swaps]
        edges, edge_perm, sems = refs[4 + n_swaps :]
    px = lax.axis_index("xs") % 2
    layers, cells_x = fields.shape[1:3]
    copies = []
    for k, start in enumerate((0, cells_x - TILE)):
        rows_at = pl.ds(start, TILE)
        copies.append((fields.at[:, :, rows_at, :], edges.at[k]))
        copies.append((permittivity.at[:, rows_at, :], edge_perm.at[k]))
    if n_adj:
        blocks[...] = jnp.zeros(blocks.shape, jnp.float32)
        copies.append((values, blocks.at[pl.ds(0, n_adj), :]))
        copies.append((rows, rows_s))
        copies.append((owners, owners_s))
    copies = [pltpu.make_async_copy(s, d, sems.at[k]) for k, (s, d) in enumerate(copies)]
    for copy in copies:
        copy.start()
    for copy in copies:
        copy.wait()

    def edge_of(k):
        return lambda c, z: edges[k, c, z] if c < 6 else time_step / edge_perm[k, z]

    def pack(first, last):
        pack_edge(edge_of(0), first, layers, False)
        pack_edge(edge_of(1), last, layers, True)

    pl.when(px == 0)(lambda: pack(to_odd, to_even))
    pl.when(px == 1)(lambda: pack(to_even, to_odd))

    def pack_corner(message, k, to_next):
        for g, parts in enumerate(Y_GROUPS):
            packed = [
                pack_strip(lambda z: edge_of(k)(c, z), layers, 5 if to_next else 3) for c in parts
            ]
            message[g * TILE : (g + 1) * TILE, :] = pack_group(packed, to_next)

    for swap, message in enumerate(to_diag):
        is_next = lax.axis_index("ys") % 2 == swap
        for k in (0, 1):
            for to_next in (False, True):
                pl.when((px == k) & (is_next == to_next))(
                    functools.partial(pack_corner, message, k, to_next)
                )
    if n_adj:
        for b in range(n_adj):
            code = rows_s[b] + cells_x * owners_s[b]
            blocks[n_adj + b : n_adj + b + 1, :] = jnp.full(
                (1, blocks.shape[1]), code, jnp.int32
            ).astype(jnp.float32)
        to_even[x_message_rows(layers) :, :] = blocks[...]
        to_odd[x_message_rows(layers) :, :] = blocks[...]
        to_diag[0][len(Y_GROUPS) * TILE :, :] = blocks[...]


def pack_strip(tile_of, layers, shift):
    total = None
    for z in range(layers):
        block = tile_of(z)
        moved = pltpu.roll(block, (SLOT * z + shift) % block.shape[1], 1)
        total = moved if z == 0 else jnp.where(lanes_of(block.shape) // SLOT == z, moved, total)
    return total


def pack_strips(tile_of, layers):
    tiles = [tile_of(z) for z in range(layers)]
    return [pack_strip(lambda z: tiles[z], layers, shift) for shift in (3, 5)]


def pack_group(edges, to_next):
    width = edges[0].shape[1]
    place = lanes_of(edges[0].shape) % SLOT
    total = pltpu.roll(edges[0], width - 2 if to_next else width - 3, 1)
    if len(edges) > 1:
        middle = pltpu.roll(edges[1], 1, 1) if to_next else edges[1]
        total = jnp.where(place < 3, total, jnp.where(place < 6, middle, pltpu.roll(edges[2], 3, 1)))
    return total


def place_group(before, after, slot):
    width = before.shape[1]
    lower, upper = ((0, 5), (width - 3, 2), (width - 5, width - 1))[slot]
    return (pltpu.roll(before, lower, 1) if lower else before), pltpu.roll(after, upper, 1)


def pack_y(fields, permittivity, even, *refs, n_rows):
    blocks, refs = (refs[0], refs[1:]) if n_rows else (None, refs)
    strips, *to_y = refs
    layers, cells_x, width = fields.shape[1:]
    ring = cells_x + TILE
    px = lax.axis_index("xs") % 2

    def fill(message, to_next):
        for r in range(ring // TILE):
            rows = slice(r * TILE, (r + 1) * TILE)
            for g, parts in enumerate(Y_GROUPS):
                packed = []
                for c in parts:

                    def tile_of(z):
                        if r * TILE == cells_x:
                            return halo_tile(even, even, px, c, z, layers)
                        return own_tile(fields, permittivity, c, z, rows)

                    packed.append(pack_strip(tile_of, layers, 5 if to_next else 3))
                    if r * TILE < cells_x:
                        strips[int(to_next), c, rows, :] = packed[-1]
                at = slice(g * ring + r * TILE, g * ring + (r + 1) * TILE)
                message[at, :] = pack_group(packed, to_next)

    for swap, message in enumerate(to_y):
        is_next = lax.axis_index("ys") % 2 == swap
        for to_next in (False, True):
            pl.when(is_next == to_next)(functools.partial(fill, message, to_next))
    if n_rows:
        end = len(Y_GROUPS) * ring
        to_y[0][end : end + n_rows, :] = blocks[...]
        to_y[0][end + n_rows : end + 2 * n_rows, :] = even[x_message_rows(layers) :, :]


def own_tile(fields, permittivity, c, z, rows):
    return fields[c, z, rows, :] if c < 6 else time_step / permittivity[z, rows, :]


def row_index(shape):
    fold = lax.broadcasted_iota(jnp.int32, shape, 0)
    return lax.broadcasted_iota(jnp.int32, shape, 1) * shape[0] + fold


def gather_sources(sets, px, me, totals, n_adj, cells_x):
    mine, other = totals[0], totals[1]
    row_at = row_index(mine.shape).astype(jnp.float32)
    own_index = jnp.where(me == 0, 0.0, 1.0)
    for ref, start, is_next in sets:
        for b in range(n_adj):
            value = ref[start + b : start + b + 1, :]
            code = ref[start + n_adj + b : start + n_adj + b + 1, :]
            owner = jnp.where(code >= cells_x, 1.0, 0.0)
            row = code - cells_x * owner
            if is_next is not None:
                after = jnp.where(row < REACH, row + cells_x, -1.0)
                before = jnp.where(row >= cells_x - REACH, row + TILE, -1.0)
                row = jnp.where(is_next, after, before)
            is_mine = owner == own_index
            mine = mine + jnp.where(row_at == jnp.where(is_mine, row, -1.0), value, 0.0)
            other = other + jnp.where(row_at == jnp.where(is_mine, -1.0, row), value, 0.0)
    totals[0], totals[1] = mine, other


def place_sources(totals, me, source):
    mine, other = totals[0], totals[1]
    lane = lanes_of(mine.shape)
    slot = (lane >= SLOT * ZS) & (lane < SLOT * (ZS + 1))
    place = lane - SLOT * ZS
    shift = SLOT * ZS + 3
    before = jnp.where(me == 0, 0.0, pltpu.roll(other, shift, 2))
    source[0] = mine
    source[1] = jnp.where(slot, jnp.where(place < 3, before, pltpu.roll(mine, shift, 2)), 0.0)
    shift = SLOT * ZS + 5
    after = jnp.where(me == 0, pltpu.roll(other, shift, 2), 0.0)
    source[2] = jnp.where(slot, jnp.where(place < 5, pltpu.roll(mine, shift, 2), after), 0.0)


def next_x(v):
    return jnp.concatenate([v[1:], pltpu.roll(v[0:1], v.shape[1] - 1, 1)], 0)


def prev_x(v):
    return jnp.concatenate([pltpu.roll(v[-1:], 1, 1), v[:-1]], 0)


def lane_roll(v, shift):
    return pltpu.roll(v, shift % v.shape[2], 2)


def zeros(shape):
    return jnp.zeros(shape, jnp.float32)


def unfold(ref, fold):
    return jnp.stack([ref[pl.ds(j, TILE, stride=fold), :] for j in range(fold)])


def fold_back(ref, v):
    for j in range(v.shape[0]):
        ref[pl.ds(j, TILE, stride=v.shape[0]), :] = v[j]


def step_size(full):
    outside = (row_index(full) >= full[0] * TILE - REACH) & (lax.axis_index("xs") == 0)
    return jnp.where(outside, 0.0, time_step)


def evolve_strips(strips, halo_strips, y_halos, diag_halos, source, strip, edge_e, edge_h):
    me = lax.axis_index("ys")
    ring, width = strips.shape[2] + TILE, strips.shape[3]
    fold = ring // TILE
    full = (fold, TILE, width)
    for g, parts in enumerate(Y_GROUPS):
        for r in range(fold):
            before, after = zeros((TILE, width)), zeros((TILE, width))
            at = g * ring + r * TILE
            for k, (y_ref, d_ref) in enumerate(zip(y_halos, diag_halos)):
                block = y_ref[at : at + TILE, :]
                if r + 1 == fold:
                    odd_half = (rows_of(block.shape) >= REACH) == (lax.axis_index("xs") % 2 == 0)
                    corner = jnp.where(at_end("xs"), 0.0, d_ref[g * TILE : (g + 1) * TILE, :])
                    block = jnp.where(odd_half, corner, block)
                if k:
                    block = jnp.where(at_end("ys"), 0.0, block)
                is_next = me % 2 == k
                after = jnp.where(is_next, block, after)
                before = jnp.where(is_next, before, block)
            place = lanes_of(before.shape) % SLOT
            rows = slice(r * TILE, (r + 1) * TILE)
            for slot, c in enumerate(parts):
                lower, upper = place_group(before, after, slot)
                own = [strips[k, c, rows, :] if r + 1 < fold else halo_strips[k, c] for k in (0, 1)]
                strip[0, c, rows, :] = jnp.where(place < 3, lower, own[0])
                strip[1, c, rows, :] = jnp.where(place >= 5, upper, own[1])
    lane = lanes_of(full)
    place = lane % SLOT
    for side in (0, 1):
        ex, ey, ez, hx, hy, hz, co = [unfold(strip.at[side, c], fold) for c in range(PARTS)]
        dt = step_size(full)
        if not side:
            dt = jnp.where((place < 3) & (me == 0), 0.0, dt)
        for step in range(STEPS):

            def next_z(v):
                return jnp.where(lane < width - SLOT, lane_roll(v, -SLOT), 0.0)

            def prev_z(v):
                return jnp.where(lane >= SLOT, lane_roll(v, SLOT), 0.0)

            if side:
                edge_e[step] = jnp.where(place == 5, ex, lane_roll(ez, 1))
                if step + 1 == STEPS:
                    continue
            hx = hx - dt * (lane_roll(ez, -1) - ez - (next_z(ey) - ey))
            hy = hy - dt * (next_z(ex) - ex - (next_x(ez) - ez))
            hz = hz - dt * (next_x(ey) - ey - (lane_roll(ex, -1) - ex))
            if not side:
                edge_h[step] = jnp.where(place == 2, hz, lane_roll(hx, 1))
                if step + 1 == STEPS:
                    continue
            ex = ex + co * (hz - lane_roll(hz, 1) - (hy - prev_z(hy)))
            ey = ey + co * (hx - prev_z(hx) - (hz - prev_x(hz)))
            ez = ez + co * (hy - prev_x(hy) - (hx - lane_roll(hx, 1)) - source[1 + side])


def surface_layers(layers):
    return range(max(ZS - STEPS, 0), min(ZS + STEPS + 1, layers))


def prepare_surface(*refs, n_adj, n_rows, n_swaps):
    fields, permittivity, even, odd, angle_wave = refs[1:6]
    strips, state, coeffs, halo_strips, angles = refs[6 + bool(n_adj) : 11 + bool(n_adj)]
    rows, angles_s, sem = refs[-3:]
    fetch = pltpu.make_async_copy(angle_wave, angles_s, sem)
    fetch.start()
    px = lax.axis_index("xs") % 2
    layers, cells_x, width = fields.shape[1:]
    ring = cells_x + TILE
    fold = ring // TILE

    def fill(side):
        for c in range(PARTS):
            for r in range(cells_x // TILE):
                at = slice(r * TILE, (r + 1) * TILE)
                strips[side, c, at, :] = pack_strip(
                    lambda z: own_tile(fields, permittivity, c, z, at), layers, 5 if side else 3
                )

    if n_swaps == 1:
        for side in (0, 1):
            pl.when(lax.axis_index("ys") % 2 == side)(functools.partial(fill, side))
    for c in range(PARTS):
        halos = [halo_tile(even, odd, px, c, z, layers) for z in range(layers)]
        for side, tile in enumerate(pack_strips(lambda z: halos[z], layers)):
            halo_strips[side, c] = tile
        for z in surface_layers(layers):
            rows[c, z, 0:cells_x, :] = fields[c, z] if c < 6 else time_step / permittivity[z]
            rows[c, z, cells_x:ring, :] = halos[z]
            folded = unfold(rows.at[c, z], fold)
            if c < 6:
                state[c, z] = folded
            else:
                coeffs[z] = folded
    if n_adj:
        blocks, totals = refs[6], refs[12]
        totals[...] = zeros(totals.shape)
        end = x_message_rows(layers)
        rows[0, 0, 0:n_rows, :] = jnp.where(at_end("xs"), 0.0, odd[end:, :])
        sets = [(blocks, 0, None), (even, end, px == 0), (rows.at[0, 0], 0, px == 1)]
        gather_sources(sets, px, lax.axis_index("ys"), totals, n_adj, cells_x)
    fetch.wait()
    per_block = angle_wave.shape[0] // lax.axis_size("xs")
    for k in range(angles.shape[0]):
        owner = lax.axis_index("xs") ^ (k // per_block * NEAR)
        one = angles_s[owner * per_block + k % per_block]
        angles[k : k + 1, :] = jnp.full((1, angles.shape[1]), one, jnp.int32)


def surface_steps(*refs, n_adj, n_rows, n_swaps):
    before, coeffs, halo_strips, strips = refs[:4]
    y_halos, diag_halos = refs[4 : 4 + n_swaps], refs[4 + n_swaps : 4 + 2 * n_swaps]
    given, out, source, edge_e, edge_h, rows, state, strip, totals = refs[4 + 2 * n_swaps :]
    px = lax.axis_index("xs") % 2
    me = lax.axis_index("ys")
    layers = before.shape[1]
    full = before.shape[2:]
    fold, width = full[0], full[2]
    cells_x = (fold - 1) * TILE
    lane = lanes_of(full)

    if n_adj:
        end = len(Y_GROUPS) * fold * TILE
        sets = [
            (y_halos[0], end, None),
            (y_halos[0], end + n_rows, px == 0),
            (rows.at[0], 0, px == 1),
        ]
        corner_rows = diag_halos[0][len(Y_GROUPS) * TILE :, :]
        rows[0, 0:n_rows, :] = jnp.where(at_end("xs"), 0.0, corner_rows)
        totals[...] = given[...]
        gather_sources(sets, px, me, totals, n_adj, cells_x)
        place_sources(totals, me, source)
    else:
        source[...] = given[...]
    evolve_strips(strips, halo_strips, y_halos, diag_halos, source, strip, edge_e, edge_h)

    dt = step_size(full)
    for step in range(STEPS):
        final = step + 1 == STEPS
        low, high = max(ZS - STEPS + step, 0), min(ZS + STEPS - 1 - step, layers - 1)

        def load(c, z):
            return state[c, z] if step else before[c, z]

        def store(c, z, v):
            if not final:
                state[c, z] = v
            elif z == ZS and c in (0, 1, 3, 4):
                fold_back(rows.at[c], v)

        below = None
        ex, ey = load(0, low), load(1, low)
        for z in range(low, high + 1):
            ez, hx, hy, hz = [load(c, z) for c in range(2, 6)]
            if z + 1 < layers:
                ex_above, ey_above = load(0, z + 1), load(1, z + 1)
            else:
                ex_above, ey_above = jnp.zeros(full, jnp.float32), jnp.zeros(full, jnp.float32)
            edge = lane_roll(edge_e[step], width - 1 - (SLOT * z + 5))
            ex_y = jnp.where(lane == width - 1, edge, lane_roll(ex, -1))
            ez_y = lane_roll(jnp.where(lane == 0, edge, ez), -1)
            hx = hx - dt * (ez_y - ez - (ey_above - ey))
            hy = hy - dt * (ex_above - ex - (next_x(ez) - ez))
            hz = hz - dt * (next_x(ey) - ey - (ex_y - ex))
            for c, v in ((3, hx), (4, hy), (5, hz)):
                store(c, z, v)
            if z == 0 or below:
                co = coeffs[z]
                hx_z = hx - below[0] if z else hx
                hy_z = hy - below[1] if z else hy
                edge = lane_roll(edge_h[step], width - 1 - (SLOT * z + 2))
                hx_y = jnp.where(lane == 0, edge, lane_roll(hx, 1))
                hz_y = lane_roll(jnp.where(lane == width - 1, edge, hz), 1)
                store(0, z, ex + co * (hz - hz_y - hy_z))
                store(1, z, ey + co * (hx_z - (hz - prev_x(hz))))
                change = hy - prev_x(hy) - (hx - hx_y)
                if z == ZS:
                    change = change - source[0]
                store(2, z, ez + co * change)
            below = (hx, hy)
            ex, ey = ex_above, ey_above
    for k, (c, sign) in enumerate(((4, -1.0), (3, 1.0), (1, 1.0), (0, -1.0))):
        out[:, k * width : (k + 1) * width] = sign * rows[c, 0:cells_x, :]


def take_steps(first, last, layers, refs, load, store, load_coeff, after_layer=None):
    source, edge_e, edge_h = refs
    full = source.shape[1:]
    width = full[2]
    lane = lanes_of(full)
    dt = step_size(full)
    for step in range(first, last):

        def advance_h(z):
            ex, ey, ez, hx, hy, hz = [load(step, c, z) for c in range(6)]
            edge = lane_roll(edge_e[step], 2 * width - 1 - (SLOT * z + 5))
            ex_y = jnp.where(lane == width - 1, edge, lane_roll(ex, -1))
            ez_y = lane_roll(jnp.where(lane == 0, edge, ez), -1)
            store(step, 3, z, hx - dt * (ez_y - ez - (load(step, 1, z + 1) - ey)))
            store(step, 4, z, hy - dt * (load(step, 0, z + 1) - ex - (next_x(ez) - ez)))
            store(step, 5, z, hz - dt * (next_x(ey) - ey - (ex_y - ex)))

        def advance_e(z):
            hx, hy, hz = [load(step + 1, c, z) for c in range(3, 6)]
            co = load_coeff(z)
            edge = lane_roll(edge_h[step], 2 * width - 1 - (SLOT * z + 2))
            hx_y = jnp.where(lane == 0, edge, lane_roll(hx, 1))
            hz_y = lane_roll(jnp.where(lane == width - 1, edge, hz), 1)
            change = hz - hz_y - (hy - load(step + 1, 4, z - 1))
            store(step, 0, z, load(step, 0, z) + co * change)
            change = hx - load(step + 1, 3, z - 1) - (hz - prev_x(hz))
            store(step, 1, z, load(step, 1, z) + co * change)
            change = hy - prev_x(hy) - (hx - hx_y) - jnp.where(z == ZS, source[0], 0.0)
            store(step, 2, z, load(step, 2, z) + co * change)
            if after_layer and step + 1 == last:
                after_layer(z)

        repeat(0, layers, advance_h, TOGETHER)
        repeat(0, layers, advance_e, TOGETHER)


def zero_outside(ref, layers):
    for c in (0, 1):
        ref[c, layers + 1] = zeros(ref.shape[2:])
        ref[c + 3, 0] = zeros(ref.shape[2:])


def early_steps(*refs):
    fields, permittivity, even, odd, *carried = refs[:7]
    state, coeffs, grid, coeff_rows = refs[7:]
    px = lax.axis_index("xs") % 2
    layers, cells_x, width = fields.shape[1:]
    ring = cells_x + TILE
    fold = ring // TILE

    def build(z):
        for c in range(PARTS):
            ref = grid.at[c, z + 1] if c < 6 else coeff_rows.at[z]
            ref[0:cells_x, :] = fields[c, z] if c < 6 else time_step / permittivity[z]
            ref[cells_x:ring, :] = halo_tile(even, odd, px, c, z, layers)
        coeffs[z] = unfold(coeff_rows.at[z], fold)

    repeat(0, layers, build, TOGETHER // 2)
    for c in (0, 1):
        grid[c, layers + 1] = zeros((ring, width))
    zero_outside(state, layers)

    def load(step, c, z):
        return state[c, z + 1] if step else unfold(grid.at[c, z + 1], fold)

    def store(step, c, z, v):
        state[c, z + 1] = v

    take_steps(0, EARLY, layers, carried, load, store, lambda z: coeffs[z])


def later_steps(*refs):
    before, coeffs, *carried = refs[:5]
    out, state, grid, sems = refs[5:]
    layers, cells_x = out.shape[1:3]

    def copy_out(z):
        done = grid.at[:, z, pl.ds(0, cells_x), :]
        return pltpu.make_async_copy(done, out.at[:, z], sems.at[z])

    zero_outside(state, layers)

    def load(step, c, z):
        return (before if step == EARLY else state)[c, z + 1]

    def store(step, c, z, v):
        if step + 1 < STEPS or c >= 3:
            state[c, z + 1] = v
        if step + 1 == STEPS:
            fold_back(grid.at[c, z], v)

    take_steps(
        EARLY,
        STEPS,
        layers,
        carried,
        load,
        store,
        lambda z: coeffs[z],
        lambda z: copy_out(z).start(),
    )
    repeat(0, layers, lambda z: copy_out(z).wait())


def multiply(weights, *refs, n_tiles):
    tiles, parts = refs[:n_tiles], refs[n_tiles:]
    total = jnp.dot(
        weights[...],
        jnp.concatenate([tile[...] for tile in tiles], 0),
        precision=lax.Precision.HIGHEST,
        preferred_element_type=jnp.float32,
    )
    rows = parts[0].shape[0]
    for k, part in enumerate(parts):
        part[...] = total[k * rows : (k + 1) * rows]


def add_parts(*refs):
    parts, out = refs[:-1], refs[-1]
    total = parts[0][...]
    for part in parts[1:]:
        total = total + part[...]
    width = out.shape[2]
    for k in range(out.shape[1]):
        out[:, k, :] = total[:, k * width : (k + 1) * width]


def shape_of(*dims):
    return jax.ShapeDtypeStruct(dims, jnp.float32)


def far_field_weights(angles, xs_size, cells_x):
    column = jnp.arange(NEAR * cells_x, dtype=jnp.int32)
    owner = lax.axis_index("xs") ^ (column // cells_x)
    phase = angles * (X0 + owner * cells_x + column % cells_x)[None, :] % GRID_X
    angle = phase.astype(jnp.float32) * (2.0 * math.pi / GRID_X)
    scale = 1.0 / math.sqrt(cells_x * xs_size)
    both = jnp.stack([jnp.cos(angle) * scale, -jnp.sin(angle) * scale], axis=1)
    return both.reshape(-1, NEAR * cells_x)


def far_field_exchange(tile, angles, xs_size, beside, finish):
    cells_x, columns = tile.shape
    weights = far_field_weights(angles, xs_size, cells_x)

    def across(block, mask):
        return lax.ppermute(block, "xs", [(i, i ^ mask) for i in range(xs_size)])

    third = across(tile, 2)
    second = across(tile, 1)
    fourth = across(tile, 3)
    third, fourth, beside = lax.optimization_barrier((third, fourth, beside))
    far = xs_size // NEAR
    rows = weights.shape[0] // far
    parts = pl.pallas_call(
        functools.partial(multiply, n_tiles=NEAR),
        out_shape=(shape_of(rows, columns),) * far,
        in_specs=[VMEM] * (NEAR + 1),
        out_specs=(VMEM,) * far,
        compiler_params=PARAMS,
        name="partial_spectrum",
    )(weights, tile, second, third, fourth)
    arrived = [across(parts[k], k * NEAR) for k in range(far - 1, 0, -1)]
    finished = finish(beside)
    far_field = pl.pallas_call(
        add_parts,
        out_shape=shape_of(rows, 4, columns // 4),
        in_specs=[VMEM] * far,
        out_specs=VMEM,
        compiler_params=PARAMS,
        name="add_arrived",
    )(parts[0], *arrived)
    return far_field, finished


def gathered_sources(adj_values, adj_owner, adj_row, cells_x, cells_y):
    groups = lax.axis_size("ys")
    owners = adj_owner[:, 0]
    hits = (owners[:, None] == jnp.arange(groups, dtype=jnp.int32)[None, :]).astype(jnp.int32)
    before = jnp.cumsum(hits, axis=0) - hits
    slot_index = owners * CAP + jnp.sum(before * hits, axis=1)
    placing = (jnp.arange(groups * CAP, dtype=jnp.int32)[:, None] == slot_index[None, :]).astype(
        jnp.float32
    )
    rows = jnp.broadcast_to(adj_row.astype(jnp.float32)[:, None], (adj_row.shape[0], 1))
    outgoing = jnp.dot(
        placing, jnp.concatenate([adj_values, rows], 1), precision=lax.Precision.HIGHEST
    ).reshape(groups, CAP, cells_y + 1)
    incoming = lax.all_to_all(outgoing, "ys", split_axis=0, concat_axis=0, tiled=True)
    incoming = incoming.reshape(groups * CAP, cells_y + 1)
    landing = (
        jnp.arange(cells_x, dtype=jnp.float32)[:, None] == incoming[:, cells_y][None, :]
    ).astype(jnp.float32)
    current = jnp.dot(landing, incoming[:, :cells_y], precision=lax.Precision.HIGHEST)

    def shifted(block, axis, distance):
        size = lax.axis_size(axis)
        route = [(i, i + distance) for i in range(size) if 0 <= i + distance < size]
        return lax.ppermute(block, axis, route)

    after = shifted(current[:REACH], "xs", -1)
    before = shifted(current[-REACH:], "xs", 1)
    ringed = jnp.concatenate([current, after, before], 0)
    right = shifted(ringed[:, :3], "ys", -1)
    left = shifted(ringed[:, -3:], "ys", 1)
    start, end = SLOT * ZS, cells_y - SLOT * (ZS + 1)
    first = jnp.pad(jnp.concatenate([left, ringed[:, :5]], 1), ((0, 0), (start, end)))
    second = jnp.pad(jnp.concatenate([ringed[:, -5:], right], 1), ((0, 0), (start, end)))
    folded = jnp.stack([ringed, first, second]).reshape(3, TILE, -1, cells_y)
    return folded.transpose(0, 2, 1, 3)


def on_device(fields, permittivity, adj_values, adj_owner, adj_row, angle_wave):
    layers, cells_x, cells_y = fields.shape[1:]
    xs_size, ys_size = lax.axis_size("xs"), lax.axis_size("ys")
    raw = ys_size == 2
    n_adj = adj_values.shape[0] if raw else 0
    n_rows = -(-2 * n_adj // TILE) * TILE
    ring = cells_x + TILE
    x_rows = x_message_rows(layers) + n_rows
    y_rows = len(Y_GROUPS) * ring + 2 * n_rows
    d_rows = len(Y_GROUPS) * TILE + n_rows
    y_swaps = swaps(ys_size)

    extra = (adj_values, adj_row, adj_owner.reshape(-1)) if raw else ()
    x_message = shape_of(x_rows, cells_y)
    made = (x_message,) * 2 + ((shape_of(n_rows, cells_y),) if raw else ())
    made += (shape_of(d_rows, cells_y),) * len(y_swaps)
    to_even, to_odd, *packed = pl.pallas_call(
        functools.partial(pack_x, n_adj=n_adj, n_swaps=len(y_swaps)),
        out_shape=made,
        in_specs=[ANY] * (2 + len(extra)),
        out_specs=(VMEM,) * len(made),
        scratch_shapes=[
            pltpu.VMEM((2, 6, layers, TILE, cells_y), jnp.float32),
            pltpu.VMEM((2, layers, TILE, cells_y), jnp.float32),
        ]
        + ([pltpu.SMEM((n_adj,), jnp.int32)] * 2 if raw else [])
        + [pltpu.SemaphoreType.DMA((4 + len(extra),))],
        compiler_params=PARAMS,
        name="pack_x_edges",
    )(*[pltpu.with_memory_space_constraint(x, pltpu.HBM) for x in (fields, permittivity, *extra)])
    blocks, to_diag = (packed[:1], packed[1:]) if raw else ([], packed)
    both = ("xs", "ys")
    from_even = lax.ppermute(to_even, "xs", swaps(xs_size)[0])
    straight = odd_route(xs_size, ys_size, [(i, i) for i in range(ys_size)])
    from_odd = lax.ppermute(to_odd, both, straight)
    diag_halos = [
        lax.ppermute(message, both, odd_route(xs_size, ys_size, route))
        for message, route in zip(to_diag, y_swaps)
    ]

    made = (shape_of(2, PARTS, cells_x, cells_y),) + (shape_of(y_rows, cells_y),) * len(y_swaps)
    strips, *to_y = pl.pallas_call(
        functools.partial(pack_y, n_rows=n_rows),
        out_shape=made,
        in_specs=[VMEM] * (3 + len(blocks)),
        out_specs=(VMEM,) * len(made),
        compiler_params=PARAMS,
        name="pack_y_edges",
    )(fields, permittivity, from_even, *blocks)
    y_halos = [lax.ppermute(message, "ys", route) for message, route in zip(to_y, y_swaps)]

    fold = ring // TILE
    folded = (fold, TILE, cells_y)
    n_angles = angle_wave.shape[0] // NEAR
    made = (
        strips,
        shape_of(6, layers, *folded),
        shape_of(layers, *folded),
        shape_of(2, PARTS, TILE, cells_y),
        jax.ShapeDtypeStruct((n_angles, NEAR * cells_x), jnp.int32),
    ) + ((shape_of(2, *folded),) if raw else ())
    prepared = pl.pallas_call(
        functools.partial(prepare_surface, n_adj=n_adj, n_rows=n_rows, n_swaps=len(y_swaps)),
        out_shape=[jax.ShapeDtypeStruct(x.shape, x.dtype) for x in made],
        in_specs=[VMEM] * 5 + [ANY] + [VMEM] * len(blocks),
        input_output_aliases={0: 0},
        out_specs=(VMEM,) * len(made),
        scratch_shapes=[
            pltpu.VMEM((PARTS, layers, ring, cells_y), jnp.float32),
            pltpu.SMEM(angle_wave.shape, jnp.int32),
            pltpu.SemaphoreType.DMA(()),
        ],
        compiler_params=PARAMS,
        name="prepare_surface",
    )(
        strips,
        fields,
        permittivity,
        from_even,
        from_odd,
        pltpu.with_memory_space_constraint(angle_wave, pltpu.HBM),
        *blocks,
    )
    strips, *prepared = prepared
    angles = prepared[3]
    if raw:
        sources = prepared[4:]
    else:
        sources = (gathered_sources(adj_values, adj_owner, adj_row, cells_x, cells_y),)
    operands = (*prepared[:3], strips, *y_halos, *diag_halos, *sources)
    tile, *carried = pl.pallas_call(
        functools.partial(surface_steps, n_adj=n_adj, n_rows=n_rows, n_swaps=len(y_swaps)),
        out_shape=(
            shape_of(cells_x, 4 * cells_y),
            shape_of(3, *folded),
            shape_of(STEPS, *folded),
            shape_of(STEPS, *folded),
        ),
        in_specs=[VMEM] * len(operands),
        out_specs=(VMEM,) * 4,
        scratch_shapes=[
            pltpu.VMEM((6, ring, cells_y), jnp.float32),
            pltpu.VMEM((6, layers, *folded), jnp.float32),
            pltpu.VMEM((2, PARTS, ring, cells_y), jnp.float32),
            pltpu.VMEM((2, *folded), jnp.float32),
        ],
        compiler_params=PARAMS,
        name="surface_steps",
    )(*operands)

    state_shape = (6, layers + 2, *folded)
    operands = (fields, permittivity, from_even, from_odd, *carried)
    stepped = pl.pallas_call(
        early_steps,
        out_shape=(shape_of(*state_shape), shape_of(layers, *folded)),
        in_specs=[VMEM] * len(operands),
        out_specs=(VMEM, VMEM),
        scratch_shapes=[
            pltpu.VMEM((6, layers + 2, ring, cells_y), jnp.float32),
            pltpu.VMEM((layers, ring, cells_y), jnp.float32),
        ],
        compiler_params=PARAMS,
        name="early_steps",
    )(*operands)

    def finish(stepped):
        return pl.pallas_call(
            later_steps,
            out_shape=shape_of(*fields.shape),
            in_specs=[VMEM] * 5,
            out_specs=ANY,
            scratch_shapes=[
                pltpu.VMEM(state_shape, jnp.float32),
                pltpu.VMEM((6, layers, ring, cells_y), jnp.float32),
                pltpu.SemaphoreType.DMA((layers,)),
            ],
            compiler_params=PARAMS,
            name="later_steps",
        )(*stepped, *carried)

    far, new_fields = far_field_exchange(tile, angles, xs_size, stepped, finish)
    per_block = angle_wave.shape[0] // xs_size
    return (new_fields, far.reshape(per_block, 2, 4, cells_y))


def solution(mesh):
    placed = (
        P(None, None, "xs", "ys"),
        P(None, "xs", "ys"),
        P(("xs", "ys"), None),
        P(("xs", "ys"), None),
        P(("xs", "ys")),
        P(),
    )
    return jax.shard_map(
        on_device,
        mesh=mesh,
        in_specs=placed,
        out_specs=(P(None, None, "xs", "ys"), P("xs", None, None, "ys")),
        check_vma=False,
    )
```

```python
import functools
import math

import jax
import jax.numpy as jnp
from jax import lax
from jax.experimental import pallas as pl
from jax.experimental.pallas import tpu as pltpu
from jax.sharding import PartitionSpec as P

STEPS = 3
CAP = 4
GRID_X = 5000
X0 = 2000
ZS = 8

time_step = 0.5

TILE = 8
REACH = 4
SLOT = 8
PARTS = 7
X_GROUPS = ((0, 1, 3), (2, 4, 6), (5,))
Y_GROUPS = ((0, 2, 4), (1, 3, 6), (5,))
TOGETHER = 8
EARLY = 2
NEAR = 4

VMEM = pl.BlockSpec(memory_space=pltpu.VMEM)
ANY = pl.BlockSpec(memory_space=pl.ANY)
PARAMS = pltpu.CompilerParams(vmem_limit_bytes=24 * 1024 * 1024)


def lanes_of(shape):
    return lax.broadcasted_iota(jnp.int32, shape, len(shape) - 1)


def rows_of(shape):
    return lax.broadcasted_iota(jnp.int32, shape, len(shape) - 2)


def swaps(size):
    found = []
    for first in (0, 1):
        pairs = [(i, i + 1) for i in range(first, size - 1, 2)]
        if first and size > 2 and size % 2 == 0:
            pairs.append((size - 1, 0))
        if pairs:
            found.append(pairs + [(j, i) for i, j in pairs])
    return found


def odd_route(xs_size, ys_size, y_route):
    ends = [0] + ([xs_size - 1] if xs_size % 2 == 0 else [])
    pairs = [(i, i + 1) for i in range(1, xs_size - 1, 2)]
    pairs += [(j, i) for i, j in pairs]
    route = [(a * ys_size + s, b * ys_size + t) for a, b in pairs for s, t in y_route]
    near = swaps(ys_size)[0]
    return route + [(e * ys_size + s, e * ys_size + t) for e in ends for s, t in near]


def at_end(axis):
    index = lax.axis_index(axis)
    return (index == 0) | (index == lax.axis_size(axis) - 1)


def x_message_rows(layers):
    return (2 * layers + layers // 2) * TILE


def halo_tile(even, odd, px, c, z, layers):
    group = [c in parts for parts in X_GROUPS].index(True)
    slot = X_GROUPS[group].index(c)
    tile = 2 * z + group if group < 2 else 2 * layers + z // 2
    at = pl.ds(tile * TILE if isinstance(z, int) else pl.multiple_of(tile * TILE, TILE), TILE)
    from_even, from_odd = even[at, :], jnp.where(at_end("xs"), 0.0, odd[at, :])
    after = jnp.where(px == 0, from_even, from_odd)
    before = jnp.where(px == 0, from_odd, from_even)
    lower = rows_of(after.shape) < REACH

    def placed(first, count):
        back = (TILE - first) % TILE
        to_end = (TILE - count - first) % TILE
        return jnp.where(
            lower,
            pltpu.roll(after, back, 0) if back else after,
            pltpu.roll(before, to_end, 0) if to_end else before,
        )

    if group < 2:
        return placed(3 * slot, 3 if slot < 2 else 2)
    if isinstance(z, int):
        return placed(4 * (z % 2), 3)
    return jnp.where(z % 2 == 0, placed(0, 3), placed(4, 3))


def repeat(first, last, body, together=1):
    count = last - first
    if together >= count:
        for i in range(first, last):
            body(i)
        return
    rounds = count // together

    def several(n, _):
        for k in range(together):
            body(first + n * together + k)

    lax.fori_loop(0, rounds, several, None)
    for i in range(first + rounds * together, last):
        body(i)


def pack_edge(tile_of, message, layers, last):
    def turn(v, shift):
        return pltpu.roll(v, shift, 0) if shift else v

    def send(tile, v):
        message[tile * TILE : (tile + 1) * TILE, :] = v

    row = rows_of((TILE, message.shape[1]))
    shifts = (3, 6, 0) if last else (0, 3, 6)
    for z in range(layers):
        for g in range(2):
            a, b, c = [turn(tile_of(c, z), shift) for c, shift in zip(X_GROUPS[g], shifts)]
            send(2 * z + g, jnp.where(row < 3, a, jnp.where(row < 6, b, c)))
    shifts = (3, 7) if last else (0, 4)
    for pair in range(layers // 2):
        a, b = [turn(tile_of(X_GROUPS[2][0], 2 * pair + k), shifts[k]) for k in (0, 1)]
        send(2 * layers + pair, jnp.where(row < REACH, a, b))


def pack_x(*refs, n_adj, n_swaps):
    fields, permittivity = refs[:2]
    if n_adj:
        values, rows, owners, to_even, to_odd, blocks = refs[2:8]
        to_diag = refs[8 : 8 + n_swaps]
        edges, edge_perm, rows_s, owners_s, sems = refs[8 + n_swaps :]
    else:
        to_even, to_odd = refs[2:4]
        to_diag = refs[4 : 4 + n_swaps]
        edges, edge_perm, sems = refs[4 + n_swaps :]
    px = lax.axis_index("xs") % 2
    layers, cells_x = fields.shape[1:3]
    copies = []
    for k, start in enumerate((0, cells_x - TILE)):
        rows_at = pl.ds(start, TILE)
        copies.append((fields.at[:, :, rows_at, :], edges.at[k]))
        copies.append((permittivity.at[:, rows_at, :], edge_perm.at[k]))
    if n_adj:
        blocks[...] = jnp.zeros(blocks.shape, jnp.float32)
        copies.append((values, blocks.at[pl.ds(0, n_adj), :]))
        copies.append((rows, rows_s))
        copies.append((owners, owners_s))
    copies = [pltpu.make_async_copy(s, d, sems.at[k]) for k, (s, d) in enumerate(copies)]
    for copy in copies:
        copy.start()
    for copy in copies:
        copy.wait()

    def edge_of(k):
        return lambda c, z: edges[k, c, z] if c < 6 else time_step / edge_perm[k, z]

    def pack(first, last):
        pack_edge(edge_of(0), first, layers, False)
        pack_edge(edge_of(1), last, layers, True)

    pl.when(px == 0)(lambda: pack(to_odd, to_even))
    pl.when(px == 1)(lambda: pack(to_even, to_odd))

    def pack_corner(message, k, to_next):
        for g, parts in enumerate(Y_GROUPS):
            packed = [
                pack_strip(lambda z: edge_of(k)(c, z), layers, 5 if to_next else 3) for c in parts
            ]
            message[g * TILE : (g + 1) * TILE, :] = pack_group(packed, to_next)

    for swap, message in enumerate(to_diag):
        is_next = lax.axis_index("ys") % 2 == swap
        for k in (0, 1):
            for to_next in (False, True):
                pl.when((px == k) & (is_next == to_next))(
                    functools.partial(pack_corner, message, k, to_next)
                )
    if n_adj:
        for b in range(n_adj):
            code = rows_s[b] + cells_x * owners_s[b]
            blocks[n_adj + b : n_adj + b + 1, :] = jnp.full(
                (1, blocks.shape[1]), code, jnp.int32
            ).astype(jnp.float32)
        to_even[x_message_rows(layers) :, :] = blocks[...]
        to_odd[x_message_rows(layers) :, :] = blocks[...]
        to_diag[0][len(Y_GROUPS) * TILE :, :] = blocks[...]


def pack_strip(tile_of, layers, shift):
    total = None
    for z in range(layers):
        block = tile_of(z)
        moved = pltpu.roll(block, (SLOT * z + shift) % block.shape[1], 1)
        total = moved if z == 0 else jnp.where(lanes_of(block.shape) // SLOT == z, moved, total)
    return total


def pack_strips(tile_of, layers):
    tiles = [tile_of(z) for z in range(layers)]
    return [pack_strip(lambda z: tiles[z], layers, shift) for shift in (3, 5)]


def pack_group(edges, to_next):
    width = edges[0].shape[1]
    place = lanes_of(edges[0].shape) % SLOT
    total = pltpu.roll(edges[0], width - 2 if to_next else width - 3, 1)
    if len(edges) > 1:
        middle = pltpu.roll(edges[1], 1, 1) if to_next else edges[1]
        total = jnp.where(place < 3, total, jnp.where(place < 6, middle, pltpu.roll(edges[2], 3, 1)))
    return total


def place_group(before, after, slot):
    width = before.shape[1]
    lower, upper = ((0, 5), (width - 3, 2), (width - 5, width - 1))[slot]
    return (pltpu.roll(before, lower, 1) if lower else before), pltpu.roll(after, upper, 1)


def pack_y(fields, permittivity, even, *refs, n_rows):
    blocks, refs = (refs[0], refs[1:]) if n_rows else (None, refs)
    strips, *to_y = refs
    layers, cells_x, width = fields.shape[1:]
    ring = cells_x + TILE
    px = lax.axis_index("xs") % 2

    def fill(message, to_next):
        for r in range(ring // TILE):
            rows = slice(r * TILE, (r + 1) * TILE)
            for g, parts in enumerate(Y_GROUPS):
                packed = []
                for c in parts:

                    def tile_of(z):
                        if r * TILE == cells_x:
                            return halo_tile(even, even, px, c, z, layers)
                        return own_tile(fields, permittivity, c, z, rows)

                    packed.append(pack_strip(tile_of, layers, 5 if to_next else 3))
                    if r * TILE < cells_x:
                        strips[int(to_next), c, rows, :] = packed[-1]
                at = slice(g * ring + r * TILE, g * ring + (r + 1) * TILE)
                message[at, :] = pack_group(packed, to_next)

    for swap, message in enumerate(to_y):
        is_next = lax.axis_index("ys") % 2 == swap
        for to_next in (False, True):
            pl.when(is_next == to_next)(functools.partial(fill, message, to_next))
    if n_rows:
        end = len(Y_GROUPS) * ring
        to_y[0][end : end + n_rows, :] = blocks[...]
        to_y[0][end + n_rows : end + 2 * n_rows, :] = even[x_message_rows(layers) :, :]


def own_tile(fields, permittivity, c, z, rows):
    return fields[c, z, rows, :] if c < 6 else time_step / permittivity[z, rows, :]


def row_index(shape):
    fold = lax.broadcasted_iota(jnp.int32, shape, 0)
    return lax.broadcasted_iota(jnp.int32, shape, 1) * shape[0] + fold


def gather_sources(sets, px, me, totals, n_adj, cells_x):
    mine, other = totals[0], totals[1]
    row_at = row_index(mine.shape).astype(jnp.float32)
    own_index = jnp.where(me == 0, 0.0, 1.0)
    for ref, start, is_next in sets:
        for b in range(n_adj):
            value = ref[start + b : start + b + 1, :]
            code = ref[start + n_adj + b : start + n_adj + b + 1, :]
            owner = jnp.where(code >= cells_x, 1.0, 0.0)
            row = code - cells_x * owner
            if is_next is not None:
                after = jnp.where(row < REACH, row + cells_x, -1.0)
                before = jnp.where(row >= cells_x - REACH, row + TILE, -1.0)
                row = jnp.where(is_next, after, before)
            is_mine = owner == own_index
            mine = mine + jnp.where(row_at == jnp.where(is_mine, row, -1.0), value, 0.0)
            other = other + jnp.where(row_at == jnp.where(is_mine, -1.0, row), value, 0.0)
    totals[0], totals[1] = mine, other


def place_sources(totals, me, source):
    mine, other = totals[0], totals[1]
    lane = lanes_of(mine.shape)
    slot = (lane >= SLOT * ZS) & (lane < SLOT * (ZS + 1))
    place = lane - SLOT * ZS
    shift = SLOT * ZS + 3
    before = jnp.where(me == 0, 0.0, pltpu.roll(other, shift, 2))
    source[0] = mine
    source[1] = jnp.where(slot, jnp.where(place < 3, before, pltpu.roll(mine, shift, 2)), 0.0)
    shift = SLOT * ZS + 5
    after = jnp.where(me == 0, pltpu.roll(other, shift, 2), 0.0)
    source[2] = jnp.where(slot, jnp.where(place < 5, pltpu.roll(mine, shift, 2), after), 0.0)


def next_x(v):
    return jnp.concatenate([v[1:], pltpu.roll(v[0:1], v.shape[1] - 1, 1)], 0)


def prev_x(v):
    return jnp.concatenate([pltpu.roll(v[-1:], 1, 1), v[:-1]], 0)


def lane_roll(v, shift):
    return pltpu.roll(v, shift % v.shape[2], 2)


def zeros(shape):
    return jnp.zeros(shape, jnp.float32)


def unfold(ref, fold):
    return jnp.stack([ref[pl.ds(j, TILE, stride=fold), :] for j in range(fold)])


def fold_back(ref, v):
    for j in range(v.shape[0]):
        ref[pl.ds(j, TILE, stride=v.shape[0]), :] = v[j]


def step_size(full):
    outside = (row_index(full) >= full[0] * TILE - REACH) & (lax.axis_index("xs") == 0)
    return jnp.where(outside, 0.0, time_step)


def evolve_strips(strips, halo_strips, y_halos, diag_halos, source, strip, edge_e, edge_h):
    me = lax.axis_index("ys")
    ring, width = strips.shape[2] + TILE, strips.shape[3]
    fold = ring // TILE
    full = (fold, TILE, width)
    for g, parts in enumerate(Y_GROUPS):
        for r in range(fold):
            before, after = zeros((TILE, width)), zeros((TILE, width))
            at = g * ring + r * TILE
            for k, (y_ref, d_ref) in enumerate(zip(y_halos, diag_halos)):
                block = y_ref[at : at + TILE, :]
                if r + 1 == fold:
                    odd_half = (rows_of(block.shape) >= REACH) == (lax.axis_index("xs") % 2 == 0)
                    corner = jnp.where(at_end("xs"), 0.0, d_ref[g * TILE : (g + 1) * TILE, :])
                    block = jnp.where(odd_half, corner, block)
                if k:
                    block = jnp.where(at_end("ys"), 0.0, block)
                is_next = me % 2 == k
                after = jnp.where(is_next, block, after)
                before = jnp.where(is_next, before, block)
            place = lanes_of(before.shape) % SLOT
            rows = slice(r * TILE, (r + 1) * TILE)
            for slot, c in enumerate(parts):
                lower, upper = place_group(before, after, slot)
                own = [strips[k, c, rows, :] if r + 1 < fold else halo_strips[k, c] for k in (0, 1)]
                strip[0, c, rows, :] = jnp.where(place < 3, lower, own[0])
                strip[1, c, rows, :] = jnp.where(place >= 5, upper, own[1])
    lane = lanes_of(full)
    place = lane % SLOT
    for side in (0, 1):
        ex, ey, ez, hx, hy, hz, co = [unfold(strip.at[side, c], fold) for c in range(PARTS)]
        dt = step_size(full)
        if not side:
            dt = jnp.where((place < 3) & (me == 0), 0.0, dt)
        for step in range(STEPS):

            def next_z(v):
                return jnp.where(lane < width - SLOT, lane_roll(v, -SLOT), 0.0)

            def prev_z(v):
                return jnp.where(lane >= SLOT, lane_roll(v, SLOT), 0.0)

            if side:
                edge_e[step] = jnp.where(place == 5, ex, lane_roll(ez, 1))
                if step + 1 == STEPS:
                    continue
            hx = hx - dt * (lane_roll(ez, -1) - ez - (next_z(ey) - ey))
            hy = hy - dt * (next_z(ex) - ex - (next_x(ez) - ez))
            hz = hz - dt * (next_x(ey) - ey - (lane_roll(ex, -1) - ex))
            if not side:
                edge_h[step] = jnp.where(place == 2, hz, lane_roll(hx, 1))
                if step + 1 == STEPS:
                    continue
            ex = ex + co * (hz - lane_roll(hz, 1) - (hy - prev_z(hy)))
            ey = ey + co * (hx - prev_z(hx) - (hz - prev_x(hz)))
            ez = ez + co * (hy - prev_x(hy) - (hx - lane_roll(hx, 1)) - source[1 + side])


def surface_layers(layers):
    return range(max(ZS - STEPS, 0), min(ZS + STEPS + 1, layers))


def prepare_surface(*refs, n_adj, n_rows, n_swaps):
    fields, permittivity, even, odd, angle_wave = refs[1:6]
    strips, state, coeffs, halo_strips, angles = refs[6 + bool(n_adj) : 11 + bool(n_adj)]
    rows, angles_s, sem = refs[-3:]
    fetch = pltpu.make_async_copy(angle_wave, angles_s, sem)
    fetch.start()
    px = lax.axis_index("xs") % 2
    layers, cells_x, width = fields.shape[1:]
    ring = cells_x + TILE
    fold = ring // TILE

    def fill(side):
        for c in range(PARTS):
            for r in range(cells_x // TILE):
                at = slice(r * TILE, (r + 1) * TILE)
                strips[side, c, at, :] = pack_strip(
                    lambda z: own_tile(fields, permittivity, c, z, at), layers, 5 if side else 3
                )

    if n_swaps == 1:
        for side in (0, 1):
            pl.when(lax.axis_index("ys") % 2 == side)(functools.partial(fill, side))
    for c in range(PARTS):
        halos = [halo_tile(even, odd, px, c, z, layers) for z in range(layers)]
        for side, tile in enumerate(pack_strips(lambda z: halos[z], layers)):
            halo_strips[side, c] = tile
        for z in surface_layers(layers):
            rows[c, z, 0:cells_x, :] = fields[c, z] if c < 6 else time_step / permittivity[z]
            rows[c, z, cells_x:ring, :] = halos[z]
            folded = unfold(rows.at[c, z], fold)
            if c < 6:
                state[c, z] = folded
            else:
                coeffs[z] = folded
    if n_adj:
        blocks, totals = refs[6], refs[12]
        totals[...] = zeros(totals.shape)
        end = x_message_rows(layers)
        rows[0, 0, 0:n_rows, :] = jnp.where(at_end("xs"), 0.0, odd[end:, :])
        sets = [(blocks, 0, None), (even, end, px == 0), (rows.at[0, 0], 0, px == 1)]
        gather_sources(sets, px, lax.axis_index("ys"), totals, n_adj, cells_x)
    fetch.wait()
    per_block = angle_wave.shape[0] // lax.axis_size("xs")
    for k in range(angles.shape[0]):
        owner = lax.axis_index("xs") ^ (k // per_block * NEAR)
        one = angles_s[owner * per_block + k % per_block]
        angles[k : k + 1, :] = jnp.full((1, angles.shape[1]), one, jnp.int32)


def surface_steps(*refs, n_adj, n_rows, n_swaps):
    before, coeffs, halo_strips, strips = refs[:4]
    y_halos, diag_halos = refs[4 : 4 + n_swaps], refs[4 + n_swaps : 4 + 2 * n_swaps]
    given, out, source, edge_e, edge_h, rows, state, strip, totals = refs[4 + 2 * n_swaps :]
    px = lax.axis_index("xs") % 2
    me = lax.axis_index("ys")
    layers = before.shape[1]
    full = before.shape[2:]
    fold, width = full[0], full[2]
    cells_x = (fold - 1) * TILE
    lane = lanes_of(full)

    if n_adj:
        end = len(Y_GROUPS) * fold * TILE
        sets = [
            (y_halos[0], end, None),
            (y_halos[0], end + n_rows, px == 0),
            (rows.at[0], 0, px == 1),
        ]
        corner_rows = diag_halos[0][len(Y_GROUPS) * TILE :, :]
        rows[0, 0:n_rows, :] = jnp.where(at_end("xs"), 0.0, corner_rows)
        totals[...] = given[...]
        gather_sources(sets, px, me, totals, n_adj, cells_x)
        place_sources(totals, me, source)
    else:
        source[...] = given[...]
    evolve_strips(strips, halo_strips, y_halos, diag_halos, source, strip, edge_e, edge_h)

    dt = step_size(full)
    for step in range(STEPS):
        final = step + 1 == STEPS
        low, high = max(ZS - STEPS + step, 0), min(ZS + STEPS - 1 - step, layers - 1)

        def load(c, z):
            return state[c, z] if step else before[c, z]

        def store(c, z, v):
            if not final:
                state[c, z] = v
            elif z == ZS and c in (0, 1, 3, 4):
                fold_back(rows.at[c], v)

        below = None
        ex, ey = load(0, low), load(1, low)
        for z in range(low, high + 1):
            ez, hx, hy, hz = [load(c, z) for c in range(2, 6)]
            if z + 1 < layers:
                ex_above, ey_above = load(0, z + 1), load(1, z + 1)
            else:
                ex_above, ey_above = jnp.zeros(full, jnp.float32), jnp.zeros(full, jnp.float32)
            edge = lane_roll(edge_e[step], width - 1 - (SLOT * z + 5))
            ex_y = jnp.where(lane == width - 1, edge, lane_roll(ex, -1))
            ez_y = lane_roll(jnp.where(lane == 0, edge, ez), -1)
            hx = hx - dt * (ez_y - ez - (ey_above - ey))
            hy = hy - dt * (ex_above - ex - (next_x(ez) - ez))
            hz = hz - dt * (next_x(ey) - ey - (ex_y - ex))
            for c, v in ((3, hx), (4, hy), (5, hz)):
                store(c, z, v)
            if z == 0 or below:
                co = coeffs[z]
                hx_z = hx - below[0] if z else hx
                hy_z = hy - below[1] if z else hy
                edge = lane_roll(edge_h[step], width - 1 - (SLOT * z + 2))
                hx_y = jnp.where(lane == 0, edge, lane_roll(hx, 1))
                hz_y = lane_roll(jnp.where(lane == width - 1, edge, hz), 1)
                store(0, z, ex + co * (hz - hz_y - hy_z))
                store(1, z, ey + co * (hx_z - (hz - prev_x(hz))))
                change = hy - prev_x(hy) - (hx - hx_y)
                if z == ZS:
                    change = change - source[0]
                store(2, z, ez + co * change)
            below = (hx, hy)
            ex, ey = ex_above, ey_above
    for k, (c, sign) in enumerate(((4, -1.0), (3, 1.0), (1, 1.0), (0, -1.0))):
        out[:, k * width : (k + 1) * width] = sign * rows[c, 0:cells_x, :]


def take_steps(first, last, layers, refs, load, store, load_coeff, after_layer=None):
    source, edge_e, edge_h = refs
    full = source.shape[1:]
    width = full[2]
    lane = lanes_of(full)
    dt = step_size(full)
    for step in range(first, last):

        def advance_h(z):
            ex, ey, ez, hx, hy, hz = [load(step, c, z) for c in range(6)]
            edge = lane_roll(edge_e[step], 2 * width - 1 - (SLOT * z + 5))
            ex_y = jnp.where(lane == width - 1, edge, lane_roll(ex, -1))
            ez_y = lane_roll(jnp.where(lane == 0, edge, ez), -1)
            store(step, 3, z, hx - dt * (ez_y - ez - (load(step, 1, z + 1) - ey)))
            store(step, 4, z, hy - dt * (load(step, 0, z + 1) - ex - (next_x(ez) - ez)))
            store(step, 5, z, hz - dt * (next_x(ey) - ey - (ex_y - ex)))

        def advance_e(z):
            hx, hy, hz = [load(step + 1, c, z) for c in range(3, 6)]
            co = load_coeff(z)
            edge = lane_roll(edge_h[step], 2 * width - 1 - (SLOT * z + 2))
            hx_y = jnp.where(lane == 0, edge, lane_roll(hx, 1))
            hz_y = lane_roll(jnp.where(lane == width - 1, edge, hz), 1)
            change = hz - hz_y - (hy - load(step + 1, 4, z - 1))
            store(step, 0, z, load(step, 0, z) + co * change)
            change = hx - load(step + 1, 3, z - 1) - (hz - prev_x(hz))
            store(step, 1, z, load(step, 1, z) + co * change)
            change = hy - prev_x(hy) - (hx - hx_y) - jnp.where(z == ZS, source[0], 0.0)
            store(step, 2, z, load(step, 2, z) + co * change)
            if after_layer and step + 1 == last:
                after_layer(z)

        repeat(0, layers, advance_h, TOGETHER)
        repeat(0, layers, advance_e, TOGETHER)


def zero_outside(ref, layers):
    for c in (0, 1):
        ref[c, layers + 1] = zeros(ref.shape[2:])
        ref[c + 3, 0] = zeros(ref.shape[2:])


def early_steps(*refs):
    fields, permittivity, even, odd, *carried = refs[:7]
    state, coeffs, grid, coeff_rows = refs[7:]
    px = lax.axis_index("xs") % 2
    layers, cells_x, width = fields.shape[1:]
    ring = cells_x + TILE
    fold = ring // TILE

    def build(z):
        for c in range(PARTS):
            ref = grid.at[c, z + 1] if c < 6 else coeff_rows.at[z]
            ref[0:cells_x, :] = fields[c, z] if c < 6 else time_step / permittivity[z]
            ref[cells_x:ring, :] = halo_tile(even, odd, px, c, z, layers)
        coeffs[z] = unfold(coeff_rows.at[z], fold)

    repeat(0, layers, build, TOGETHER // 2)
    for c in (0, 1):
        grid[c, layers + 1] = zeros((ring, width))
    zero_outside(state, layers)

    def load(step, c, z):
        return state[c, z + 1] if step else unfold(grid.at[c, z + 1], fold)

    def store(step, c, z, v):
        state[c, z + 1] = v

    take_steps(0, EARLY, layers, carried, load, store, lambda z: coeffs[z])


def later_steps(*refs):
    before, coeffs, *carried = refs[:5]
    out, state, grid, sems = refs[5:]
    layers, cells_x = out.shape[1:3]

    def copy_out(z):
        done = grid.at[:, z, pl.ds(0, cells_x), :]
        return pltpu.make_async_copy(done, out.at[:, z], sems.at[z])

    zero_outside(state, layers)

    def load(step, c, z):
        return (before if step == EARLY else state)[c, z + 1]

    def store(step, c, z, v):
        if step + 1 < STEPS or c >= 3:
            state[c, z + 1] = v
        if step + 1 == STEPS:
            fold_back(grid.at[c, z], v)

    take_steps(
        EARLY,
        STEPS,
        layers,
        carried,
        load,
        store,
        lambda z: coeffs[z],
        lambda z: copy_out(z).start(),
    )
    repeat(0, layers, lambda z: copy_out(z).wait())


def multiply(weights, *refs, n_tiles):
    tiles, parts = refs[:n_tiles], refs[n_tiles:]
    total = jnp.dot(
        weights[...],
        jnp.concatenate([tile[...] for tile in tiles], 0),
        precision=lax.Precision.HIGHEST,
        preferred_element_type=jnp.float32,
    )
    rows = parts[0].shape[0]
    for k, part in enumerate(parts):
        part[...] = total[k * rows : (k + 1) * rows]


def add_parts(*refs):
    parts, out = refs[:-1], refs[-1]
    total = parts[0][...]
    for part in parts[1:]:
        total = total + part[...]
    width = out.shape[2]
    for k in range(out.shape[1]):
        out[:, k, :] = total[:, k * width : (k + 1) * width]


def shape_of(*dims):
    return jax.ShapeDtypeStruct(dims, jnp.float32)


def far_field_weights(angles, xs_size, cells_x):
    column = jnp.arange(NEAR * cells_x, dtype=jnp.int32)
    owner = lax.axis_index("xs") ^ (column // cells_x)
    phase = angles * (X0 + owner * cells_x + column % cells_x)[None, :] % GRID_X
    angle = phase.astype(jnp.float32) * (2.0 * math.pi / GRID_X)
    scale = 1.0 / math.sqrt(cells_x * xs_size)
    both = jnp.stack([jnp.cos(angle) * scale, -jnp.sin(angle) * scale], axis=1)
    return both.reshape(-1, NEAR * cells_x)


def far_field_exchange(tile, angles, xs_size, beside, finish):
    cells_x, columns = tile.shape
    weights = far_field_weights(angles, xs_size, cells_x)

    def across(block, mask):
        return lax.ppermute(block, "xs", [(i, i ^ mask) for i in range(xs_size)])

    third = across(tile, 2)
    second = across(tile, 1)
    fourth = across(tile, 3)
    third, fourth, beside = lax.optimization_barrier((third, fourth, beside))
    far = xs_size // NEAR
    rows = weights.shape[0] // far
    parts = pl.pallas_call(
        functools.partial(multiply, n_tiles=NEAR),
        out_shape=(shape_of(rows, columns),) * far,
        in_specs=[VMEM] * (NEAR + 1),
        out_specs=(VMEM,) * far,
        compiler_params=PARAMS,
        name="partial_spectrum",
    )(weights, tile, second, third, fourth)
    order = [far // 2] + [k for k in range(far - 1, 0, -1) if k != far // 2]
    arrived = [across(parts[k], k * NEAR) for k in order]
    finished = finish(beside)
    far_field = pl.pallas_call(
        add_parts,
        out_shape=shape_of(rows, 4, columns // 4),
        in_specs=[VMEM] * far,
        out_specs=VMEM,
        compiler_params=PARAMS,
        name="add_arrived",
    )(parts[0], *arrived)
    return far_field, finished


def gathered_sources(adj_values, adj_owner, adj_row, cells_x, cells_y):
    groups = lax.axis_size("ys")
    owners = adj_owner[:, 0]
    hits = (owners[:, None] == jnp.arange(groups, dtype=jnp.int32)[None, :]).astype(jnp.int32)
    before = jnp.cumsum(hits, axis=0) - hits
    slot_index = owners * CAP + jnp.sum(before * hits, axis=1)
    placing = (jnp.arange(groups * CAP, dtype=jnp.int32)[:, None] == slot_index[None, :]).astype(
        jnp.float32
    )
    rows = jnp.broadcast_to(adj_row.astype(jnp.float32)[:, None], (adj_row.shape[0], 1))
    outgoing = jnp.dot(
        placing, jnp.concatenate([adj_values, rows], 1), precision=lax.Precision.HIGHEST
    ).reshape(groups, CAP, cells_y + 1)
    incoming = lax.all_to_all(outgoing, "ys", split_axis=0, concat_axis=0, tiled=True)
    incoming = incoming.reshape(groups * CAP, cells_y + 1)
    landing = (
        jnp.arange(cells_x, dtype=jnp.float32)[:, None] == incoming[:, cells_y][None, :]
    ).astype(jnp.float32)
    current = jnp.dot(landing, incoming[:, :cells_y], precision=lax.Precision.HIGHEST)

    def shifted(block, axis, distance):
        size = lax.axis_size(axis)
        route = [(i, i + distance) for i in range(size) if 0 <= i + distance < size]
        return lax.ppermute(block, axis, route)

    after = shifted(current[:REACH], "xs", -1)
    before = shifted(current[-REACH:], "xs", 1)
    ringed = jnp.concatenate([current, after, before], 0)
    right = shifted(ringed[:, :3], "ys", -1)
    left = shifted(ringed[:, -3:], "ys", 1)
    start, end = SLOT * ZS, cells_y - SLOT * (ZS + 1)
    first = jnp.pad(jnp.concatenate([left, ringed[:, :5]], 1), ((0, 0), (start, end)))
    second = jnp.pad(jnp.concatenate([ringed[:, -5:], right], 1), ((0, 0), (start, end)))
    folded = jnp.stack([ringed, first, second]).reshape(3, TILE, -1, cells_y)
    return folded.transpose(0, 2, 1, 3)


def on_device(fields, permittivity, adj_values, adj_owner, adj_row, angle_wave):
    layers, cells_x, cells_y = fields.shape[1:]
    xs_size, ys_size = lax.axis_size("xs"), lax.axis_size("ys")
    raw = ys_size == 2
    n_adj = adj_values.shape[0] if raw else 0
    n_rows = -(-2 * n_adj // TILE) * TILE
    ring = cells_x + TILE
    x_rows = x_message_rows(layers) + n_rows
    y_rows = len(Y_GROUPS) * ring + 2 * n_rows
    d_rows = len(Y_GROUPS) * TILE + n_rows
    y_swaps = swaps(ys_size)

    extra = (adj_values, adj_row, adj_owner.reshape(-1)) if raw else ()
    x_message = shape_of(x_rows, cells_y)
    made = (x_message,) * 2 + ((shape_of(n_rows, cells_y),) if raw else ())
    made += (shape_of(d_rows, cells_y),) * len(y_swaps)
    to_even, to_odd, *packed = pl.pallas_call(
        functools.partial(pack_x, n_adj=n_adj, n_swaps=len(y_swaps)),
        out_shape=made,
        in_specs=[ANY] * (2 + len(extra)),
        out_specs=(VMEM,) * len(made),
        scratch_shapes=[
            pltpu.VMEM((2, 6, layers, TILE, cells_y), jnp.float32),
            pltpu.VMEM((2, layers, TILE, cells_y), jnp.float32),
        ]
        + ([pltpu.SMEM((n_adj,), jnp.int32)] * 2 if raw else [])
        + [pltpu.SemaphoreType.DMA((4 + len(extra),))],
        compiler_params=PARAMS,
        name="pack_x_edges",
    )(*[pltpu.with_memory_space_constraint(x, pltpu.HBM) for x in (fields, permittivity, *extra)])
    blocks, to_diag = (packed[:1], packed[1:]) if raw else ([], packed)
    both = ("xs", "ys")
    from_even = lax.ppermute(to_even, "xs", swaps(xs_size)[0])
    straight = odd_route(xs_size, ys_size, [(i, i) for i in range(ys_size)])
    from_odd = lax.ppermute(to_odd, both, straight)
    diag_halos = [
        lax.ppermute(message, both, odd_route(xs_size, ys_size, route))
        for message, route in zip(to_diag, y_swaps)
    ]

    made = (shape_of(2, PARTS, cells_x, cells_y),) + (shape_of(y_rows, cells_y),) * len(y_swaps)
    strips, *to_y = pl.pallas_call(
        functools.partial(pack_y, n_rows=n_rows),
        out_shape=made,
        in_specs=[VMEM] * (3 + len(blocks)),
        out_specs=(VMEM,) * len(made),
        compiler_params=PARAMS,
        name="pack_y_edges",
    )(fields, permittivity, from_even, *blocks)
    y_halos = [lax.ppermute(message, "ys", route) for message, route in zip(to_y, y_swaps)]

    fold = ring // TILE
    folded = (fold, TILE, cells_y)
    n_angles = angle_wave.shape[0] // NEAR
    made = (
        strips,
        shape_of(6, layers, *folded),
        shape_of(layers, *folded),
        shape_of(2, PARTS, TILE, cells_y),
        jax.ShapeDtypeStruct((n_angles, NEAR * cells_x), jnp.int32),
    ) + ((shape_of(2, *folded),) if raw else ())
    prepared = pl.pallas_call(
        functools.partial(prepare_surface, n_adj=n_adj, n_rows=n_rows, n_swaps=len(y_swaps)),
        out_shape=[jax.ShapeDtypeStruct(x.shape, x.dtype) for x in made],
        in_specs=[VMEM] * 5 + [ANY] + [VMEM] * len(blocks),
        input_output_aliases={0: 0},
        out_specs=(VMEM,) * len(made),
        scratch_shapes=[
            pltpu.VMEM((PARTS, layers, ring, cells_y), jnp.float32),
            pltpu.SMEM(angle_wave.shape, jnp.int32),
            pltpu.SemaphoreType.DMA(()),
        ],
        compiler_params=PARAMS,
        name="prepare_surface",
    )(
        strips,
        fields,
        permittivity,
        from_even,
        from_odd,
        pltpu.with_memory_space_constraint(angle_wave, pltpu.HBM),
        *blocks,
    )
    strips, *prepared = prepared
    angles = prepared[3]
    if raw:
        sources = prepared[4:]
    else:
        sources = (gathered_sources(adj_values, adj_owner, adj_row, cells_x, cells_y),)
    operands = (*prepared[:3], strips, *y_halos, *diag_halos, *sources)
    tile, *carried = pl.pallas_call(
        functools.partial(surface_steps, n_adj=n_adj, n_rows=n_rows, n_swaps=len(y_swaps)),
        out_shape=(
            shape_of(cells_x, 4 * cells_y),
            shape_of(3, *folded),
            shape_of(STEPS, *folded),
            shape_of(STEPS, *folded),
        ),
        in_specs=[VMEM] * len(operands),
        out_specs=(VMEM,) * 4,
        scratch_shapes=[
            pltpu.VMEM((6, ring, cells_y), jnp.float32),
            pltpu.VMEM((6, layers, *folded), jnp.float32),
            pltpu.VMEM((2, PARTS, ring, cells_y), jnp.float32),
            pltpu.VMEM((2, *folded), jnp.float32),
        ],
        compiler_params=PARAMS,
        name="surface_steps",
    )(*operands)

    state_shape = (6, layers + 2, *folded)
    operands = (fields, permittivity, from_even, from_odd, *carried)
    stepped = pl.pallas_call(
        early_steps,
        out_shape=(shape_of(*state_shape), shape_of(layers, *folded)),
        in_specs=[VMEM] * len(operands),
        out_specs=(VMEM, VMEM),
        scratch_shapes=[
            pltpu.VMEM((6, layers + 2, ring, cells_y), jnp.float32),
            pltpu.VMEM((layers, ring, cells_y), jnp.float32),
        ],
        compiler_params=PARAMS,
        name="early_steps",
    )(*operands)

    def finish(stepped):
        return pl.pallas_call(
            later_steps,
            out_shape=shape_of(*fields.shape),
            in_specs=[VMEM] * 5,
            out_specs=ANY,
            scratch_shapes=[
                pltpu.VMEM(state_shape, jnp.float32),
                pltpu.VMEM((6, layers, ring, cells_y), jnp.float32),
                pltpu.SemaphoreType.DMA((layers,)),
            ],
            compiler_params=PARAMS,
            name="later_steps",
        )(*stepped, *carried)

    far, new_fields = far_field_exchange(tile, angles, xs_size, stepped, finish)
    per_block = angle_wave.shape[0] // xs_size
    return (new_fields, far.reshape(per_block, 2, 4, cells_y))


def solution(mesh):
    placed = (
        P(None, None, "xs", "ys"),
        P(None, "xs", "ys"),
        P(("xs", "ys"), None),
        P(("xs", "ys"), None),
        P(("xs", "ys")),
        P(),
    )
    return jax.shard_map(
        on_device,
        mesh=mesh,
        in_specs=placed,
        out_specs=(P(None, None, "xs", "ys"), P("xs", None, None, "ys")),
        check_vma=False,
    )
```
